32 devices in a mesh: groups: 1, ep: 16 (over z, y, x), sub: 2 (over core).
Axes of the slice: x: 2, y: 2, z: 4, core: 2. Of those that a mesh axis runs over, the one named last changes fastest.
Arguments:
- hidden_in: bfloat16 [256, 3584], P(('groups', 'ep', 'sub')), may hold values from -6 to 6
- expert_routes: int32 [256, 8], P(('groups', 'ep', 'sub')), may hold values from 0 to 15, all different within a row; in each aligned block of 8 rows (0 to 7, 8 to 15, ...) at most 8 rows name the same one
- route_scores: float32 [256, 8], P(('groups', 'ep', 'sub')), may hold values from 0.1 to 1
- expert_gate: bfloat16 [16, 3584, 1024], P('ep', None, 'sub'), may hold values from -0.09375 to 0.09375
- expert_up: bfloat16 [16, 3584, 1024], P('ep', None, 'sub'), may hold values from -0.09375 to 0.09375
- expert_down: bfloat16 [16, 1024, 3584], P('ep', 'sub'), may hold values from -0.1875 to 0.1875
- query_latent: bfloat16 [128, 128, 576], P(('groups', 'ep', 'sub')), may hold values from -49 to 49
- latent_cache: bfloat16 [128, 256, 576], P(('groups', 'ep', 'sub')), may hold values from -8 to 8
- cache_lengths: int32 [128], P(('groups', 'ep', 'sub')), may hold values from 2 to 256, as said below
Outputs:
- moe_output: bfloat16 [256, 3584], P(('groups', 'ep', 'sub'))
- attention_latent: bfloat16 [128, 128, 512], P(('groups', 'ep', 'sub'))
The draws below stay inside these ranges and needn't reach their ends.
Inputs may be any that keep to these rules, and one draw needn't show every extreme that they name: `expert_routes`: each row names 8 different experts. Among the 8 rows of one device (aligned blocks), no expert is named more than 8 times, a bound that some block reaches. `cache_lengths`: some row has length 256.
All inputs are finite; a program needn't handle non-finite values.
Results may differ from the reference program's by a relative error of at most 0.0085.
Values may be sent and summed in bfloat16 or wider, within the bound.
No kernel may reach another device: no remote copies, remote signals or barrier semaphores. Data moves between devices by JAX's collectives and lax.ppermute only.
A program may use at most 64 MiB of HBM per device.

```python
import math
import jax
import jax.numpy as jnp
import numpy as np
from jax import lax

D = 3584
FF = 1024
HEADS = 128
LATENT = 512
ROPE = 64
TOPK = 8
TOK_DEV = 8
ATT_ROWS = 4
CACHE = 256
EXPERTS = 16
CAP = 8
TOKENS = 256
ATT_TOTAL = 128
N_EP = 16
N_SUB = 2


def shared_base(key):
    return jnp.clip(jax.random.normal(key, (ATT_TOTAL, CACHE, LATENT + ROPE), jnp.float32), -4.0, 4.0)


def draw_latent_cache(key, part):
    base_rows = shared_base(key)
    return base_rows.astype(jnp.bfloat16)


def draw_query_latent(key, part):
    key = jax.random.fold_in(key, 12)
    return jnp.clip(jax.random.normal(key, (ATT_TOTAL, HEADS, LATENT + ROPE), jnp.float32), -4.0, 4.0).astype(jnp.bfloat16)


def draw_cache_lengths(key, part):
    key = jax.random.fold_in(key, 13)
    first_key, second_key, third_key = jax.random.split(key, 3)
    devices = ATT_TOTAL // ATT_ROWS
    device_top = jax.random.randint(first_key, (devices, 1), 2, CACHE + 1)
    lengths_all = jax.random.randint(second_key, (devices, ATT_ROWS), 2, device_top + 1).reshape(-1)
    longest = jax.random.randint(third_key, (), 0, ATT_TOTAL)
    return lengths_all.at[longest].set(CACHE).astype(jnp.int32)


def shard_levels(key, dims, shards, low, top_value):
    def one(dim, blocks):
        draws = jax.random.uniform(jax.random.fold_in(jax.random.fold_in(key, 6), dim), (blocks,), jnp.float32, low / len(shards), top_value / len(shards))
        return jnp.repeat(jnp.exp(draws), dims[dim] // blocks).reshape((-1,) + (1,) * (len(dims) - dim - 1))

    gain = one(*shards[0])
    for cut in shards[1:]:
        gain = gain * one(*cut)
    return gain


def routed_block(stream_key, own, number, rows, amount, top, most, lean):
    order = jax.random.permutation(stream_key, amount)
    packed, common = load_shares(amount, rows * top, most, lean, True), load_shares(amount, rows * top, most, lean, False)
    places = jnp.arange(amount)

    def named(sizes, turn):
        used = int((sizes > 0).sum())
        fixed = max(1, used // 4)
        moved = fixed + (places - fixed + turn * (used - fixed)) % max(1, amount - fixed)
        return jnp.zeros((amount,), jnp.int32).at[order[jnp.where(places < fixed, places, moved)]].set(jnp.asarray(sizes, jnp.int32))

    sizes = jnp.where(number % 4 == 0, named(packed, number // 4), named(common, number - number // 4 - 1))
    mixed = jax.random.permutation(jax.random.fold_in(own, 3), amount)
    source_of, receiver = mixed[0:amount // 2 * 2:2], mixed[1:amount // 2 * 2:2]
    slack = jnp.minimum(sizes[source_of] - 1, most - sizes[receiver]) // 2
    slack = jnp.where((source_of == order[0]) | (receiver == order[0]) | (sizes[receiver] == 0), 0, jnp.maximum(slack, 0))
    moved = jax.random.randint(jax.random.fold_in(own, 4), (amount // 2,), 0, 1 << 20) % (slack + 1)
    sizes = sizes.at[source_of].add(-moved).at[receiver].add(moved)
    members = jnp.searchsorted(jnp.cumsum(sizes), jnp.arange(rows * top), side="right").astype(jnp.int32)
    table = members.reshape(top, rows).T
    table = table[jax.random.permutation(jax.random.fold_in(own, 1), rows)]
    turn = jax.random.randint(jax.random.fold_in(own, 2), (rows, 1), 0, top)
    return jnp.take_along_axis(table, (jnp.arange(top)[None, :] + turn) % top, axis=1)


def load_shares(number_of, total, bound, lean, full):
    portions = [(1 << 20) // math.isqrt(standing ** lean) + 1 for standing in range(1, number_of + 1)]
    largest = bound if full else min(bound, max(-(-total // number_of), total * portions[0] // sum(portions)))
    least = 1 if total - largest >= number_of - 1 else 0
    holding, surplus = [largest] + [least] * (number_of - 1), total - largest - least * (number_of - 1)
    while surplus > 0:
        movable = [i for i in range(1, number_of) if holding[i] < largest] or [i for i in range(1, number_of) if holding[i] < bound]
        mass, left = sum([portions[i] for i in movable]), surplus
        for i in movable:
            extra = min(bound - holding[i], max(1, left * portions[i] // mass), surplus)
            holding[i] = holding[i] + extra
            surplus = surplus - extra
    return np.array(holding)


def centred(own_key, dims, spread, reach, cuts=(), kind=jnp.bfloat16):
    values = jax.random.normal(own_key, dims, jnp.float32) * spread
    if len(cuts) > 0:
        values = shard_levels(own_key, dims, cuts, -0.22, 0.18) * values
    return jnp.clip(values, min=-reach, max=reach).astype(kind)


def setup_inputs(seed: int = 0, part: int = 0) -> dict:
    keys = jax.random.split(jax.random.key(seed), 10)
    part_keys = jax.random.split(jax.random.fold_in(keys[9], part), 10)
    hidden_in = centred(part_keys[0], (TOKENS, D), 1.0, 6.0, ((0, 32),))
    expert_routes_keys = jax.random.split(jax.random.fold_in(part_keys[1], 1), TOKENS // TOK_DEV)
    expert_routes_turns = jax.random.permutation(jax.random.fold_in(part_keys[1], 3), TOKENS // TOK_DEV)
    expert_routes = jax.vmap(lambda own, number: routed_block(jax.random.fold_in(part_keys[1], 2), own, number, TOK_DEV, EXPERTS, TOPK, CAP, 2))(expert_routes_keys, expert_routes_turns).reshape((TOKENS, TOPK))
    route_scores = jnp.clip(jnp.exp(math.log(1.0) - 2.3025851 * jax.random.uniform(part_keys[2], (TOKENS, TOPK), jnp.float32) ** shard_levels(part_keys[2], (TOKENS, TOPK), ((0, 32),), -0.2, 0.2)), 0.1, 1.0)
    expert_gate = centred(keys[3], (EXPERTS, D, FF), D ** -0.5, 0.09375, ((0, 16), (2, 2)))
    expert_up = centred(keys[4], (EXPERTS, D, FF), D ** -0.5, 0.09375, ((0, 16), (2, 2)))
    expert_down = centred(keys[5], (EXPERTS, FF, D), FF ** -0.5, 0.1875, ((0, 16), (1, 2)))
    query_latent = draw_query_latent(jax.random.fold_in(jax.random.fold_in(keys[9], part), 71), part)
    latent_cache = draw_latent_cache(jax.random.fold_in(jax.random.fold_in(keys[9], part), 71), part)
    cache_lengths = draw_cache_lengths(jax.random.fold_in(jax.random.fold_in(keys[9], part), 71), part)
    return {"hidden_in": hidden_in, "expert_routes": expert_routes, "route_scores": route_scores, "expert_gate": expert_gate, "expert_up": expert_up, "expert_down": expert_down, "query_latent": query_latent, "latent_cache": latent_cache, "cache_lengths": cache_lengths}


SOFTMAX_SCALE = 192.0 ** -0.5
ROUTE_SCALE = 2.5


def attend(query_latent, latent_cache, cache_lengths):
    scores = jnp.einsum("rhc,rtc->rht", query_latent.astype(jnp.float32), latent_cache.astype(jnp.float32)) * SOFTMAX_SCALE
    positions = jnp.arange(latent_cache.shape[1], dtype=jnp.int32)
    visible = positions[None, None, :] < cache_lengths[:, None, None]
    scores = jnp.where(visible, scores, jnp.float32(-1e30))
    largest = jnp.max(scores, axis=2, keepdims=True)
    powered = jnp.where(visible, jnp.exp(scores - largest), jnp.float32(0.0))
    probability = (powered / jnp.sum(powered, axis=2, keepdims=True)).astype(jnp.bfloat16)
    values = latent_cache[:, :, :LATENT]
    mixed = jnp.einsum("rht,rtc->rhc", probability.astype(jnp.float32), values.astype(jnp.float32))
    return mixed.astype(jnp.bfloat16)


def reference(hidden_in, expert_routes, route_scores, expert_gate, expert_up, expert_down, query_latent, latent_cache, cache_lengths):
    blocks = N_EP * N_SUB
    per_block = TOK_DEV * TOPK
    flat_routes = expert_routes.reshape(blocks, per_block)
    onehot_table = (flat_routes[:, :, None] == jnp.arange(EXPERTS, dtype=jnp.int32)[None, None, :]).astype(jnp.int32)
    earlier = jnp.cumsum(onehot_table, axis=1) - onehot_table
    slot_index = jnp.sum(earlier * onehot_table, axis=2)
    block_index = jnp.arange(blocks, dtype=jnp.int32)[:, None]
    destination = (flat_routes * (blocks * CAP) + block_index * CAP + slot_index).reshape(-1).astype(jnp.int32)
    owners = (block_index * TOK_DEV + jnp.arange(per_block, dtype=jnp.int32)[None, :] // TOPK).reshape(-1).astype(jnp.int32)
    source_rows = jnp.full((EXPERTS * blocks * CAP,), TOKENS, jnp.int32).at[destination].set(owners)
    source_rows = source_rows.reshape(EXPERTS, blocks * CAP)
    padded = jnp.concatenate([hidden_in, jnp.zeros((1, D), hidden_in.dtype)], axis=0)
    half_width = FF // N_SUB

    def one_expert(inputs):
        gate_matrix, up_matrix, down_matrix, chosen = inputs
        expert_rows = padded[chosen]
        gate_value = jnp.dot(expert_rows, gate_matrix, preferred_element_type=jnp.float32)
        up_value = jnp.dot(expert_rows, up_matrix, preferred_element_type=jnp.float32)
        hidden = (jax.nn.silu(gate_value) * up_value).astype(jnp.bfloat16)
        summed = jnp.zeros((blocks * CAP, D), jnp.float32)
        for piece_index in range(N_SUB):
            lower = piece_index * half_width
            partial_value = jnp.dot(hidden[:, lower:lower + half_width], down_matrix[lower:lower + half_width], preferred_element_type=jnp.float32).astype(jnp.bfloat16)
            summed = summed + lax.optimization_barrier(partial_value).astype(jnp.float32)
        return summed.astype(jnp.bfloat16)

    expert_out = lax.map(one_expert, (expert_gate, expert_up, expert_down, source_rows))
    picked = expert_out.reshape(-1, D)[destination].astype(jnp.float32).reshape(TOKENS, TOPK, D)
    weights = ROUTE_SCALE * route_scores / jnp.sum(route_scores, axis=1, keepdims=True)
    moe_output = jnp.sum(picked * weights[:, :, None], axis=1).astype(jnp.bfloat16)
    attention_latent = attend(query_latent, latent_cache, cache_lengths)
    return (moe_output, attention_latent)
```

```python
import jax
import jax.numpy as jnp
from jax import lax
from jax.sharding import PartitionSpec as P

LATENT = 512


SOFTMAX_SCALE = 192.0 ** (-0.5)
ROUTE_SCALE = 2.5
LANES = 128


def attend(query_latent, latent_cache, cache_lengths):
    scores = (
        jnp.einsum("rhc,rtc->rht", query_latent, latent_cache, preferred_element_type=jnp.float32)
        * SOFTMAX_SCALE
    )
    positions = jnp.arange(latent_cache.shape[1], dtype=jnp.int32)
    visible = positions[None, None, :] < cache_lengths[:, None, None]
    scores = jnp.where(visible, scores, jnp.float32(-1e30))
    largest = jnp.max(scores, axis=2, keepdims=True)
    powered = jnp.where(visible, jnp.exp(scores - largest), jnp.float32(0.0))
    probability = (powered / jnp.sum(powered, axis=2, keepdims=True)).astype(jnp.bfloat16)
    values = latent_cache[:, :, :LATENT]
    mixed = jnp.einsum("rht,rtc->rhc", probability, values, preferred_element_type=jnp.float32)
    return mixed.astype(jnp.bfloat16)


def swap(value, axis, mask):
    count = lax.axis_size(axis)
    return lax.ppermute(value, axis, [(i, i ^ mask) for i in range(count)])


def per_device(
    hidden_in,
    expert_routes,
    route_scores,
    expert_gate,
    expert_up,
    expert_down,
    query_latent,
    latent_cache,
    cache_lengths,
):
    tok_rows, model_width = hidden_in.shape
    ep_count = lax.axis_size("ep")
    inner = 4 if ep_count % 4 == 0 else 1
    outer = ep_count // inner
    experts = ep_count

    weights = ROUTE_SCALE * route_scores / jnp.sum(route_scores, axis=1, keepdims=True)
    chosen = expert_routes[:, :, None] == jnp.arange(experts, dtype=jnp.int32)[None, None, :]
    dense = jnp.sum(jnp.where(chosen, weights[:, :, None], 0.0), axis=1)
    high = lax.reduce_precision(dense, 8, 7)
    low = dense - high
    coded = jnp.concatenate([high, low], axis=1).astype(jnp.bfloat16)
    pad = -coded.shape[1] % LANES
    coded = jnp.pad(coded, ((0, 0), (0, pad)))
    own = jnp.concatenate([hidden_in, coded], axis=1)

    column = jnp.concatenate([own] + [swap(own, "ep", inner * k) for k in range(1, outer)], axis=0)
    core = jnp.concatenate([column] + [swap(column, "ep", k) for k in range(1, inner)], axis=0)
    rows = jnp.concatenate([core, swap(core, "sub", 1)], axis=0)
    half = core.shape[0]

    expert_rows, tail = rows[:, :model_width], rows[:, model_width:].astype(jnp.float32)
    me = lax.axis_index("ep")
    lane = jnp.arange(tail.shape[1], dtype=jnp.int32)
    mine = (lane == me) | (lane == me + experts)
    weight = jnp.sum(jnp.where(mine[None, :], tail, 0.0), axis=1, keepdims=True)

    gate_value = jnp.dot(expert_rows, expert_gate[0], preferred_element_type=jnp.float32)
    up_value = jnp.dot(expert_rows, expert_up[0], preferred_element_type=jnp.float32)
    hidden = (jax.nn.silu(gate_value) * up_value * weight).astype(jnp.bfloat16)
    partial = jnp.dot(hidden, expert_down[0], preferred_element_type=jnp.float32)

    other = swap(partial[half:].astype(jnp.bfloat16), "sub", 1)
    both = (partial[:half] + other.astype(jnp.float32)).astype(jnp.bfloat16)
    block = outer * tok_rows
    pieces = [both[:block]] + [swap(both[k * block : (k + 1) * block], "ep", k) for k in range(1, inner)]
    total = sum(p.astype(jnp.float32) for p in pieces).astype(jnp.bfloat16)
    pieces = [total[:tok_rows]] + [
        swap(total[k * tok_rows : (k + 1) * tok_rows], "ep", inner * k) for k in range(1, outer)
    ]
    moe_output = sum(p.astype(jnp.float32) for p in pieces).astype(jnp.bfloat16)
    attention_latent = attend(query_latent, latent_cache, cache_lengths)
    return (moe_output, attention_latent)


def solution(mesh):
    placed = (
        P(("groups", "ep", "sub"), None),
        P(("groups", "ep", "sub"), None),
        P(("groups", "ep", "sub"), None),
        P("ep", None, "sub"),
        P("ep", None, "sub"),
        P("ep", "sub", None),
        P(("groups", "ep", "sub"), None, None),
        P(("groups", "ep", "sub"), None, None),
        P(("groups", "ep", "sub")),
    )
    return jax.shard_map(
        per_device,
        mesh=mesh,
        in_specs=placed,
        out_specs=(P(("groups", "ep", "sub"), None), P(("groups", "ep", "sub"), None, None)),
        check_vma=False,
    )
```

```python
import jax
import jax.numpy as jnp
from jax import lax
from jax.experimental import pallas as pl
from jax.experimental.pallas import tpu as pltpu
from jax.sharding import PartitionSpec as P

LATENT = 512


SOFTMAX_SCALE = 192.0 ** (-0.5)
ROUTE_SCALE = 2.5
LANES = 128


def attend(query_latent, latent_cache, cache_lengths):
    scores = (
        jnp.einsum("rhc,rtc->rht", query_latent, latent_cache, preferred_element_type=jnp.float32)
        * SOFTMAX_SCALE
    )
    positions = jnp.arange(latent_cache.shape[1], dtype=jnp.int32)
    visible = positions[None, None, :] < cache_lengths[:, None, None]
    scores = jnp.where(visible, scores, jnp.float32(-1e30))
    largest = jnp.max(scores, axis=2, keepdims=True)
    powered = jnp.where(visible, jnp.exp(scores - largest), jnp.float32(0.0))
    probability = (powered / jnp.sum(powered, axis=2, keepdims=True)).astype(jnp.bfloat16)
    values = latent_cache[:, :, :LATENT]
    mixed = jnp.einsum("rht,rtc->rhc", probability, values, preferred_element_type=jnp.float32)
    return mixed.astype(jnp.bfloat16)


def rounds_up(value, step):
    return -(-value // step) * step


def pack_kernel(hidden_ref, routes_ref, scores_ref, out_ref):
    rows, model_width = hidden_ref.shape
    scores = scores_ref[...]
    routes = routes_ref[...]
    weights = ROUTE_SCALE * scores / jnp.sum(scores, axis=1, keepdims=True)
    lanes = out_ref.shape[1] - model_width
    lane = lax.broadcasted_iota(jnp.int32, (rows, lanes), 1)
    experts = lanes // 2
    dense = jnp.zeros((rows, lanes), jnp.float32)
    for k in range(routes.shape[1]):
        named = routes[:, k : k + 1]
        dense += jnp.where((lane == named) | (lane == named + experts), weights[:, k : k + 1], 0.0)
    high = dense.astype(jnp.bfloat16)
    low = (dense - high.astype(jnp.float32)).astype(jnp.bfloat16)
    out_ref[:, :model_width] = hidden_ref[...]
    out_ref[:, model_width:] = jnp.where(lane < experts, high.astype(jnp.float32), low.astype(jnp.float32)).astype(
        jnp.bfloat16
    )


def pack(hidden_in, expert_routes, route_scores, experts):
    rows, model_width = hidden_in.shape
    lanes = rounds_up(2 * experts, LANES)
    return pl.pallas_call(
        pack_kernel,
        out_shape=jax.ShapeDtypeStruct((rows, model_width + lanes), jnp.bfloat16),
        compiler_params=pltpu.CompilerParams(vmem_limit_bytes=2 << 20),
        cost_estimate=pl.CostEstimate(flops=1 << 16, bytes_accessed=4 * rows * model_width, transcendentals=0),
    )(hidden_in, expert_routes, route_scores)


def expert_kernel(me_ref, rows_ref, gate_ref, up_ref, down_ref, mine_ref, other_ref, hidden_ref):
    total, _ = rows_ref.shape
    model_width, units = gate_ref.shape
    lanes = rows_ref.shape[1] - model_width
    half = total // 2
    me = me_ref[0]
    block = min(total, 256)
    chunk = 256

    @pl.loop(0, total // block)
    def _(i):
        here = pl.ds(pl.multiple_of(i * block, block), block)
        tail = rows_ref[here, model_width:].astype(jnp.float32)
        lane = lax.broadcasted_iota(jnp.int32, (block, lanes), 1)
        taken = (lane == me) | (lane == me + lanes // 2)
        weight = jnp.sum(jnp.where(taken, tail, 0.0), axis=1, keepdims=True)
        for c in range(units // chunk):
            cols = slice(c * chunk, (c + 1) * chunk)
            x = rows_ref[here, :model_width]
            gate_value = jnp.dot(x, gate_ref[:, cols], preferred_element_type=jnp.float32)
            up_value = jnp.dot(x, up_ref[:, cols], preferred_element_type=jnp.float32)
            value = gate_value / (1.0 + jnp.exp(-gate_value)) * up_value * weight
            hidden_ref[here, cols] = value.astype(jnp.bfloat16)

    step = 512

    @pl.loop(0, model_width // step)
    def _(c):
        cols = pl.ds(pl.multiple_of(c * step, step), step)
        for i in range(total // block):
            value = jnp.dot(
                hidden_ref[i * block : (i + 1) * block, :], down_ref[:, cols], preferred_element_type=jnp.float32
            ).astype(jnp.bfloat16)
            low, high = i * block, (i + 1) * block
            if high <= half:
                mine_ref[low:high, cols] = value
            elif low >= half:
                other_ref[low - half : high - half, cols] = value
            else:
                mine_ref[low:half, cols] = value[: half - low]
                other_ref[: high - half, cols] = value[half - low :]


def expert_block(rows, expert_gate, expert_up, expert_down, me):
    total, width = rows.shape
    model_width, units = expert_gate.shape
    half = total // 2
    vmem = pl.BlockSpec(memory_space=pltpu.VMEM)
    out = jax.ShapeDtypeStruct((half, model_width), jnp.bfloat16)
    weights = [pltpu.with_memory_space_constraint(w, pltpu.VMEM) for w in (expert_gate, expert_up, expert_down)]
    return pl.pallas_call(
        expert_kernel,
        out_shape=(out, out),
        in_specs=[pl.BlockSpec(memory_space=pltpu.SMEM), vmem, vmem, vmem, vmem],
        out_specs=(vmem, vmem),
        scratch_shapes=[pltpu.VMEM((total, units), jnp.bfloat16)],
        compiler_params=pltpu.CompilerParams(vmem_limit_bytes=(16 << 20) + 8 * total * width),
        cost_estimate=pl.CostEstimate(
            flops=6 * total * model_width * units,
            bytes_accessed=6 * model_width * units + 4 * total * width,
            transcendentals=total * units,
        ),
    )(me.reshape(1), rows, *weights)


def per_device(
    hidden_in,
    expert_routes,
    route_scores,
    expert_gate,
    expert_up,
    expert_down,
    query_latent,
    latent_cache,
    cache_lengths,
):
    tok_rows, model_width = hidden_in.shape
    ep_count, sub_count = lax.axis_size("ep"), lax.axis_size("sub")
    inner = 4 if ep_count % 4 == 0 else 1
    outer = ep_count // inner

    def swap(value, even, odd):
        pairs = [
            (i * sub_count + s, (i ^ (odd if s else even)) * sub_count + s)
            for i in range(ep_count)
            for s in range(sub_count)
        ]
        return lax.ppermute(value, ("ep", "sub"), pairs)

    def first(value, k):
        return swap(value, inner * k, k if inner == outer else inner * k)

    def second(value, k):
        return swap(value, k, inner * k if inner == outer else k)

    def over_cores(value):
        return lax.ppermute(value, "sub", [(i, i ^ 1) for i in range(sub_count)])

    def order(count):
        return list(range(1, count))[::-1]

    own = pack(hidden_in, expert_routes, route_scores, ep_count)
    near = {k: first(own, k) for k in order(outer)}
    side = {k: second(own, k) for k in order(inner)}
    column = jnp.concatenate([near[k] for k in range(1, outer)], axis=0)
    far = {k: second(column, k) for k in (order(inner)[1:] + order(inner)[:1])}
    core = jnp.concatenate(
        [own, column] + [side[k] for k in range(1, inner)] + [far[k] for k in range(1, inner)], axis=0
    )
    rows = jnp.concatenate([core, over_cores(core)], axis=0)

    mine, other = expert_block(rows, expert_gate[0], expert_up[0], expert_down[0], lax.axis_index("ep"))

    both = (mine.astype(jnp.float32) + over_cores(other).astype(jnp.float32)).astype(jnp.bfloat16)
    place = {}
    at = outer * tok_rows
    for k in range(1, inner):
        place["side", k] = both[at : at + tok_rows]
        at += tok_rows
    for k in range(1, inner):
        place["far", k] = both[at : at + (outer - 1) * tok_rows]
        at += (outer - 1) * tok_rows
    far = [second(place["far", k], k) for k in order(inner)]
    side = [second(place["side", k], k) for k in order(inner)]
    column = (
        both[tok_rows : outer * tok_rows].astype(jnp.float32) + sum(p.astype(jnp.float32) for p in far)
    ).astype(jnp.bfloat16)
    near = [first(column[(k - 1) * tok_rows : k * tok_rows], k) for k in order(outer)]
    moe_output = (
        both[:tok_rows].astype(jnp.float32) + sum(p.astype(jnp.float32) for p in side + near)
    ).astype(jnp.bfloat16)
    attention_latent = attend(query_latent, latent_cache, cache_lengths)
    return (moe_output, attention_latent)


def solution(mesh):
    placed = (
        P(("groups", "ep", "sub"), None),
        P(("groups", "ep", "sub"), None),
        P(("groups", "ep", "sub"), None),
        P("ep", None, "sub"),
        P("ep", None, "sub"),
        P("ep", "sub", None),
        P(("groups", "ep", "sub"), None, None),
        P(("groups", "ep", "sub"), None, None),
        P(("groups", "ep", "sub")),
    )
    return jax.shard_map(
        per_device,
        mesh=mesh,
        in_specs=placed,
        out_specs=(P(("groups", "ep", "sub"), None), P(("groups", "ep", "sub"), None, None)),
        check_vma=False,
    )
```

```python
import functools

import jax
import jax.numpy as jnp
from jax import lax
from jax.experimental import pallas as pl
from jax.experimental.pallas import tpu as pltpu
from jax.sharding import PartitionSpec as P

LATENT = 512


SOFTMAX_SCALE = 192.0 ** (-0.5)
ROUTE_SCALE = 2.5
LANES = 128


VMEM = pl.BlockSpec(memory_space=pltpu.VMEM)
SMEM = pl.BlockSpec(memory_space=pltpu.SMEM)
ANY = pl.BlockSpec(memory_space=pl.ANY)
HBM = pl.BlockSpec(memory_space=pltpu.HBM)


def in_vmem(shape, dtype):
    return pltpu.VMEM(shape, dtype)


def stored(value):
    return pltpu.with_memory_space_constraint(value, pltpu.HBM)


def held(value):
    return pltpu.with_memory_space_constraint(value, pltpu.VMEM)


def attend_kernel(lengths_ref, query_ref, cache_ref, gate_ref, up_ref, down_ref, after_ref, out_ref, *rest):
    copies = [
        pltpu.make_async_copy(source, target, rest[3].at[i])
        for i, (source, target) in enumerate(zip((gate_ref, up_ref, down_ref), rest[:3], strict=True))
    ]
    for copy in copies:
        copy.start()
    latent = out_ref.shape[2]
    for r in range(query_ref.shape[0]):
        query, cache = query_ref[r], cache_ref[r]
        scores = SOFTMAX_SCALE * lax.dot_general(
            query, cache, (((0,), (0,)), ((), ())), preferred_element_type=jnp.float32
        )
        visible = lax.broadcasted_iota(jnp.int32, scores.shape, 1) < lengths_ref[r]
        scores = jnp.where(visible, scores, -1e30)
        largest = jnp.max(scores, axis=1, keepdims=True)
        powered = jnp.where(visible, jnp.exp(scores - largest), 0.0)
        probability = (powered / jnp.sum(powered, axis=1, keepdims=True)).astype(jnp.bfloat16)
        out_ref[r] = lax.dot_general(
            probability, cache[:latent], (((1,), (1,)), ((), ())), preferred_element_type=jnp.float32
        ).astype(jnp.bfloat16)
    for copy in copies:
        copy.wait()


def attend(query_latent, latent_cache, cache_lengths, weights, after):
    rows, heads, entries = query_latent.shape
    positions = latent_cache.shape[1]
    return pl.pallas_call(
        attend_kernel,
        out_shape=(
            jax.ShapeDtypeStruct((rows, heads, LATENT), jnp.bfloat16),
            *(in_vmem(w.shape, w.dtype) for w in weights),
        ),
        in_specs=[SMEM, VMEM, VMEM, HBM, HBM, HBM, ANY],
        out_specs=(VMEM,) * 4,
        scratch_shapes=[pltpu.SemaphoreType.DMA((3,))],
        compiler_params=pltpu.CompilerParams(vmem_limit_bytes=8 << 20),
        cost_estimate=pl.CostEstimate(
            flops=4 * rows * heads * positions * entries,
            bytes_accessed=2 * sum(w.size for w in weights),
            transcendentals=rows * heads * positions,
        ),
    )(cache_lengths, jnp.swapaxes(query_latent, 1, 2), jnp.swapaxes(latent_cache, 1, 2), *(stored(w) for w in weights), after)


def rounds_up(value, step):
    return -(-value // step) * step


def pack_kernel(hidden_ref, routes_ref, scores_ref, out_ref, rows_ref, named_ref, affinity_ref, sems):
    rows, model_width = hidden_ref.shape
    copies = [
        pltpu.make_async_copy(source, target, sems.at[i])
        for i, (source, target) in enumerate(
            ((routes_ref, named_ref), (scores_ref, affinity_ref), (hidden_ref, rows_ref))
        )
    ]
    for copy in copies:
        copy.start()
    copies[0].wait()
    copies[1].wait()
    scores = affinity_ref[...]
    routes = named_ref[...]
    weights = ROUTE_SCALE * scores / jnp.sum(scores, axis=1, keepdims=True)
    lanes = out_ref.shape[1] - model_width
    lane = lax.broadcasted_iota(jnp.int32, (rows, lanes), 1)
    experts = lanes // 2
    dense = jnp.zeros((rows, lanes), jnp.float32)
    for k in range(routes.shape[1]):
        named = routes[:, k : k + 1]
        dense += jnp.where((lane == named) | (lane == named + experts), weights[:, k : k + 1], 0.0)
    high = dense.astype(jnp.bfloat16).astype(jnp.float32)
    out_ref[:, model_width:] = jnp.where(lane < experts, high, dense - high).astype(jnp.bfloat16)
    copies[2].wait()
    out_ref[:, :model_width] = rows_ref[...]


def pack(hidden_in, expert_routes, route_scores, experts):
    rows, model_width = hidden_in.shape
    lanes = rounds_up(2 * experts, LANES)
    return pl.pallas_call(
        pack_kernel,
        out_shape=in_vmem((rows, model_width + lanes), jnp.bfloat16),
        in_specs=[HBM] * 3,
        out_specs=VMEM,
        scratch_shapes=[
            pltpu.VMEM(hidden_in.shape, hidden_in.dtype),
            pltpu.VMEM(expert_routes.shape, expert_routes.dtype),
            pltpu.VMEM(route_scores.shape, route_scores.dtype),
            pltpu.SemaphoreType.DMA((3,)),
        ],
        compiler_params=pltpu.CompilerParams(vmem_limit_bytes=4 << 20),
        cost_estimate=pl.CostEstimate(flops=1 << 16, bytes_accessed=4 * rows * model_width, transcendentals=0),
    )(stored(hidden_in), stored(expert_routes), stored(route_scores))


def expert_kernel(me_ref, rows_ref, gate_ref, up_ref, down_ref, mine_ref, other_ref, hidden_ref):
    total, _ = rows_ref.shape
    model_width, units = gate_ref.shape
    lanes = rows_ref.shape[1] - model_width
    half = total // 2
    me = me_ref[0]
    block = min(total, 256)
    chunk = 256

    @pl.loop(0, total // block)
    def _(i):
        here = pl.ds(pl.multiple_of(i * block, block), block)
        tail = rows_ref[here, model_width:].astype(jnp.float32)
        lane = lax.broadcasted_iota(jnp.int32, (block, lanes), 1)
        taken = (lane == me) | (lane == me + lanes // 2)
        weight = jnp.sum(jnp.where(taken, tail, 0.0), axis=1, keepdims=True)
        for c in range(units // chunk):
            cols = slice(c * chunk, (c + 1) * chunk)
            x = rows_ref[here, :model_width]
            gate_value = jnp.dot(x, gate_ref[:, cols], preferred_element_type=jnp.float32)
            up_value = jnp.dot(x, up_ref[:, cols], preferred_element_type=jnp.float32)
            value = gate_value / (1.0 + jnp.exp(-gate_value)) * up_value * weight
            hidden_ref[here, cols] = value.astype(jnp.bfloat16)

    step = 512

    @pl.loop(0, model_width // step)
    def _(c):
        cols = pl.ds(pl.multiple_of(c * step, step), step)
        for i in range(total // block):
            value = jnp.dot(
                hidden_ref[i * block : (i + 1) * block, :], down_ref[:, cols], preferred_element_type=jnp.float32
            ).astype(jnp.bfloat16)
            low, high = i * block, (i + 1) * block
            if high <= half:
                mine_ref[low:high, cols] = value
            elif low >= half:
                other_ref[low - half : high - half, cols] = value
            else:
                mine_ref[low:half, cols] = value[: half - low]
                other_ref[: high - half, cols] = value[half - low :]


def expert_block(rows, expert_gate, expert_up, expert_down, me):
    total, width = rows.shape
    model_width, units = expert_gate.shape
    out = in_vmem((total // 2, model_width), jnp.bfloat16)
    return pl.pallas_call(
        expert_kernel,
        out_shape=(out, out),
        in_specs=[SMEM] + [VMEM] * 4,
        out_specs=(VMEM, VMEM),
        scratch_shapes=[pltpu.VMEM((total, units), jnp.bfloat16)],
        compiler_params=pltpu.CompilerParams(vmem_limit_bytes=(8 << 20) + 4 * total * units),
        cost_estimate=pl.CostEstimate(
            flops=6 * total * model_width * units,
            bytes_accessed=4 * total * width,
            transcendentals=total * units,
        ),
    )(me.reshape(1), held(rows), *(held(w) for w in (expert_gate, expert_up, expert_down)))


def add_kernel(base_count, sizes, *refs):
    values = [ref[...].astype(jnp.float32) for ref in refs[:base_count]]
    total = values[0]
    for value in values[1:]:
        total += value
    low = 0
    for out_ref, size in zip(refs[base_count:], sizes, strict=True):
        out_ref[...] = total[low : low + size].astype(jnp.bfloat16)
        low += size


def add(values, sizes, last=False):
    rows, width = values[0].shape
    shape = jax.ShapeDtypeStruct if last else in_vmem
    return pl.pallas_call(
        functools.partial(add_kernel, len(values), sizes),
        out_shape=tuple(shape((size, width), jnp.bfloat16) for size in sizes),
        in_specs=[VMEM] * len(values),
        out_specs=(VMEM,) * len(sizes),
        compiler_params=pltpu.CompilerParams(vmem_limit_bytes=(4 << 20) + 8 * rows * width),
        cost_estimate=pl.CostEstimate(
            flops=len(values) * rows * width,
            bytes_accessed=2 * len(values) * rows * width,
            transcendentals=0,
        ),
    )(*(held(v) for v in values))


def per_device(
    hidden_in,
    expert_routes,
    route_scores,
    expert_gate,
    expert_up,
    expert_down,
    query_latent,
    latent_cache,
    cache_lengths,
):
    tok_rows, model_width = hidden_in.shape
    ep_count, sub_count = lax.axis_size("ep"), lax.axis_size("sub")
    inner = 4 if ep_count % 4 == 0 else 1
    outer = ep_count // inner

    def swap(value, even, odd):
        pairs = [
            (i * sub_count + s, (i ^ (odd if s else even)) * sub_count + s)
            for i in range(ep_count)
            for s in range(sub_count)
        ]
        return lax.ppermute(value, ("ep", "sub"), pairs)

    def first(value, k):
        return swap(value, inner * k, k if inner == outer else inner * k)

    def second(value, k):
        return swap(value, k, inner * k if inner == outer else k)

    def over_cores(value):
        return lax.ppermute(value, "sub", [(i, i ^ 1) for i in range(sub_count)])

    def order(count):
        return list(range(1, count))[::-1]

    own = pack(hidden_in, expert_routes, route_scores, ep_count)
    near = {k: first(own, k) for k in order(outer)}
    side = {k: second(own, k) for k in order(inner)}
    column = jnp.concatenate([near[k] for k in range(1, outer)], axis=0)
    far = {k: second(column, k) for k in (order(inner)[1:] + order(inner)[:1])}
    attention_latent, *weights = attend(
        query_latent,
        latent_cache,
        cache_lengths,
        (expert_gate[0], expert_up[0], expert_down[0]),
        column,
    )
    early = jnp.concatenate([own, column] + [side[k] for k in range(1, inner)], axis=0)
    pieces = [early] + [far[k] for k in range(1, inner)]
    rows = jnp.concatenate(pieces + [over_cores(p) for p in pieces], axis=0)

    mine, other = expert_block(rows, *weights, lax.axis_index("ep"))

    step = (outer - 1) * tok_rows
    sizes = [tok_rows, step] + [tok_rows] * (inner - 1) + [step] * (inner - 1)
    kept, column, *parts = add([mine, over_cores(other)], sizes)
    far = [second(parts[inner - 1 + k - 1], k) for k in order(inner)]
    side = [second(parts[k - 1], k) for k in order(inner)]
    near = add([column, *far], [tok_rows] * (outer - 1))
    near = [first(near[k - 1], k) for k in order(outer)]
    (moe_output,) = add([kept, *side, *near], [tok_rows], last=True)
    return (moe_output, attention_latent)


def solution(mesh):
    placed = (
        P(("groups", "ep", "sub"), None),
        P(("groups", "ep", "sub"), None),
        P(("groups", "ep", "sub"), None),
        P("ep", None, "sub"),
        P("ep", None, "sub"),
        P("ep", "sub", None),
        P(("groups", "ep", "sub"), None, None),
        P(("groups", "ep", "sub"), None, None),
        P(("groups", "ep", "sub")),
    )
    return jax.shard_map(
        per_device,
        mesh=mesh,
        in_specs=placed,
        out_specs=(P(("groups", "ep", "sub"), None), P(("groups", "ep", "sub"), None, None)),
        check_vma=False,
    )
```

```python
import functools

import jax
import jax.numpy as jnp
from jax import lax
from jax.experimental import pallas as pl
from jax.experimental.pallas import tpu as pltpu
from jax.sharding import PartitionSpec as P

LATENT = 512


SOFTMAX_SCALE = 192.0 ** (-0.5)
ROUTE_SCALE = 2.5
LANES = 128
FETCHES = 2


VMEM = pl.BlockSpec(memory_space=pltpu.VMEM)
SMEM = pl.BlockSpec(memory_space=pltpu.SMEM)
ANY = pl.BlockSpec(memory_space=pl.ANY)
HBM = pl.BlockSpec(memory_space=pltpu.HBM)


def in_vmem(shape, dtype):
    return pltpu.VMEM(shape, dtype)


def stored(value):
    return pltpu.with_memory_space_constraint(value, pltpu.HBM)


def held(value):
    return pltpu.with_memory_space_constraint(value, pltpu.VMEM)


def attend_kernel(
    lengths_hbm, query_hbm, cache_hbm, gate_hbm, up_hbm, down_hbm, after_ref,
    out_ref, gate_ref, up_ref, down_ref, token_ref, lengths_ref, query_ref, cache_ref, sems,
):
    pairs = [(lengths_hbm, lengths_ref), (query_hbm, query_ref), (cache_hbm, cache_ref)]
    for source, target in ((gate_hbm, gate_ref), (up_hbm, up_ref), (down_hbm, down_ref)):
        rows = source.shape[0] // FETCHES
        pairs += [(source.at[pl.ds(i * rows, rows)], target.at[pl.ds(i * rows, rows)]) for i in range(FETCHES)]
    copies = [pltpu.make_async_copy(s, t, sems.at[i]) for i, (s, t) in enumerate(pairs)]
    for copy in copies:
        copy.start()
    for copy in copies[:3]:
        copy.wait()
    latent = out_ref.shape[2]
    for r in range(query_ref.shape[0]):
        query, cache = query_ref[r], cache_ref[r]
        scores = SOFTMAX_SCALE * lax.dot_general(
            query, cache, (((0,), (0,)), ((), ())), preferred_element_type=jnp.float32
        )
        visible = lax.broadcasted_iota(jnp.int32, scores.shape, 1) < lengths_ref[r]
        scores = jnp.where(visible, scores, -1e30)
        largest = jnp.max(scores, axis=1, keepdims=True)
        powered = jnp.where(visible, jnp.exp(scores - largest), 0.0)
        probability = (powered / jnp.sum(powered, axis=1, keepdims=True)).astype(jnp.bfloat16)
        out_ref[r] = lax.dot_general(
            probability, cache[:latent], (((1,), (1,)), ((), ())), preferred_element_type=jnp.float32
        ).astype(jnp.bfloat16)
    token_ref[...] = jnp.zeros_like(token_ref)
    for copy in copies[3:]:
        copy.wait()


def attend(query_latent, latent_cache, cache_lengths, weights, after):
    rows, heads, entries = query_latent.shape
    positions = latent_cache.shape[1]
    query, cache = jnp.swapaxes(query_latent, 1, 2), jnp.swapaxes(latent_cache, 1, 2)
    operands = (cache_lengths, query, cache, *weights)
    return pl.pallas_call(
        attend_kernel,
        out_shape=(
            jax.ShapeDtypeStruct((rows, heads, LATENT), jnp.bfloat16),
            *(in_vmem(w.shape, w.dtype) for w in weights),
            in_vmem((8, LANES), jnp.float32),
        ),
        in_specs=[HBM] * 6 + [ANY],
        out_specs=(VMEM,) * 5,
        scratch_shapes=[
            pltpu.SMEM(cache_lengths.shape, jnp.int32),
            pltpu.VMEM(query.shape, query.dtype),
            pltpu.VMEM(cache.shape, cache.dtype),
            pltpu.SemaphoreType.DMA((3 + 3 * FETCHES,)),
        ],
        compiler_params=pltpu.CompilerParams(vmem_limit_bytes=12 << 20),
        cost_estimate=pl.CostEstimate(
            flops=4 * rows * heads * positions * entries,
            bytes_accessed=2 * sum(w.size for w in weights),
            transcendentals=rows * heads * positions,
        ),
    )(*(stored(v) for v in operands), after)


def rounds_up(value, step):
    return -(-value // step) * step


def pack_kernel(hidden_ref, routes_ref, scores_ref, out_ref, rows_ref, named_ref, affinity_ref, sems):
    rows, model_width = hidden_ref.shape
    copies = [
        pltpu.make_async_copy(source, target, sems.at[i])
        for i, (source, target) in enumerate(
            ((routes_ref, named_ref), (scores_ref, affinity_ref), (hidden_ref, rows_ref))
        )
    ]
    for copy in copies:
        copy.start()
    copies[0].wait()
    copies[1].wait()
    scores = affinity_ref[...]
    routes = named_ref[...]
    weights = ROUTE_SCALE * scores / jnp.sum(scores, axis=1, keepdims=True)
    lanes = out_ref.shape[1] - model_width
    lane = lax.broadcasted_iota(jnp.int32, (rows, lanes), 1)
    experts = lanes // 2
    dense = jnp.zeros((rows, lanes), jnp.float32)
    for k in range(routes.shape[1]):
        named = routes[:, k : k + 1]
        dense += jnp.where((lane == named) | (lane == named + experts), weights[:, k : k + 1], 0.0)
    high = dense.astype(jnp.bfloat16).astype(jnp.float32)
    out_ref[:, model_width:] = jnp.where(lane < experts, high, dense - high).astype(jnp.bfloat16)
    copies[2].wait()
    out_ref[:, :model_width] = rows_ref[...]


def pack(hidden_in, expert_routes, route_scores, experts):
    rows, model_width = hidden_in.shape
    lanes = rounds_up(2 * experts, LANES)
    return pl.pallas_call(
        pack_kernel,
        out_shape=in_vmem((rows, model_width + lanes), jnp.bfloat16),
        in_specs=[HBM] * 3,
        out_specs=VMEM,
        scratch_shapes=[
            pltpu.VMEM(hidden_in.shape, hidden_in.dtype),
            pltpu.VMEM(expert_routes.shape, expert_routes.dtype),
            pltpu.VMEM(route_scores.shape, route_scores.dtype),
            pltpu.SemaphoreType.DMA((3,)),
        ],
        compiler_params=pltpu.CompilerParams(vmem_limit_bytes=4 << 20),
        cost_estimate=pl.CostEstimate(flops=1 << 16, bytes_accessed=4 * rows * model_width, transcendentals=0),
    )(stored(hidden_in), stored(expert_routes), stored(route_scores))


def join_kernel(*refs):
    value = jnp.concatenate([ref[...].astype(jnp.float32) for ref in refs[:-1]], axis=0)
    refs[-1][...] = value.astype(jnp.bfloat16)


def join(pieces):
    total, width = sum(p.shape[0] for p in pieces), pieces[0].shape[1]
    return pl.pallas_call(
        join_kernel,
        out_shape=in_vmem((total, width), jnp.bfloat16),
        in_specs=[VMEM] * len(pieces),
        out_specs=VMEM,
        compiler_params=pltpu.CompilerParams(vmem_limit_bytes=(2 << 20) + 8 * total * width),
        cost_estimate=pl.CostEstimate(flops=total * width, bytes_accessed=4 * total * width, transcendentals=0),
    )(*(held(p) for p in pieces))


def tie_kernel(value_ref, after_ref, out_ref):
    pass


def tie(value, after):
    return pl.pallas_call(
        tie_kernel,
        out_shape=in_vmem(value.shape, value.dtype),
        in_specs=[VMEM, VMEM],
        out_specs=VMEM,
        input_output_aliases={0: 0},
        compiler_params=pltpu.CompilerParams(vmem_limit_bytes=1 << 20),
        cost_estimate=pl.CostEstimate(flops=0, bytes_accessed=0, transcendentals=0),
    )(held(value), held(after))


def expert_kernel(count, *refs):
    pieces = refs[:count]
    gate_ref, up_ref, down_ref, mine_ref, other_ref, rows_ref, hidden_ref = refs[count:]
    total, _ = rows_ref.shape
    model_width, units = gate_ref.shape
    lanes = rows_ref.shape[1] - model_width
    half = total // 2
    me = lax.axis_index("ep")
    block = min(total, 256)
    chunk = 256

    low = 0
    for piece in pieces:
        rows_ref[low : low + piece.shape[0], :] = piece[...]
        low += piece.shape[0]

    @pl.loop(0, total // block)
    def _(i):
        here = pl.ds(pl.multiple_of(i * block, block), block)
        tail = rows_ref[here, model_width:].astype(jnp.float32)
        lane = lax.broadcasted_iota(jnp.int32, (block, lanes), 1)
        taken = (lane == me) | (lane == me + lanes // 2)
        weight = jnp.sum(jnp.where(taken, tail, 0.0), axis=1, keepdims=True)
        for c in range(units // chunk):
            cols = slice(c * chunk, (c + 1) * chunk)
            x = rows_ref[here, :model_width]
            gate_value = jnp.dot(x, gate_ref[:, cols], preferred_element_type=jnp.float32)
            up_value = jnp.dot(x, up_ref[:, cols], preferred_element_type=jnp.float32)
            value = gate_value / (1.0 + jnp.exp(-gate_value)) * up_value * weight
            hidden_ref[here, cols] = value.astype(jnp.bfloat16)

    step = 512

    @pl.loop(0, model_width // step)
    def _(c):
        cols = pl.ds(pl.multiple_of(c * step, step), step)
        for i in range(total // block):
            value = jnp.dot(
                hidden_ref[i * block : (i + 1) * block, :], down_ref[:, cols], preferred_element_type=jnp.float32
            ).astype(jnp.bfloat16)
            low, high = i * block, (i + 1) * block
            if high <= half:
                mine_ref[low:high, cols] = value
            elif low >= half:
                other_ref[low - half : high - half, cols] = value
            else:
                mine_ref[low:half, cols] = value[: half - low]
                other_ref[: high - half, cols] = value[half - low :]


def expert_block(pieces, expert_gate, expert_up, expert_down):
    total, width = sum(p.shape[0] for p in pieces), pieces[0].shape[1]
    model_width, units = expert_gate.shape
    out = in_vmem((total // 2, model_width), jnp.bfloat16)
    return pl.pallas_call(
        functools.partial(expert_kernel, len(pieces)),
        out_shape=(out, out),
        in_specs=[VMEM] * (len(pieces) + 3),
        out_specs=(VMEM, VMEM),
        scratch_shapes=[pltpu.VMEM((total, width), jnp.bfloat16), pltpu.VMEM((total, units), jnp.bfloat16)],
        compiler_params=pltpu.CompilerParams(vmem_limit_bytes=(8 << 20) + 4 * total * units + 2 * total * width),
        cost_estimate=pl.CostEstimate(
            flops=6 * total * model_width * units,
            bytes_accessed=4 * total * width,
            transcendentals=total * units,
        ),
    )(*(held(p) for p in pieces), *(held(w) for w in (expert_gate, expert_up, expert_down)))


def add_kernel(count, rows, sizes, *refs):
    total = None
    for ref, (low, high) in zip(refs[:count], rows, strict=True):
        value = ref[...].astype(jnp.float32)[low:high]
        total = value if total is None else total + value
    low = 0
    for out_ref, size in zip(refs[count:], sizes, strict=True):
        out_ref[...] = total[low : low + size].astype(jnp.bfloat16)
        low += size


def add(values, rows, sizes, last=False):
    width = values[0].shape[1]
    shape = jax.ShapeDtypeStruct if last else in_vmem
    elements = sum(v.size for v in values)
    return pl.pallas_call(
        functools.partial(add_kernel, len(values), rows, sizes),
        out_shape=tuple(shape((size, width), jnp.bfloat16) for size in sizes),
        in_specs=[VMEM] * len(values),
        out_specs=(VMEM,) * len(sizes),
        compiler_params=pltpu.CompilerParams(vmem_limit_bytes=(4 << 20) + 8 * values[0].size),
        cost_estimate=pl.CostEstimate(flops=elements, bytes_accessed=2 * elements, transcendentals=0),
    )(*(held(v) for v in values))


def per_device(
    hidden_in,
    expert_routes,
    route_scores,
    expert_gate,
    expert_up,
    expert_down,
    query_latent,
    latent_cache,
    cache_lengths,
):
    tok_rows, model_width = hidden_in.shape
    ep_count, sub_count = lax.axis_size("ep"), lax.axis_size("sub")
    inner = 4
    outer = ep_count // inner

    def swap(value, even, odd):
        pairs = [
            (i * sub_count + s, (i ^ (odd if s else even)) * sub_count + s)
            for i in range(ep_count)
            for s in range(sub_count)
        ]
        return lax.ppermute(value, ("ep", "sub"), pairs)

    def first(value, k):
        return swap(value, inner * k, k if inner == outer else inner * k)

    def second(value, k):
        return swap(value, k, inner * k if inner == outer else k)

    def over_cores(value):
        return lax.ppermute(value, "sub", [(i, i ^ 1) for i in range(sub_count)])

    own = pack(hidden_in, expert_routes, route_scores, ep_count)
    near = {k: first(own, k) for k in range(outer - 1, 0, -1)}
    block = join([own] + [near[k] for k in range(1, outer)])
    steps = [*range(inner - 2, 0, -1), inner - 1]
    far = {k: second(block, k) for k in steps}
    attention_latent, *weights, token = attend(
        query_latent,
        latent_cache,
        cache_lengths,
        (expert_gate[0], expert_up[0], expert_down[0]),
        block,
    )
    pieces = [block] + [tie(far[k], token) for k in range(1, inner)]
    pieces += [over_cores(p) for p in pieces]
    mine, other = expert_block(pieces, *weights)

    size = outer * tok_rows
    kept, column, *parts = add(
        [mine, over_cores(other)], [(0, size * inner)] * 2, [tok_rows, size - tok_rows] + [size] * (inner - 1)
    )
    far = [second(parts[k - 1], k) for k in steps]
    near = add(
        [column, *far], [(0, size - tok_rows)] + [(tok_rows, size)] * len(far), [tok_rows] * (outer - 1)
    )
    near = [first(near[k - 1], k) for k in range(outer - 1, 0, -1)]
    (moe_output,) = add([kept, *far, *near], [(0, tok_rows)] * (1 + len(far) + len(near)), [tok_rows], last=True)
    return (moe_output, attention_latent)


def solution(mesh):
    placed = (
        P(("groups", "ep", "sub"), None),
        P(("groups", "ep", "sub"), None),
        P(("groups", "ep", "sub"), None),
        P("ep", None, "sub"),
        P("ep", None, "sub"),
        P("ep", "sub", None),
        P(("groups", "ep", "sub"), None, None),
        P(("groups", "ep", "sub"), None, None),
        P(("groups", "ep", "sub")),
    )
    return jax.shard_map(
        per_device,
        mesh=mesh,
        in_specs=placed,
        out_specs=(P(("groups", "ep", "sub"), None), P(("groups", "ep", "sub"), None, None)),
        check_vma=False,
    )
```

```python
import functools

import jax
import jax.numpy as jnp
from jax import lax
from jax.experimental import pallas as pl
from jax.experimental.pallas import tpu as pltpu
from jax.sharding import PartitionSpec as P

LATENT = 512


SOFTMAX_SCALE = 192.0 ** (-0.5)
ROUTE_SCALE = 2.5
LANES = 128
FETCHES = 2


VMEM = pl.BlockSpec(memory_space=pltpu.VMEM)
SMEM = pl.BlockSpec(memory_space=pltpu.SMEM)
ANY = pl.BlockSpec(memory_space=pl.ANY)
HBM = pl.BlockSpec(memory_space=pltpu.HBM)


def in_vmem(shape, dtype):
    return pltpu.VMEM(shape, dtype)


def stored(value):
    return pltpu.with_memory_space_constraint(value, pltpu.HBM)


def held(value):
    return pltpu.with_memory_space_constraint(value, pltpu.VMEM)


def attend_kernel(
    lengths_hbm, query_hbm, cache_hbm, gate_hbm, up_hbm, down_hbm, after_ref,
    out_ref, gate_ref, up_ref, down_ref, token_ref, lengths_ref, query_ref, cache_ref, sems,
):
    pairs = [(lengths_hbm, lengths_ref), (query_hbm, query_ref), (cache_hbm, cache_ref)]
    for source, target in ((gate_hbm, gate_ref), (up_hbm, up_ref), (down_hbm, down_ref)):
        rows = source.shape[0] // FETCHES
        pairs += [(source.at[pl.ds(i * rows, rows)], target.at[pl.ds(i * rows, rows)]) for i in range(FETCHES)]
    copies = [pltpu.make_async_copy(s, t, sems.at[i]) for i, (s, t) in enumerate(pairs)]
    for copy in copies:
        copy.start()
    for copy in copies[:3]:
        copy.wait()
    latent = out_ref.shape[2]
    for r in range(query_ref.shape[0]):
        query, cache = query_ref[r], cache_ref[r]
        scores = SOFTMAX_SCALE * lax.dot_general(
            query, cache, (((0,), (0,)), ((), ())), preferred_element_type=jnp.float32
        )
        visible = lax.broadcasted_iota(jnp.int32, scores.shape, 1) < lengths_ref[r]
        scores = jnp.where(visible, scores, -1e30)
        largest = jnp.max(scores, axis=1, keepdims=True)
        powered = jnp.where(visible, jnp.exp(scores - largest), 0.0)
        probability = (powered / jnp.sum(powered, axis=1, keepdims=True)).astype(jnp.bfloat16)
        out_ref[r] = lax.dot_general(
            probability, cache[:latent], (((1,), (1,)), ((), ())), preferred_element_type=jnp.float32
        ).astype(jnp.bfloat16)
    token_ref[...] = jnp.zeros_like(token_ref)
    for copy in copies[3:]:
        copy.wait()


def attend(query_latent, latent_cache, cache_lengths, weights, after):
    rows, heads, entries = query_latent.shape
    positions = latent_cache.shape[1]
    query, cache = jnp.swapaxes(query_latent, 1, 2), jnp.swapaxes(latent_cache, 1, 2)
    operands = (cache_lengths, query, cache, *weights)
    return pl.pallas_call(
        attend_kernel,
        out_shape=(
            jax.ShapeDtypeStruct((rows, heads, LATENT), jnp.bfloat16),
            *(in_vmem(w.shape, w.dtype) for w in weights),
            in_vmem((8, LANES), jnp.float32),
        ),
        in_specs=[HBM] * 6 + [ANY],
        out_specs=(VMEM,) * 5,
        scratch_shapes=[
            pltpu.SMEM(cache_lengths.shape, jnp.int32),
            pltpu.VMEM(query.shape, query.dtype),
            pltpu.VMEM(cache.shape, cache.dtype),
            pltpu.SemaphoreType.DMA((3 + 3 * FETCHES,)),
        ],
        compiler_params=pltpu.CompilerParams(vmem_limit_bytes=12 << 20),
        cost_estimate=pl.CostEstimate(
            flops=4 * rows * heads * positions * entries,
            bytes_accessed=2 * sum(w.size for w in weights),
            transcendentals=rows * heads * positions,
        ),
    )(*(stored(v) for v in operands), after)


def rounds_up(value, step):
    return -(-value // step) * step


def pack_kernel(hidden_ref, routes_ref, scores_ref, out_ref, rows_ref, named_ref, affinity_ref, sems):
    rows, model_width = hidden_ref.shape
    copies = [
        pltpu.make_async_copy(source, target, sems.at[i])
        for i, (source, target) in enumerate(
            ((routes_ref, named_ref), (scores_ref, affinity_ref), (hidden_ref, rows_ref))
        )
    ]
    for copy in copies:
        copy.start()
    copies[0].wait()
    copies[1].wait()
    scores = affinity_ref[...]
    routes = named_ref[...]
    weights = ROUTE_SCALE * scores / jnp.sum(scores, axis=1, keepdims=True)
    lanes = out_ref.shape[1] - model_width
    lane = lax.broadcasted_iota(jnp.int32, (rows, lanes), 1)
    experts = lanes // 2
    dense = jnp.zeros((rows, lanes), jnp.float32)
    for k in range(routes.shape[1]):
        named = routes[:, k : k + 1]
        dense += jnp.where((lane == named) | (lane == named + experts), weights[:, k : k + 1], 0.0)
    high = dense.astype(jnp.bfloat16).astype(jnp.float32)
    out_ref[:, model_width:] = jnp.where(lane < experts, high, dense - high).astype(jnp.bfloat16)
    copies[2].wait()
    out_ref[:, :model_width] = rows_ref[...]


def pack(hidden_in, expert_routes, route_scores, experts):
    rows, model_width = hidden_in.shape
    lanes = rounds_up(2 * experts, LANES)
    return pl.pallas_call(
        pack_kernel,
        out_shape=in_vmem((rows, model_width + lanes), jnp.bfloat16),
        in_specs=[HBM] * 3,
        out_specs=VMEM,
        scratch_shapes=[
            pltpu.VMEM(hidden_in.shape, hidden_in.dtype),
            pltpu.VMEM(expert_routes.shape, expert_routes.dtype),
            pltpu.VMEM(route_scores.shape, route_scores.dtype),
            pltpu.SemaphoreType.DMA((3,)),
        ],
        compiler_params=pltpu.CompilerParams(vmem_limit_bytes=4 << 20),
        cost_estimate=pl.CostEstimate(flops=1 << 16, bytes_accessed=4 * rows * model_width, transcendentals=0),
    )(stored(hidden_in), stored(expert_routes), stored(route_scores))


def join_kernel(*refs):
    value = jnp.concatenate([ref[...].astype(jnp.float32) for ref in refs[:-1]], axis=0)
    refs[-1][...] = value.astype(jnp.bfloat16)


def join(pieces):
    total, width = sum(p.shape[0] for p in pieces), pieces[0].shape[1]
    return pl.pallas_call(
        join_kernel,
        out_shape=in_vmem((total, width), jnp.bfloat16),
        in_specs=[VMEM] * len(pieces),
        out_specs=VMEM,
        compiler_params=pltpu.CompilerParams(vmem_limit_bytes=(2 << 20) + 8 * total * width),
        cost_estimate=pl.CostEstimate(flops=total * width, bytes_accessed=4 * total * width, transcendentals=0),
    )(*(held(p) for p in pieces))


def tie_kernel(value_ref, after_ref, out_ref):
    pass


def tie(value, after):
    return pl.pallas_call(
        tie_kernel,
        out_shape=in_vmem(value.shape, value.dtype),
        in_specs=[VMEM, VMEM],
        out_specs=VMEM,
        input_output_aliases={0: 0},
        compiler_params=pltpu.CompilerParams(vmem_limit_bytes=1 << 20),
        cost_estimate=pl.CostEstimate(flops=0, bytes_accessed=0, transcendentals=0),
    )(held(value), held(after))


def expert_kernel(count, *refs):
    pieces = refs[:count]
    gate_ref, up_ref, down_ref, mine_ref, other_ref, rows_ref, hidden_ref = refs[count:]
    total, _ = rows_ref.shape
    model_width, units = gate_ref.shape
    lanes = rows_ref.shape[1] - model_width
    half = total // 2
    me = lax.axis_index("ep")
    block = min(total, 256)
    chunk = 256

    low = 0
    for piece in pieces:
        rows_ref[low : low + piece.shape[0], :] = piece[...]
        low += piece.shape[0]

    def units_of(here):
        tail = rows_ref[here, model_width:].astype(jnp.float32)
        lane = lax.broadcasted_iota(jnp.int32, (block, lanes), 1)
        taken = (lane == me) | (lane == me + lanes // 2)
        weight = jnp.sum(jnp.where(taken, tail, 0.0), axis=1, keepdims=True)
        for c in range(units // chunk):
            cols = slice(c * chunk, (c + 1) * chunk)
            x = rows_ref[here, :model_width]
            gate_value = jnp.dot(x, gate_ref[:, cols], preferred_element_type=jnp.float32)
            up_value = jnp.dot(x, up_ref[:, cols], preferred_element_type=jnp.float32)
            value = gate_value / (1.0 + jnp.exp(-gate_value)) * up_value * weight
            hidden_ref[here, cols] = value.astype(jnp.bfloat16)

    def results_of(cols):
        for i in range(total // block):
            low, high = i * block, (i + 1) * block
            value = jnp.dot(hidden_ref[low:high, :], down_ref[:, cols], preferred_element_type=jnp.float32)
            value = value.astype(jnp.bfloat16)
            if high <= half:
                mine_ref[low:high, cols] = value
            elif low >= half:
                other_ref[low - half : high - half, cols] = value
            else:
                mine_ref[low:half, cols] = value[: half - low]
                other_ref[: high - half, cols] = value[half - low :]

    step = 512
    if total == block:
        units_of(slice(0, block))
        for c in range(model_width // step):
            results_of(slice(c * step, (c + 1) * step))
    else:
        pl.loop(0, total // block)(lambda i: units_of(pl.ds(pl.multiple_of(i * block, block), block)))
        pl.loop(0, model_width // step)(lambda c: results_of(pl.ds(pl.multiple_of(c * step, step), step)))


def expert_block(pieces, expert_gate, expert_up, expert_down):
    total, width = sum(p.shape[0] for p in pieces), pieces[0].shape[1]
    model_width, units = expert_gate.shape
    out = in_vmem((total // 2, model_width), jnp.bfloat16)
    return pl.pallas_call(
        functools.partial(expert_kernel, len(pieces)),
        out_shape=(out, out),
        in_specs=[VMEM] * (len(pieces) + 3),
        out_specs=(VMEM, VMEM),
        scratch_shapes=[pltpu.VMEM((total, width), jnp.bfloat16), pltpu.VMEM((total, units), jnp.bfloat16)],
        compiler_params=pltpu.CompilerParams(vmem_limit_bytes=(8 << 20) + 4 * total * units + 2 * total * width),
        cost_estimate=pl.CostEstimate(
            flops=6 * total * model_width * units,
            bytes_accessed=4 * total * width,
            transcendentals=total * units,
        ),
    )(*(held(p) for p in pieces), *(held(w) for w in (expert_gate, expert_up, expert_down)))


def add_kernel(count, rows, sizes, *refs):
    total = None
    for ref, (low, high) in zip(refs[:count], rows, strict=True):
        value = ref[...].astype(jnp.float32)[low:high]
        total = value if total is None else total + value
    low = 0
    for out_ref, size in zip(refs[count:], sizes, strict=True):
        out_ref[...] = total[low : low + size].astype(jnp.bfloat16)
        low += size


def add(values, rows, sizes, last=False):
    width = values[0].shape[1]
    shape = jax.ShapeDtypeStruct if last else in_vmem
    elements = sum(v.size for v in values)
    return pl.pallas_call(
        functools.partial(add_kernel, len(values), rows, sizes),
        out_shape=tuple(shape((size, width), jnp.bfloat16) for size in sizes),
        in_specs=[VMEM] * len(values),
        out_specs=(VMEM,) * len(sizes),
        compiler_params=pltpu.CompilerParams(vmem_limit_bytes=(4 << 20) + 8 * values[0].size),
        cost_estimate=pl.CostEstimate(flops=elements, bytes_accessed=2 * elements, transcendentals=0),
    )(*(held(v) for v in values))


def per_device(
    hidden_in,
    expert_routes,
    route_scores,
    expert_gate,
    expert_up,
    expert_down,
    query_latent,
    latent_cache,
    cache_lengths,
):
    tok_rows, model_width = hidden_in.shape
    ep_count, sub_count = lax.axis_size("ep"), lax.axis_size("sub")
    inner = 4
    outer = ep_count // inner

    def swap(value, even, odd):
        pairs = [
            (i * sub_count + s, (i ^ (odd if s else even)) * sub_count + s)
            for i in range(ep_count)
            for s in range(sub_count)
        ]
        return lax.ppermute(value, ("ep", "sub"), pairs)

    def first(value, k):
        return swap(value, inner * k, k if inner == outer else inner * k)

    def second(value, k):
        return swap(value, k, inner * k if inner == outer else k)

    def over_cores(value):
        return lax.ppermute(value, "sub", [(i, i ^ 1) for i in range(sub_count)])

    own = pack(hidden_in, expert_routes, route_scores, ep_count)
    near = {k: first(own, k) for k in range(outer - 1, 0, -1)}
    block = join([own] + [near[k] for k in range(1, outer)])
    steps = [*range(inner - 2, 0, -1), inner - 1]
    far = {k: second(block, k) for k in steps}
    attention_latent, *weights, token = attend(
        query_latent,
        latent_cache,
        cache_lengths,
        (expert_gate[0], expert_up[0], expert_down[0]),
        block,
    )
    pieces = [block] + [tie(far[k], token) for k in range(1, inner)]
    pieces += [over_cores(p) for p in pieces]
    mine, other = expert_block(pieces, *weights)

    size = (outer - 1) * tok_rows
    kept, column, *parts = add([mine, over_cores(other)], [(0, mine.shape[0])] * 2, [tok_rows, size] * inner)
    far = [second(parts[2 * k - 1], k) for k in steps]
    side = [second(parts[2 * k - 2], k) for k in steps]
    near = add([column, *far], [(0, size)] * inner, [tok_rows] * (outer - 1))
    near = [first(near[k - 1], k) for k in range(outer - 1, 0, -1)]
    (moe_output,) = add([kept, *side, *near], [(0, tok_rows)] * (1 + len(side) + len(near)), [tok_rows], last=True)
    return (moe_output, attention_latent)


def solution(mesh):
    placed = (
        P(("groups", "ep", "sub"), None),
        P(("groups", "ep", "sub"), None),
        P(("groups", "ep", "sub"), None),
        P("ep", None, "sub"),
        P("ep", None, "sub"),
        P("ep", "sub", None),
        P(("groups", "ep", "sub"), None, None),
        P(("groups", "ep", "sub"), None, None),
        P(("groups", "ep", "sub")),
    )
    return jax.shard_map(
        per_device,
        mesh=mesh,
        in_specs=placed,
        out_specs=(P(("groups", "ep", "sub"), None), P(("groups", "ep", "sub"), None, None)),
        check_vma=False,
    )
```

```python
import functools

import jax
import jax.numpy as jnp
from jax import lax
from jax.experimental import pallas as pl
from jax.experimental.pallas import tpu as pltpu
from jax.sharding import PartitionSpec as P

LATENT = 512


SOFTMAX_SCALE = 192.0 ** (-0.5)
ROUTE_SCALE = 2.5
LANES = 128
FETCHES = 2


VMEM = pl.BlockSpec(memory_space=pltpu.VMEM)
SMEM = pl.BlockSpec(memory_space=pltpu.SMEM)
ANY = pl.BlockSpec(memory_space=pl.ANY)
HBM = pl.BlockSpec(memory_space=pltpu.HBM)


def in_vmem(shape, dtype):
    return pltpu.VMEM(shape, dtype)


def stored(value):
    return pltpu.with_memory_space_constraint(value, pltpu.HBM)


def held(value):
    return pltpu.with_memory_space_constraint(value, pltpu.VMEM)


def attend_kernel(
    lengths_hbm, query_hbm, cache_hbm, gate_hbm, up_hbm, down_hbm, after_ref,
    out_ref, gate_ref, up_ref, down_ref, token_ref, lengths_ref, query_ref, cache_ref, sems,
):
    pairs = [(lengths_hbm, lengths_ref), (query_hbm, query_ref), (cache_hbm, cache_ref)]
    for source, target in ((gate_hbm, gate_ref), (up_hbm, up_ref), (down_hbm, down_ref)):
        rows = source.shape[0] // FETCHES
        pairs += [(source.at[pl.ds(i * rows, rows)], target.at[pl.ds(i * rows, rows)]) for i in range(FETCHES)]
    copies = [pltpu.make_async_copy(s, t, sems.at[i]) for i, (s, t) in enumerate(pairs)]
    for copy in copies:
        copy.start()
    for copy in copies[:3]:
        copy.wait()
    latent = out_ref.shape[2]
    for r in range(query_ref.shape[0]):
        query, cache = query_ref[r], cache_ref[r]
        scores = SOFTMAX_SCALE * lax.dot_general(
            query, cache, (((0,), (0,)), ((), ())), preferred_element_type=jnp.float32
        )
        visible = lax.broadcasted_iota(jnp.int32, scores.shape, 1) < lengths_ref[r]
        scores = jnp.where(visible, scores, -1e30)
        largest = jnp.max(scores, axis=1, keepdims=True)
        powered = jnp.where(visible, jnp.exp(scores - largest), 0.0)
        probability = (powered / jnp.sum(powered, axis=1, keepdims=True)).astype(jnp.bfloat16)
        out_ref[r] = lax.dot_general(
            probability, cache[:latent], (((1,), (1,)), ((), ())), preferred_element_type=jnp.float32
        ).astype(jnp.bfloat16)
    token_ref[...] = jnp.zeros_like(token_ref)
    for copy in copies[3:]:
        copy.wait()


def attend(query_latent, latent_cache, cache_lengths, weights, after):
    rows, heads, entries = query_latent.shape
    positions = latent_cache.shape[1]
    query, cache = jnp.swapaxes(query_latent, 1, 2), jnp.swapaxes(latent_cache, 1, 2)
    operands = (cache_lengths, query, cache, *weights)
    return pl.pallas_call(
        attend_kernel,
        out_shape=(
            jax.ShapeDtypeStruct((rows, heads, LATENT), jnp.bfloat16),
            *(in_vmem(w.shape, w.dtype) for w in weights),
            in_vmem((8, LANES), jnp.float32),
        ),
        in_specs=[HBM] * 6 + [ANY],
        out_specs=(VMEM,) * 5,
        scratch_shapes=[
            pltpu.SMEM(cache_lengths.shape, jnp.int32),
            pltpu.VMEM(query.shape, query.dtype),
            pltpu.VMEM(cache.shape, cache.dtype),
            pltpu.SemaphoreType.DMA((3 + 3 * FETCHES,)),
        ],
        compiler_params=pltpu.CompilerParams(vmem_limit_bytes=12 << 20),
        cost_estimate=pl.CostEstimate(
            flops=4 * rows * heads * positions * entries,
            bytes_accessed=2 * sum(w.size for w in weights),
            transcendentals=rows * heads * positions,
        ),
    )(*(stored(v) for v in operands), after)


def rounds_up(value, step):
    return -(-value // step) * step


def pack_kernel(hidden_ref, routes_ref, scores_ref, out_ref, rows_ref, named_ref, affinity_ref, sems):
    rows, model_width = hidden_ref.shape
    copies = [
        pltpu.make_async_copy(source, target, sems.at[i])
        for i, (source, target) in enumerate(
            ((routes_ref, named_ref), (scores_ref, affinity_ref), (hidden_ref, rows_ref))
        )
    ]
    for copy in copies:
        copy.start()
    copies[0].wait()
    copies[1].wait()
    scores = affinity_ref[...]
    routes = named_ref[...]
    weights = ROUTE_SCALE * scores / jnp.sum(scores, axis=1, keepdims=True)
    lanes = out_ref.shape[1] - model_width
    lane = lax.broadcasted_iota(jnp.int32, (rows, lanes), 1)
    experts = lanes // 2
    dense = jnp.zeros((rows, lanes), jnp.float32)
    for k in range(routes.shape[1]):
        named = routes[:, k : k + 1]
        dense += jnp.where((lane == named) | (lane == named + experts), weights[:, k : k + 1], 0.0)
    high = dense.astype(jnp.bfloat16).astype(jnp.float32)
    out_ref[:, model_width:] = jnp.where(lane < experts, high, dense - high).astype(jnp.bfloat16)
    copies[2].wait()
    out_ref[:, :model_width] = rows_ref[...]


def pack(hidden_in, expert_routes, route_scores, experts):
    rows, model_width = hidden_in.shape
    lanes = rounds_up(2 * experts, LANES)
    return pl.pallas_call(
        pack_kernel,
        out_shape=in_vmem((rows, model_width + lanes), jnp.bfloat16),
        in_specs=[HBM] * 3,
        out_specs=VMEM,
        scratch_shapes=[
            pltpu.VMEM(hidden_in.shape, hidden_in.dtype),
            pltpu.VMEM(expert_routes.shape, expert_routes.dtype),
            pltpu.VMEM(route_scores.shape, route_scores.dtype),
            pltpu.SemaphoreType.DMA((3,)),
        ],
        compiler_params=pltpu.CompilerParams(vmem_limit_bytes=4 << 20),
        cost_estimate=pl.CostEstimate(flops=1 << 16, bytes_accessed=4 * rows * model_width, transcendentals=0),
    )(stored(hidden_in), stored(expert_routes), stored(route_scores))


def join_kernel(count, *refs):
    value = jnp.concatenate([ref[...].astype(jnp.float32) for ref in refs[:count]], axis=0)
    refs[-1][...] = value.astype(jnp.bfloat16)


def join(pieces, after=()):
    total, width = sum(p.shape[0] for p in pieces), pieces[0].shape[1]
    operands = [*pieces, *after]
    return pl.pallas_call(
        functools.partial(join_kernel, len(pieces)),
        out_shape=in_vmem((total, width), jnp.bfloat16),
        in_specs=[VMEM] * len(operands),
        out_specs=VMEM,
        compiler_params=pltpu.CompilerParams(vmem_limit_bytes=(2 << 20) + 8 * total * width),
        cost_estimate=pl.CostEstimate(flops=total * width, bytes_accessed=4 * total * width, transcendentals=0),
    )(*(held(p) for p in operands))


def tie_kernel(value_ref, after_ref, out_ref):
    pass


def tie(value, after):
    return pl.pallas_call(
        tie_kernel,
        out_shape=in_vmem(value.shape, value.dtype),
        in_specs=[VMEM, VMEM],
        out_specs=VMEM,
        input_output_aliases={0: 0},
        compiler_params=pltpu.CompilerParams(vmem_limit_bytes=1 << 20),
        cost_estimate=pl.CostEstimate(flops=0, bytes_accessed=0, transcendentals=0),
    )(held(value), held(after))


def expert_kernel(count, *refs):
    pieces = refs[:count]
    gate_ref, up_ref, down_ref, mine_ref, other_ref, rows_ref, hidden_ref = refs[count:]
    total, _ = rows_ref.shape
    model_width, units = gate_ref.shape
    lanes = rows_ref.shape[1] - model_width
    half = total // 2
    me = lax.axis_index("ep")
    block = min(total, 256)
    chunk = 256

    low = 0
    for piece in pieces:
        rows_ref[low : low + piece.shape[0], :] = piece[...]
        low += piece.shape[0]

    def units_of(here):
        tail = rows_ref[here, model_width:].astype(jnp.float32)
        lane = lax.broadcasted_iota(jnp.int32, (block, lanes), 1)
        taken = (lane == me) | (lane == me + lanes // 2)
        weight = jnp.sum(jnp.where(taken, tail, 0.0), axis=1, keepdims=True)
        for c in range(units // chunk):
            cols = slice(c * chunk, (c + 1) * chunk)
            x = rows_ref[here, :model_width]
            gate_value = jnp.dot(x, gate_ref[:, cols], preferred_element_type=jnp.float32)
            up_value = jnp.dot(x, up_ref[:, cols], preferred_element_type=jnp.float32)
            value = gate_value / (1.0 + jnp.exp(-gate_value)) * up_value * weight
            hidden_ref[here, cols] = value.astype(jnp.bfloat16)

    def results_of(cols):
        for i in range(total // block):
            low, high = i * block, (i + 1) * block
            value = jnp.dot(hidden_ref[low:high, :], down_ref[:, cols], preferred_element_type=jnp.float32)
            value = value.astype(jnp.bfloat16)
            if high <= half:
                mine_ref[low:high, cols] = value
            elif low >= half:
                other_ref[low - half : high - half, cols] = value
            else:
                mine_ref[low:half, cols] = value[: half - low]
                other_ref[: high - half, cols] = value[half - low :]

    step = 512
    if total == block:
        units_of(slice(0, block))
        for c in range(model_width // step):
            results_of(slice(c * step, (c + 1) * step))
    else:
        pl.loop(0, total // block)(lambda i: units_of(pl.ds(pl.multiple_of(i * block, block), block)))
        pl.loop(0, model_width // step)(lambda c: results_of(pl.ds(pl.multiple_of(c * step, step), step)))


def expert_block(pieces, expert_gate, expert_up, expert_down):
    total, width = sum(p.shape[0] for p in pieces), pieces[0].shape[1]
    model_width, units = expert_gate.shape
    out = in_vmem((total // 2, model_width), jnp.bfloat16)
    return pl.pallas_call(
        functools.partial(expert_kernel, len(pieces)),
        out_shape=(out, out),
        in_specs=[VMEM] * (len(pieces) + 3),
        out_specs=(VMEM, VMEM),
        scratch_shapes=[pltpu.VMEM((total, width), jnp.bfloat16), pltpu.VMEM((total, units), jnp.bfloat16)],
        compiler_params=pltpu.CompilerParams(vmem_limit_bytes=(8 << 20) + 4 * total * units + 2 * total * width),
        cost_estimate=pl.CostEstimate(
            flops=6 * total * model_width * units,
            bytes_accessed=4 * total * width,
            transcendentals=total * units,
        ),
    )(*(held(p) for p in pieces), *(held(w) for w in (expert_gate, expert_up, expert_down)))


def add_kernel(count, rows, sizes, *refs):
    total = None
    for ref, (low, high) in zip(refs[:count], rows, strict=True):
        value = ref[...].astype(jnp.float32)[low:high]
        total = value if total is None else total + value
    low = 0
    for out_ref, size in zip(refs[count:], sizes, strict=True):
        out_ref[...] = total[low : low + size].astype(jnp.bfloat16)
        low += size


def add(values, rows, sizes, last=False):
    width = values[0].shape[1]
    shape = jax.ShapeDtypeStruct if last else in_vmem
    elements = sum(v.size for v in values)
    return pl.pallas_call(
        functools.partial(add_kernel, len(values), rows, sizes),
        out_shape=tuple(shape((size, width), jnp.bfloat16) for size in sizes),
        in_specs=[VMEM] * len(values),
        out_specs=(VMEM,) * len(sizes),
        compiler_params=pltpu.CompilerParams(vmem_limit_bytes=(4 << 20) + 8 * values[0].size),
        cost_estimate=pl.CostEstimate(flops=elements, bytes_accessed=2 * elements, transcendentals=0),
    )(*(held(v) for v in values))


def per_device(
    hidden_in,
    expert_routes,
    route_scores,
    expert_gate,
    expert_up,
    expert_down,
    query_latent,
    latent_cache,
    cache_lengths,
):
    tok_rows, model_width = hidden_in.shape
    ep_count, sub_count = lax.axis_size("ep"), lax.axis_size("sub")
    inner = 4
    outer = ep_count // inner

    def swap(value, even, odd):
        pairs = [
            (i * sub_count + s, (i ^ (odd if s else even)) * sub_count + s)
            for i in range(ep_count)
            for s in range(sub_count)
        ]
        return lax.ppermute(value, ("ep", "sub"), pairs)

    def first(value, k):
        return swap(value, inner * k, k if inner == outer else inner * k)

    def second(value, k):
        return swap(value, k, inner * k if inner == outer else k)

    def over_cores(value):
        return lax.ppermute(value, "sub", [(i, i ^ 1) for i in range(sub_count)])

    own = pack(hidden_in, expert_routes, route_scores, ep_count)
    near = {k: first(own, k) for k in range(outer - 1, 0, -1)}
    last = inner - 1
    ahead = second(own, last)
    received = [near[k] for k in range(1, outer)]
    block, column = join([own, *received]), join(received, [ahead])
    steps = [*range(last - 1, 0, -1), last]
    far = {k: second(column if k == last else block, k) for k in steps}
    attention_latent, *weights, token = attend(
        query_latent,
        latent_cache,
        cache_lengths,
        (expert_gate[0], expert_up[0], expert_down[0]),
        block,
    )
    pieces = [block] + [tie(far[k], token) for k in range(1, last)]
    pieces += [join([ahead, far[last]], pieces)]
    pieces += [over_cores(p) for p in pieces]
    mine, other = expert_block(pieces, *weights)

    size = (outer - 1) * tok_rows
    kept, column, *parts = add([mine, over_cores(other)], [(0, mine.shape[0])] * 2, [tok_rows, size] * inner)
    far = [second(parts[2 * k - 1], k) for k in steps]
    side = [second(parts[2 * k - 2], k) for k in steps]
    near = add([column, *far], [(0, size)] * inner, [tok_rows] * (outer - 1))
    near = [first(near[k - 1], k) for k in range(outer - 1, 0, -1)]
    (moe_output,) = add([kept, *side, *near], [(0, tok_rows)] * (1 + len(side) + len(near)), [tok_rows], last=True)
    return (moe_output, attention_latent)


def solution(mesh):
    placed = (
        P(("groups", "ep", "sub"), None),
        P(("groups", "ep", "sub"), None),
        P(("groups", "ep", "sub"), None),
        P("ep", None, "sub"),
        P("ep", None, "sub"),
        P("ep", "sub", None),
        P(("groups", "ep", "sub"), None, None),
        P(("groups", "ep", "sub"), None, None),
        P(("groups", "ep", "sub")),
    )
    return jax.shard_map(
        per_device,
        mesh=mesh,
        in_specs=placed,
        out_specs=(P(("groups", "ep", "sub"), None), P(("groups", "ep", "sub"), None, None)),
        check_vma=False,
    )
```

```python
import functools

import jax
import jax.numpy as jnp
from jax import lax
from jax.experimental import pallas as pl
from jax.experimental.pallas import tpu as pltpu
from jax.sharding import PartitionSpec as P

LATENT = 512


SOFTMAX_SCALE = 192.0 ** (-0.5)
ROUTE_SCALE = 2.5
LANES = 128
FETCHES = 2


VMEM = pl.BlockSpec(memory_space=pltpu.VMEM)
SMEM = pl.BlockSpec(memory_space=pltpu.SMEM)
ANY = pl.BlockSpec(memory_space=pl.ANY)
HBM = pl.BlockSpec(memory_space=pltpu.HBM)


def in_vmem(shape, dtype):
    return pltpu.VMEM(shape, dtype)


def stored(value):
    return pltpu.with_memory_space_constraint(value, pltpu.HBM)


def held(value):
    return pltpu.with_memory_space_constraint(value, pltpu.VMEM)


def attend_kernel(
    lengths_hbm, query_hbm, cache_hbm, gate_hbm, up_hbm, down_hbm, after_ref,
    out_ref, gate_ref, up_ref, down_ref, token_ref, lengths_ref, query_ref, cache_ref, sems,
):
    pairs = [(lengths_hbm, lengths_ref), (query_hbm, query_ref), (cache_hbm, cache_ref)]
    for source, target in ((gate_hbm, gate_ref), (up_hbm, up_ref), (down_hbm, down_ref)):
        rows = source.shape[0] // FETCHES
        pairs += [(source.at[pl.ds(i * rows, rows)], target.at[pl.ds(i * rows, rows)]) for i in range(FETCHES)]
    copies = [pltpu.make_async_copy(s, t, sems.at[i]) for i, (s, t) in enumerate(pairs)]
    for copy in copies:
        copy.start()
    for copy in copies[:3]:
        copy.wait()
    latent = out_ref.shape[2]
    for r in range(query_ref.shape[0]):
        query, cache = query_ref[r], cache_ref[r]
        scores = SOFTMAX_SCALE * lax.dot_general(
            query, cache, (((0,), (0,)), ((), ())), preferred_element_type=jnp.float32
        )
        visible = lax.broadcasted_iota(jnp.int32, scores.shape, 1) < lengths_ref[r]
        scores = jnp.where(visible, scores, -1e30)
        largest = jnp.max(scores, axis=1, keepdims=True)
        powered = jnp.where(visible, jnp.exp(scores - largest), 0.0)
        probability = (powered / jnp.sum(powered, axis=1, keepdims=True)).astype(jnp.bfloat16)
        out_ref[r] = lax.dot_general(
            probability, cache[:latent], (((1,), (1,)), ((), ())), preferred_element_type=jnp.float32
        ).astype(jnp.bfloat16)
    token_ref[...] = jnp.zeros_like(token_ref)
    for copy in copies[3:]:
        copy.wait()


def attend(query_latent, latent_cache, cache_lengths, weights, after):
    rows, heads, entries = query_latent.shape
    positions = latent_cache.shape[1]
    query, cache = jnp.swapaxes(query_latent, 1, 2), jnp.swapaxes(latent_cache, 1, 2)
    operands = (cache_lengths, query, cache, *weights)
    return pl.pallas_call(
        attend_kernel,
        out_shape=(
            jax.ShapeDtypeStruct((rows, heads, LATENT), jnp.bfloat16),
            *(in_vmem(w.shape, w.dtype) for w in weights),
            in_vmem((8, LANES), jnp.float32),
        ),
        in_specs=[HBM] * 6 + [ANY],
        out_specs=(VMEM,) * 5,
        scratch_shapes=[
            pltpu.SMEM(cache_lengths.shape, jnp.int32),
            pltpu.VMEM(query.shape, query.dtype),
            pltpu.VMEM(cache.shape, cache.dtype),
            pltpu.SemaphoreType.DMA((3 + 3 * FETCHES,)),
        ],
        compiler_params=pltpu.CompilerParams(vmem_limit_bytes=12 << 20),
        cost_estimate=pl.CostEstimate(
            flops=4 * rows * heads * positions * entries,
            bytes_accessed=2 * sum(w.size for w in weights),
            transcendentals=rows * heads * positions,
        ),
    )(*(stored(v) for v in operands), after)


def rounds_up(value, step):
    return -(-value // step) * step


def pack_kernel(hidden_ref, routes_ref, scores_ref, out_ref, rows_ref, named_ref, affinity_ref, sems):
    rows, model_width = hidden_ref.shape
    copies = [
        pltpu.make_async_copy(source, target, sems.at[i])
        for i, (source, target) in enumerate(
            ((routes_ref, named_ref), (scores_ref, affinity_ref), (hidden_ref, rows_ref))
        )
    ]
    for copy in copies:
        copy.start()
    copies[0].wait()
    copies[1].wait()
    scores = affinity_ref[...]
    routes = named_ref[...]
    weights = ROUTE_SCALE * scores / jnp.sum(scores, axis=1, keepdims=True)
    lanes = out_ref.shape[1] - model_width
    lane = lax.broadcasted_iota(jnp.int32, (rows, lanes), 1)
    experts = lanes // 2
    dense = jnp.zeros((rows, lanes), jnp.float32)
    for k in range(routes.shape[1]):
        named = routes[:, k : k + 1]
        dense += jnp.where((lane == named) | (lane == named + experts), weights[:, k : k + 1], 0.0)
    high = dense.astype(jnp.bfloat16).astype(jnp.float32)
    out_ref[:, model_width:] = jnp.where(lane < experts, high, dense - high).astype(jnp.bfloat16)
    copies[2].wait()
    out_ref[:, :model_width] = rows_ref[...]


def pack(hidden_in, expert_routes, route_scores, experts):
    rows, model_width = hidden_in.shape
    lanes = rounds_up(2 * experts, LANES)
    return pl.pallas_call(
        pack_kernel,
        out_shape=in_vmem((rows, model_width + lanes), jnp.bfloat16),
        in_specs=[HBM] * 3,
        out_specs=VMEM,
        scratch_shapes=[
            pltpu.VMEM(hidden_in.shape, hidden_in.dtype),
            pltpu.VMEM(expert_routes.shape, expert_routes.dtype),
            pltpu.VMEM(route_scores.shape, route_scores.dtype),
            pltpu.SemaphoreType.DMA((3,)),
        ],
        compiler_params=pltpu.CompilerParams(vmem_limit_bytes=4 << 20),
        cost_estimate=pl.CostEstimate(flops=1 << 16, bytes_accessed=4 * rows * model_width, transcendentals=0),
    )(stored(hidden_in), stored(expert_routes), stored(route_scores))


def join_kernel(count, *refs):
    value = jnp.concatenate([ref[...].astype(jnp.float32) for ref in refs[:count]], axis=0)
    refs[-1][...] = value.astype(jnp.bfloat16)


def join(pieces, after=()):
    total, width = sum(p.shape[0] for p in pieces), pieces[0].shape[1]
    operands = [*pieces, *after]
    return pl.pallas_call(
        functools.partial(join_kernel, len(pieces)),
        out_shape=in_vmem((total, width), jnp.bfloat16),
        in_specs=[VMEM] * len(operands),
        out_specs=VMEM,
        compiler_params=pltpu.CompilerParams(vmem_limit_bytes=(2 << 20) + 8 * total * width),
        cost_estimate=pl.CostEstimate(flops=total * width, bytes_accessed=4 * total * width, transcendentals=0),
    )(*(held(p) for p in operands))


def tie_kernel(value_ref, after_ref, out_ref):
    pass


def tie(value, after):
    return pl.pallas_call(
        tie_kernel,
        out_shape=in_vmem(value.shape, value.dtype),
        in_specs=[VMEM, VMEM],
        out_specs=VMEM,
        input_output_aliases={0: 0},
        compiler_params=pltpu.CompilerParams(vmem_limit_bytes=1 << 20),
        cost_estimate=pl.CostEstimate(flops=0, bytes_accessed=0, transcendentals=0),
    )(held(value), held(after))


def expert_kernel(count, *refs):
    pieces = refs[:count]
    gate_ref, up_ref, down_ref, mine_ref, other_ref, rows_ref, hidden_ref = refs[count:]
    total, _ = rows_ref.shape
    model_width, units = gate_ref.shape
    lanes = rows_ref.shape[1] - model_width
    half = total // 2
    me = lax.axis_index("ep")
    block = min(total, 256)
    chunk = 256

    low = 0
    for piece in pieces:
        rows_ref[low : low + piece.shape[0], :] = piece[...]
        low += piece.shape[0]

    def units_of(here):
        tail = rows_ref[here, model_width:].astype(jnp.float32)
        lane = lax.broadcasted_iota(jnp.int32, (block, lanes), 1)
        taken = (lane == me) | (lane == me + lanes // 2)
        weight = jnp.sum(jnp.where(taken, tail, 0.0), axis=1, keepdims=True)
        for c in range(units // chunk):
            cols = slice(c * chunk, (c + 1) * chunk)
            x = rows_ref[here, :model_width]
            gate_value = jnp.dot(x, gate_ref[:, cols], preferred_element_type=jnp.float32)
            up_value = jnp.dot(x, up_ref[:, cols], preferred_element_type=jnp.float32)
            value = gate_value / (1.0 + jnp.exp(-gate_value)) * up_value * weight
            hidden_ref[here, cols] = value.astype(jnp.bfloat16)

    def results_of(cols):
        for i in range(total // block):
            low, high = i * block, (i + 1) * block
            value = jnp.dot(hidden_ref[low:high, :], down_ref[:, cols], preferred_element_type=jnp.float32)
            value = value.astype(jnp.bfloat16)
            if high <= half:
                mine_ref[low:high, cols] = value
            elif low >= half:
                other_ref[low - half : high - half, cols] = value
            else:
                mine_ref[low:half, cols] = value[: half - low]
                other_ref[: high - half, cols] = value[half - low :]

    step = 512
    if total == block:
        units_of(slice(0, block))
        for c in range(model_width // step):
            results_of(slice(c * step, (c + 1) * step))
    else:
        pl.loop(0, total // block)(lambda i: units_of(pl.ds(pl.multiple_of(i * block, block), block)))
        pl.loop(0, model_width // step)(lambda c: results_of(pl.ds(pl.multiple_of(c * step, step), step)))


def expert_block(pieces, expert_gate, expert_up, expert_down):
    total, width = sum(p.shape[0] for p in pieces), pieces[0].shape[1]
    model_width, units = expert_gate.shape
    out = in_vmem((total // 2, model_width), jnp.bfloat16)
    return pl.pallas_call(
        functools.partial(expert_kernel, len(pieces)),
        out_shape=(out, out),
        in_specs=[VMEM] * (len(pieces) + 3),
        out_specs=(VMEM, VMEM),
        scratch_shapes=[pltpu.VMEM((total, width), jnp.bfloat16), pltpu.VMEM((total, units), jnp.bfloat16)],
        compiler_params=pltpu.CompilerParams(vmem_limit_bytes=(8 << 20) + 4 * total * units + 2 * total * width),
        cost_estimate=pl.CostEstimate(
            flops=6 * total * model_width * units,
            bytes_accessed=4 * total * width,
            transcendentals=total * units,
        ),
    )(*(held(p) for p in pieces), *(held(w) for w in (expert_gate, expert_up, expert_down)))


def add_kernel(count, rows, sizes, *refs):
    total = None
    for ref, (low, high) in zip(refs[:count], rows, strict=True):
        value = ref[...].astype(jnp.float32)[low:high]
        total = value if total is None else total + value
    low = 0
    for out_ref, size in zip(refs[count:], sizes, strict=True):
        out_ref[...] = total[low : low + size].astype(jnp.bfloat16)
        low += size


def add(values, rows, sizes, last=False):
    width = values[0].shape[1]
    shape = jax.ShapeDtypeStruct if last else in_vmem
    elements = sum(v.size for v in values)
    return pl.pallas_call(
        functools.partial(add_kernel, len(values), rows, sizes),
        out_shape=tuple(shape((size, width), jnp.bfloat16) for size in sizes),
        in_specs=[VMEM] * len(values),
        out_specs=(VMEM,) * len(sizes),
        compiler_params=pltpu.CompilerParams(vmem_limit_bytes=(4 << 20) + 8 * values[0].size),
        cost_estimate=pl.CostEstimate(flops=elements, bytes_accessed=2 * elements, transcendentals=0),
    )(*(held(v) for v in values))


def per_device(
    hidden_in,
    expert_routes,
    route_scores,
    expert_gate,
    expert_up,
    expert_down,
    query_latent,
    latent_cache,
    cache_lengths,
):
    tok_rows, model_width = hidden_in.shape
    ep_count, sub_count = lax.axis_size("ep"), lax.axis_size("sub")
    inner = 4
    outer = ep_count // inner

    def swap(value, even, odd):
        pairs = [
            (i * sub_count + s, (i ^ (odd if s else even)) * sub_count + s)
            for i in range(ep_count)
            for s in range(sub_count)
        ]
        return lax.ppermute(value, ("ep", "sub"), pairs)

    def first(value, k):
        return swap(value, inner * k, k if inner == outer else inner * k)

    def second(value, k):
        return swap(value, k, inner * k if inner == outer else k)

    def over_cores(value):
        return lax.ppermute(value, "sub", [(i, i ^ 1) for i in range(sub_count)])

    own = pack(hidden_in, expert_routes, route_scores, ep_count)
    near = {k: first(own, k) for k in range(outer - 1, 0, -1)}
    last = inner - 1
    ahead = second(own, last)
    received = [near[k] for k in range(1, outer)]
    block, column = join([own, *received]), join(received, [ahead])
    steps = [*range(last - 1, 0, -1), last]
    far = {k: second(column if k == last else block, k) for k in steps}
    attention_latent, *weights, token = attend(
        query_latent,
        latent_cache,
        cache_lengths,
        (expert_gate[0], expert_up[0], expert_down[0]),
        block,
    )
    pieces = [block] + [tie(far[k], token) for k in range(1, last)] + [join([ahead, far[last]], [token])]
    pieces += [over_cores(p) for p in pieces]
    mine, other = expert_block(pieces, *weights)

    size = (outer - 1) * tok_rows
    kept, column, *parts = add([mine, over_cores(other)], [(0, mine.shape[0])] * 2, [tok_rows, size] * inner)
    far = [second(parts[2 * k - 1], k) for k in steps]
    side = [second(parts[2 * k - 2], k) for k in steps]
    near = add([column, *far], [(0, size)] * inner, [tok_rows] * (outer - 1))
    near = [first(near[k - 1], k) for k in range(outer - 1, 0, -1)]
    (moe_output,) = add([kept, *side, *near], [(0, tok_rows)] * (1 + len(side) + len(near)), [tok_rows], last=True)
    return (moe_output, attention_latent)


def solution(mesh):
    placed = (
        P(("groups", "ep", "sub"), None),
        P(("groups", "ep", "sub"), None),
        P(("groups", "ep", "sub"), None),
        P("ep", None, "sub"),
        P("ep", None, "sub"),
        P("ep", "sub", None),
        P(("groups", "ep", "sub"), None, None),
        P(("groups", "ep", "sub"), None, None),
        P(("groups", "ep", "sub")),
    )
    return jax.shard_map(
        per_device,
        mesh=mesh,
        in_specs=placed,
        out_specs=(P(("groups", "ep", "sub"), None), P(("groups", "ep", "sub"), None, None)),
        check_vma=False,
    )
```

```python
import functools

import jax
import jax.numpy as jnp
from jax import lax
from jax.experimental import pallas as pl
from jax.experimental.pallas import tpu as pltpu
from jax.sharding import PartitionSpec as P

LATENT = 512


SOFTMAX_SCALE = 192.0 ** (-0.5)
ROUTE_SCALE = 2.5
LANES = 128
FETCHES = 2


VMEM = pl.BlockSpec(memory_space=pltpu.VMEM)
SMEM = pl.BlockSpec(memory_space=pltpu.SMEM)
ANY = pl.BlockSpec(memory_space=pl.ANY)
HBM = pl.BlockSpec(memory_space=pltpu.HBM)


def in_vmem(shape, dtype):
    return pltpu.VMEM(shape, dtype)


def stored(value):
    return pltpu.with_memory_space_constraint(value, pltpu.HBM)


def held(value):
    return pltpu.with_memory_space_constraint(value, pltpu.VMEM)


def attend_kernel(
    lengths_hbm, query_hbm, cache_hbm, gate_hbm, up_hbm, after_ref,
    out_ref, gate_ref, up_ref, token_ref, lengths_ref, query_ref, cache_ref, sems,
):
    pairs = [(lengths_hbm, lengths_ref), (query_hbm, query_ref), (cache_hbm, cache_ref)]
    for source, target in ((gate_hbm, gate_ref), (up_hbm, up_ref)):
        rows = source.shape[0] // FETCHES
        pairs += [(source.at[pl.ds(i * rows, rows)], target.at[pl.ds(i * rows, rows)]) for i in range(FETCHES)]
    copies = [pltpu.make_async_copy(s, t, sems.at[i]) for i, (s, t) in enumerate(pairs)]
    for copy in copies:
        copy.start()
    for copy in copies[:3]:
        copy.wait()
    latent = out_ref.shape[2]
    for r in range(query_ref.shape[0]):
        query, cache = query_ref[r], cache_ref[r]
        scores = SOFTMAX_SCALE * lax.dot_general(
            query, cache, (((0,), (0,)), ((), ())), preferred_element_type=jnp.float32
        )
        visible = lax.broadcasted_iota(jnp.int32, scores.shape, 1) < lengths_ref[r]
        scores = jnp.where(visible, scores, -1e30)
        largest = jnp.max(scores, axis=1, keepdims=True)
        powered = jnp.where(visible, jnp.exp(scores - largest), 0.0)
        probability = (powered / jnp.sum(powered, axis=1, keepdims=True)).astype(jnp.bfloat16)
        out_ref[r] = lax.dot_general(
            probability, cache[:latent], (((1,), (1,)), ((), ())), preferred_element_type=jnp.float32
        ).astype(jnp.bfloat16)
    token_ref[...] = jnp.zeros_like(token_ref)
    for copy in copies[3:]:
        copy.wait()


def attend(query_latent, latent_cache, cache_lengths, weights, after):
    rows, heads, entries = query_latent.shape
    positions = latent_cache.shape[1]
    query, cache = jnp.swapaxes(query_latent, 1, 2), jnp.swapaxes(latent_cache, 1, 2)
    operands = (cache_lengths, query, cache, *weights)
    return pl.pallas_call(
        attend_kernel,
        out_shape=(
            jax.ShapeDtypeStruct((rows, heads, LATENT), jnp.bfloat16),
            *(in_vmem(w.shape, w.dtype) for w in weights),
            in_vmem((8, LANES), jnp.float32),
        ),
        in_specs=[HBM] * 5 + [ANY],
        out_specs=(VMEM,) * 4,
        scratch_shapes=[
            pltpu.SMEM(cache_lengths.shape, jnp.int32),
            pltpu.VMEM(query.shape, query.dtype),
            pltpu.VMEM(cache.shape, cache.dtype),
            pltpu.SemaphoreType.DMA((3 + 2 * FETCHES,)),
        ],
        compiler_params=pltpu.CompilerParams(vmem_limit_bytes=12 << 20),
        cost_estimate=pl.CostEstimate(
            flops=4 * rows * heads * positions * entries,
            bytes_accessed=2 * sum(w.size for w in weights),
            transcendentals=rows * heads * positions,
        ),
    )(*(stored(v) for v in operands), after)


def rounds_up(value, step):
    return -(-value // step) * step


def pack_kernel(hidden_ref, routes_ref, scores_ref, out_ref, rows_ref, named_ref, affinity_ref, sems):
    rows, model_width = hidden_ref.shape
    copies = [
        pltpu.make_async_copy(source, target, sems.at[i])
        for i, (source, target) in enumerate(
            ((routes_ref, named_ref), (scores_ref, affinity_ref), (hidden_ref, rows_ref))
        )
    ]
    for copy in copies:
        copy.start()
    copies[0].wait()
    copies[1].wait()
    scores = affinity_ref[...]
    routes = named_ref[...]
    weights = ROUTE_SCALE * scores / jnp.sum(scores, axis=1, keepdims=True)
    lanes = out_ref.shape[1] - model_width
    lane = lax.broadcasted_iota(jnp.int32, (rows, lanes), 1)
    experts = lanes // 2
    dense = jnp.zeros((rows, lanes), jnp.float32)
    for k in range(routes.shape[1]):
        named = routes[:, k : k + 1]
        dense += jnp.where((lane == named) | (lane == named + experts), weights[:, k : k + 1], 0.0)
    high = dense.astype(jnp.bfloat16).astype(jnp.float32)
    out_ref[:, model_width:] = jnp.where(lane < experts, high, dense - high).astype(jnp.bfloat16)
    copies[2].wait()
    out_ref[:, :model_width] = rows_ref[...]


def pack(hidden_in, expert_routes, route_scores, experts):
    rows, model_width = hidden_in.shape
    lanes = rounds_up(2 * experts, LANES)
    return pl.pallas_call(
        pack_kernel,
        out_shape=in_vmem((rows, model_width + lanes), jnp.bfloat16),
        in_specs=[HBM] * 3,
        out_specs=VMEM,
        scratch_shapes=[
            pltpu.VMEM(hidden_in.shape, hidden_in.dtype),
            pltpu.VMEM(expert_routes.shape, expert_routes.dtype),
            pltpu.VMEM(route_scores.shape, route_scores.dtype),
            pltpu.SemaphoreType.DMA((3,)),
        ],
        compiler_params=pltpu.CompilerParams(vmem_limit_bytes=4 << 20),
        cost_estimate=pl.CostEstimate(flops=1 << 16, bytes_accessed=4 * rows * model_width, transcendentals=0),
    )(stored(hidden_in), stored(expert_routes), stored(route_scores))


def join_kernel(count, *refs):
    value = jnp.concatenate([ref[...].astype(jnp.float32) for ref in refs[:count]], axis=0)
    refs[-1][...] = value.astype(jnp.bfloat16)


def join(pieces, after=()):
    total, width = sum(p.shape[0] for p in pieces), pieces[0].shape[1]
    operands = [*pieces, *after]
    return pl.pallas_call(
        functools.partial(join_kernel, len(pieces)),
        out_shape=in_vmem((total, width), jnp.bfloat16),
        in_specs=[VMEM] * len(operands),
        out_specs=VMEM,
        compiler_params=pltpu.CompilerParams(vmem_limit_bytes=(2 << 20) + 8 * total * width),
        cost_estimate=pl.CostEstimate(flops=total * width, bytes_accessed=4 * total * width, transcendentals=0),
    )(*(held(p) for p in operands))


def tie_kernel(value_ref, after_ref, out_ref):
    pass


def tie(value, after):
    return pl.pallas_call(
        tie_kernel,
        out_shape=in_vmem(value.shape, value.dtype),
        in_specs=[VMEM, VMEM],
        out_specs=VMEM,
        input_output_aliases={0: 0},
        compiler_params=pltpu.CompilerParams(vmem_limit_bytes=1 << 20),
        cost_estimate=pl.CostEstimate(flops=0, bytes_accessed=0, transcendentals=0),
    )(held(value), held(after))


def expert_kernel(count, *refs):
    pieces = refs[:count]
    gate_ref, up_ref, down_hbm, mine_ref, other_ref, rows_ref, hidden_ref, down_ref, sem = refs[count:]
    fetch = pltpu.make_async_copy(down_hbm, down_ref, sem)
    fetch.start()
    total, _ = rows_ref.shape
    model_width, units = gate_ref.shape
    lanes = rows_ref.shape[1] - model_width
    half = total // 2
    me = lax.axis_index("ep")
    block = min(total, 256)
    chunk = 256

    low = 0
    for piece in pieces:
        rows_ref[low : low + piece.shape[0], :] = piece[...]
        low += piece.shape[0]

    def units_of(here):
        tail = rows_ref[here, model_width:].astype(jnp.float32)
        lane = lax.broadcasted_iota(jnp.int32, (block, lanes), 1)
        taken = (lane == me) | (lane == me + lanes // 2)
        weight = jnp.sum(jnp.where(taken, tail, 0.0), axis=1, keepdims=True)
        for c in range(units // chunk):
            cols = slice(c * chunk, (c + 1) * chunk)
            x = rows_ref[here, :model_width]
            gate_value = jnp.dot(x, gate_ref[:, cols], preferred_element_type=jnp.float32)
            up_value = jnp.dot(x, up_ref[:, cols], preferred_element_type=jnp.float32)
            value = gate_value / (1.0 + jnp.exp(-gate_value)) * up_value * weight
            hidden_ref[here, cols] = value.astype(jnp.bfloat16)

    def results_of(cols):
        for i in range(total // block):
            low, high = i * block, (i + 1) * block
            value = jnp.dot(hidden_ref[low:high, :], down_ref[:, cols], preferred_element_type=jnp.float32)
            value = value.astype(jnp.bfloat16)
            if high <= half:
                mine_ref[low:high, cols] = value
            elif low >= half:
                other_ref[low - half : high - half, cols] = value
            else:
                mine_ref[low:half, cols] = value[: half - low]
                other_ref[: high - half, cols] = value[half - low :]

    step = 512
    if total == block:
        units_of(slice(0, block))
        fetch.wait()
        for c in range(model_width // step):
            results_of(slice(c * step, (c + 1) * step))
    else:
        pl.loop(0, total // block)(lambda i: units_of(pl.ds(pl.multiple_of(i * block, block), block)))
        fetch.wait()
        pl.loop(0, model_width // step)(lambda c: results_of(pl.ds(pl.multiple_of(c * step, step), step)))


def expert_block(pieces, expert_gate, expert_up, expert_down):
    total, width = sum(p.shape[0] for p in pieces), pieces[0].shape[1]
    model_width, units = expert_gate.shape
    out = in_vmem((total // 2, model_width), jnp.bfloat16)
    return pl.pallas_call(
        functools.partial(expert_kernel, len(pieces)),
        out_shape=(out, out),
        in_specs=[VMEM] * (len(pieces) + 2) + [HBM],
        out_specs=(VMEM, VMEM),
        scratch_shapes=[
            pltpu.VMEM((total, width), jnp.bfloat16),
            pltpu.VMEM((total, units), jnp.bfloat16),
            pltpu.VMEM(expert_down.shape, expert_down.dtype),
            pltpu.SemaphoreType.DMA,
        ],
        compiler_params=pltpu.CompilerParams(vmem_limit_bytes=(8 << 20) + 4 * total * units + 2 * total * width + 2 * expert_down.size),
        cost_estimate=pl.CostEstimate(
            flops=6 * total * model_width * units,
            bytes_accessed=4 * total * width,
            transcendentals=total * units,
        ),
    )(*(held(p) for p in pieces), held(expert_gate), held(expert_up), stored(expert_down))


def add_kernel(count, rows, sizes, *refs):
    total = None
    for ref, (low, high) in zip(refs[:count], rows, strict=True):
        value = ref[...].astype(jnp.float32)[low:high]
        total = value if total is None else total + value
    low = 0
    for out_ref, size in zip(refs[count:], sizes, strict=True):
        out_ref[...] = total[low : low + size].astype(jnp.bfloat16)
        low += size


def add(values, rows, sizes, last=False):
    width = values[0].shape[1]
    shape = jax.ShapeDtypeStruct if last else in_vmem
    elements = sum(v.size for v in values)
    return pl.pallas_call(
        functools.partial(add_kernel, len(values), rows, sizes),
        out_shape=tuple(shape((size, width), jnp.bfloat16) for size in sizes),
        in_specs=[VMEM] * len(values),
        out_specs=(VMEM,) * len(sizes),
        compiler_params=pltpu.CompilerParams(vmem_limit_bytes=(4 << 20) + 8 * values[0].size),
        cost_estimate=pl.CostEstimate(flops=elements, bytes_accessed=2 * elements, transcendentals=0),
    )(*(held(v) for v in values))


def per_device(
    hidden_in,
    expert_routes,
    route_scores,
    expert_gate,
    expert_up,
    expert_down,
    query_latent,
    latent_cache,
    cache_lengths,
):
    tok_rows, model_width = hidden_in.shape
    ep_count, sub_count = lax.axis_size("ep"), lax.axis_size("sub")
    inner = 4
    outer = ep_count // inner

    def swap(value, even, odd):
        pairs = [
            (i * sub_count + s, (i ^ (odd if s else even)) * sub_count + s)
            for i in range(ep_count)
            for s in range(sub_count)
        ]
        return lax.ppermute(value, ("ep", "sub"), pairs)

    def first(value, k):
        return swap(value, inner * k, k if inner == outer else inner * k)

    def second(value, k):
        return swap(value, k, inner * k if inner == outer else k)

    def over_cores(value):
        return lax.ppermute(value, "sub", [(i, i ^ 1) for i in range(sub_count)])

    own = pack(hidden_in, expert_routes, route_scores, ep_count)
    near = {k: first(own, k) for k in range(outer - 1, 0, -1)}
    last = inner - 1
    ahead = second(own, last)
    received = [near[k] for k in range(1, outer)]
    block, column = join([own, *received]), join(received, [ahead])
    steps = [*range(last - 1, 0, -1), last]
    far = {k: second(column if k == last else block, k) for k in steps}
    attention_latent, *weights, token = attend(
        query_latent,
        latent_cache,
        cache_lengths,
        (expert_gate[0], expert_up[0]),
        block,
    )
    pieces = [block] + [tie(far[k], token) for k in range(1, last)] + [join([ahead, far[last]], [token])]
    pieces += [over_cores(p) for p in pieces]
    mine, other = expert_block(pieces, *weights, expert_down[0])

    size = (outer - 1) * tok_rows
    kept, column, *parts = add([mine, over_cores(other)], [(0, mine.shape[0])] * 2, [tok_rows, size] * inner)
    far = [second(parts[2 * k - 1], k) for k in steps]
    side = [second(parts[2 * k - 2], k) for k in steps]
    near = add([column, *far], [(0, size)] * inner, [tok_rows] * (outer - 1))
    near = [first(near[k - 1], k) for k in range(outer - 1, 0, -1)]
    (moe_output,) = add([kept, *side, *near], [(0, tok_rows)] * (1 + len(side) + len(near)), [tok_rows], last=True)
    return (moe_output, attention_latent)


def solution(mesh):
    placed = (
        P(("groups", "ep", "sub"), None),
        P(("groups", "ep", "sub"), None),
        P(("groups", "ep", "sub"), None),
        P("ep", None, "sub"),
        P("ep", None, "sub"),
        P("ep", "sub", None),
        P(("groups", "ep", "sub"), None, None),
        P(("groups", "ep", "sub"), None, None),
        P(("groups", "ep", "sub")),
    )
    return jax.shard_map(
        per_device,
        mesh=mesh,
        in_specs=placed,
        out_specs=(P(("groups", "ep", "sub"), None), P(("groups", "ep", "sub"), None, None)),
        check_vma=False,
    )
```

```python
import functools

import jax
import jax.numpy as jnp
from jax import lax
from jax.experimental import pallas as pl
from jax.experimental.pallas import tpu as pltpu
from jax.sharding import PartitionSpec as P

LATENT = 512


SOFTMAX_SCALE = 192.0 ** (-0.5)
ROUTE_SCALE = 2.5
LANES = 128
FETCHES = 2


VMEM = pl.BlockSpec(memory_space=pltpu.VMEM)
SMEM = pl.BlockSpec(memory_space=pltpu.SMEM)
ANY = pl.BlockSpec(memory_space=pl.ANY)
HBM = pl.BlockSpec(memory_space=pltpu.HBM)


def in_vmem(shape, dtype):
    return pltpu.VMEM(shape, dtype)


def stored(value):
    return pltpu.with_memory_space_constraint(value, pltpu.HBM)


def held(value):
    return pltpu.with_memory_space_constraint(value, pltpu.VMEM)


def attend_kernel(
    lengths_hbm, query_hbm, cache_hbm, gate_hbm, up_hbm, down_hbm, after_ref,
    out_ref, gate_ref, up_ref, down_ref, token_ref, lengths_ref, query_ref, cache_ref, sems,
):
    pairs = [(lengths_hbm, lengths_ref), (query_hbm, query_ref), (cache_hbm, cache_ref)]
    for source, target in ((gate_hbm, gate_ref), (up_hbm, up_ref), (down_hbm, down_ref)):
        rows = source.shape[0] // FETCHES
        pairs += [(source.at[pl.ds(i * rows, rows)], target.at[pl.ds(i * rows, rows)]) for i in range(FETCHES)]
    copies = [pltpu.make_async_copy(s, t, sems.at[i]) for i, (s, t) in enumerate(pairs)]
    for copy in copies:
        copy.start()
    for copy in copies[:3]:
        copy.wait()
    latent = out_ref.shape[2]
    for r in range(query_ref.shape[0]):
        query, cache = query_ref[r], cache_ref[r]
        scores = SOFTMAX_SCALE * lax.dot_general(
            query, cache, (((0,), (0,)), ((), ())), preferred_element_type=jnp.float32
        )
        visible = lax.broadcasted_iota(jnp.int32, scores.shape, 1) < lengths_ref[r]
        scores = jnp.where(visible, scores, -1e30)
        largest = jnp.max(scores, axis=1, keepdims=True)
        powered = jnp.where(visible, jnp.exp(scores - largest), 0.0)
        probability = (powered / jnp.sum(powered, axis=1, keepdims=True)).astype(jnp.bfloat16)
        out_ref[r] = lax.dot_general(
            probability, cache[:latent], (((1,), (1,)), ((), ())), preferred_element_type=jnp.float32
        ).astype(jnp.bfloat16)
    token_ref[...] = jnp.zeros_like(token_ref)
    for copy in copies[3:]:
        copy.wait()


def attend(query_latent, latent_cache, cache_lengths, weights, after):
    rows, heads, entries = query_latent.shape
    positions = latent_cache.shape[1]
    query, cache = jnp.swapaxes(query_latent, 1, 2), jnp.swapaxes(latent_cache, 1, 2)
    operands = (cache_lengths, query, cache, *weights)
    return pl.pallas_call(
        attend_kernel,
        out_shape=(
            jax.ShapeDtypeStruct((rows, heads, LATENT), jnp.bfloat16),
            *(in_vmem(w.shape, w.dtype) for w in weights),
            in_vmem((8, LANES), jnp.float32),
        ),
        in_specs=[HBM] * 6 + [ANY],
        out_specs=(VMEM,) * 5,
        scratch_shapes=[
            pltpu.SMEM(cache_lengths.shape, jnp.int32),
            pltpu.VMEM(query.shape, query.dtype),
            pltpu.VMEM(cache.shape, cache.dtype),
            pltpu.SemaphoreType.DMA((3 + 3 * FETCHES,)),
        ],
        compiler_params=pltpu.CompilerParams(vmem_limit_bytes=12 << 20),
        cost_estimate=pl.CostEstimate(
            flops=4 * rows * heads * positions * entries,
            bytes_accessed=2 * sum(w.size for w in weights),
            transcendentals=rows * heads * positions,
        ),
    )(*(stored(v) for v in operands), after)


def rounds_up(value, step):
    return -(-value // step) * step


def pack_kernel(hidden_ref, routes_ref, scores_ref, out_ref, rows_ref, named_ref, affinity_ref, sems):
    rows, model_width = hidden_ref.shape
    copies = [
        pltpu.make_async_copy(source, target, sems.at[i])
        for i, (source, target) in enumerate(
            ((routes_ref, named_ref), (scores_ref, affinity_ref), (hidden_ref, rows_ref))
        )
    ]
    for copy in copies:
        copy.start()
    copies[0].wait()
    copies[1].wait()
    scores = affinity_ref[...]
    routes = named_ref[...]
    weights = ROUTE_SCALE * scores / jnp.sum(scores, axis=1, keepdims=True)
    lanes = out_ref.shape[1] - model_width
    lane = lax.broadcasted_iota(jnp.int32, (rows, lanes), 1)
    experts = lanes // 2
    dense = jnp.zeros((rows, lanes), jnp.float32)
    for k in range(routes.shape[1]):
        named = routes[:, k : k + 1]
        dense += jnp.where((lane == named) | (lane == named + experts), weights[:, k : k + 1], 0.0)
    high = dense.astype(jnp.bfloat16).astype(jnp.float32)
    out_ref[:, model_width:] = jnp.where(lane < experts, high, dense - high).astype(jnp.bfloat16)
    copies[2].wait()
    out_ref[:, :model_width] = rows_ref[...]


def pack(hidden_in, expert_routes, route_scores, experts):
    rows, model_width = hidden_in.shape
    lanes = rounds_up(2 * experts, LANES)
    return pl.pallas_call(
        pack_kernel,
        out_shape=in_vmem((rows, model_width + lanes), jnp.bfloat16),
        in_specs=[HBM] * 3,
        out_specs=VMEM,
        scratch_shapes=[
            pltpu.VMEM(hidden_in.shape, hidden_in.dtype),
            pltpu.VMEM(expert_routes.shape, expert_routes.dtype),
            pltpu.VMEM(route_scores.shape, route_scores.dtype),
            pltpu.SemaphoreType.DMA((3,)),
        ],
        compiler_params=pltpu.CompilerParams(vmem_limit_bytes=4 << 20),
        cost_estimate=pl.CostEstimate(flops=1 << 16, bytes_accessed=4 * rows * model_width, transcendentals=0),
    )(stored(hidden_in), stored(expert_routes), stored(route_scores))


def join_kernel(*refs):
    value = jnp.concatenate([ref[...].astype(jnp.float32) for ref in refs[:-1]], axis=0)
    refs[-1][...] = value.astype(jnp.bfloat16)


def join(pieces):
    total, width = sum(p.shape[0] for p in pieces), pieces[0].shape[1]
    return pl.pallas_call(
        join_kernel,
        out_shape=in_vmem((total, width), jnp.bfloat16),
        in_specs=[VMEM] * len(pieces),
        out_specs=VMEM,
        compiler_params=pltpu.CompilerParams(vmem_limit_bytes=(2 << 20) + 8 * total * width),
        cost_estimate=pl.CostEstimate(flops=total * width, bytes_accessed=4 * total * width, transcendentals=0),
    )(*(held(p) for p in pieces))


def tie_kernel(value_ref, after_ref, out_ref):
    pass


def tie(value, after):
    return pl.pallas_call(
        tie_kernel,
        out_shape=in_vmem(value.shape, value.dtype),
        in_specs=[VMEM, VMEM],
        out_specs=VMEM,
        input_output_aliases={0: 0},
        compiler_params=pltpu.CompilerParams(vmem_limit_bytes=1 << 20),
        cost_estimate=pl.CostEstimate(flops=0, bytes_accessed=0, transcendentals=0),
    )(held(value), held(after))


def hidden_kernel(count, *refs):
    pieces = refs[:count]
    gate_ref, up_ref, hidden_ref, rows_ref = refs[count:]
    total, _ = rows_ref.shape
    model_width, units = gate_ref.shape
    lanes = rows_ref.shape[1] - model_width
    me = lax.axis_index("ep")
    block = min(total, 256)
    chunk = 256

    low = 0
    for piece in pieces:
        rows_ref[low : low + piece.shape[0], :] = piece[...]
        low += piece.shape[0]

    def units_of(here):
        tail = rows_ref[here, model_width:].astype(jnp.float32)
        lane = lax.broadcasted_iota(jnp.int32, (block, lanes), 1)
        taken = (lane == me) | (lane == me + lanes // 2)
        weight = jnp.sum(jnp.where(taken, tail, 0.0), axis=1, keepdims=True)
        for c in range(units // chunk):
            cols = slice(c * chunk, (c + 1) * chunk)
            x = rows_ref[here, :model_width]
            gate_value = jnp.dot(x, gate_ref[:, cols], preferred_element_type=jnp.float32)
            up_value = jnp.dot(x, up_ref[:, cols], preferred_element_type=jnp.float32)
            value = gate_value / (1.0 + jnp.exp(-gate_value)) * up_value * weight
            hidden_ref[here, cols] = value.astype(jnp.bfloat16)

    if total == block:
        units_of(slice(0, block))
    else:
        pl.loop(0, total // block)(lambda i: units_of(pl.ds(pl.multiple_of(i * block, block), block)))


def hidden_units(pieces, expert_gate, expert_up):
    total, width = sum(p.shape[0] for p in pieces), pieces[0].shape[1]
    model_width, units = expert_gate.shape
    return pl.pallas_call(
        functools.partial(hidden_kernel, len(pieces)),
        out_shape=in_vmem((total, units), jnp.bfloat16),
        in_specs=[VMEM] * (len(pieces) + 2),
        out_specs=VMEM,
        scratch_shapes=[pltpu.VMEM((total, width), jnp.bfloat16)],
        compiler_params=pltpu.CompilerParams(vmem_limit_bytes=(8 << 20) + 4 * total * width),
        cost_estimate=pl.CostEstimate(
            flops=4 * total * model_width * units,
            bytes_accessed=4 * model_width * units + 2 * total * width,
            transcendentals=total * units,
        ),
    )(*(held(v) for v in (*pieces, expert_gate, expert_up)))


def down_kernel(hidden_ref, down_ref, out_ref):
    total, model_width = out_ref.shape
    block = min(total, 256)
    step = 512

    def results_of(cols):
        for i in range(total // block):
            rows = slice(i * block, (i + 1) * block)
            value = jnp.dot(hidden_ref[rows, :], down_ref[:, cols], preferred_element_type=jnp.float32)
            out_ref[rows, cols] = value.astype(jnp.bfloat16)

    if total == block:
        for c in range(model_width // step):
            results_of(slice(c * step, (c + 1) * step))
    else:
        pl.loop(0, model_width // step)(lambda c: results_of(pl.ds(pl.multiple_of(c * step, step), step)))


def down(hidden, expert_down):
    total, units = hidden.shape
    model_width = expert_down.shape[1]
    return pl.pallas_call(
        down_kernel,
        out_shape=in_vmem((total, model_width), jnp.bfloat16),
        in_specs=[VMEM] * 2,
        out_specs=VMEM,
        compiler_params=pltpu.CompilerParams(vmem_limit_bytes=8 << 20),
        cost_estimate=pl.CostEstimate(
            flops=2 * total * model_width * units,
            bytes_accessed=2 * model_width * units + 2 * total * model_width,
            transcendentals=0,
        ),
    )(held(hidden), held(expert_down))


def add_kernel(count, rows, sizes, *refs):
    total = None
    for ref, (low, high) in zip(refs[:count], rows, strict=True):
        value = ref[...].astype(jnp.float32)[low:high]
        total = value if total is None else total + value
    low = 0
    for out_ref, size in zip(refs[count:], sizes, strict=True):
        out_ref[...] = total[low : low + size].astype(jnp.bfloat16)
        low += size


def add(values, rows, sizes, last=False):
    width = values[0].shape[1]
    shape = jax.ShapeDtypeStruct if last else in_vmem
    elements = sum(v.size for v in values)
    return pl.pallas_call(
        functools.partial(add_kernel, len(values), rows, sizes),
        out_shape=tuple(shape((size, width), jnp.bfloat16) for size in sizes),
        in_specs=[VMEM] * len(values),
        out_specs=(VMEM,) * len(sizes),
        compiler_params=pltpu.CompilerParams(vmem_limit_bytes=(4 << 20) + 8 * values[0].size),
        cost_estimate=pl.CostEstimate(flops=elements, bytes_accessed=2 * elements, transcendentals=0),
    )(*(held(v) for v in values))


def per_device(
    hidden_in,
    expert_routes,
    route_scores,
    expert_gate,
    expert_up,
    expert_down,
    query_latent,
    latent_cache,
    cache_lengths,
):
    tok_rows, model_width = hidden_in.shape
    ep_count, sub_count = lax.axis_size("ep"), lax.axis_size("sub")
    inner = 4
    outer = ep_count // inner

    def swap(value, even, odd):
        pairs = [
            (i * sub_count + s, (i ^ (odd if s else even)) * sub_count + s)
            for i in range(ep_count)
            for s in range(sub_count)
        ]
        return lax.ppermute(value, ("ep", "sub"), pairs)

    def first(value, k):
        return swap(value, inner * k, k if inner == outer else inner * k)

    def second(value, k):
        return swap(value, k, inner * k if inner == outer else k)

    def over_cores(value):
        return lax.ppermute(value, "sub", [(i, i ^ 1) for i in range(sub_count)])

    own = pack(hidden_in, expert_routes, route_scores, ep_count)
    near = {k: first(own, k) for k in range(outer - 1, 0, -1)}
    block = join([own] + [near[k] for k in range(1, outer)])
    steps = [*range(inner - 2, 0, -1), inner - 1]
    far = {k: second(block, k) for k in steps}
    attention_latent, *weights, token = attend(
        query_latent,
        latent_cache,
        cache_lengths,
        (expert_gate[0], expert_up[0], expert_down[0]),
        block,
    )
    pieces = [block] + [tie(far[k], token) for k in range(1, inner)]
    received = [over_cores(p) for p in pieces]
    hidden = hidden_units(pieces, *weights[:2])
    other = down(hidden_units(received, *weights[:2]), weights[2])
    mine = down(hidden, weights[2])

    size = (outer - 1) * tok_rows
    kept, column, *parts = add([mine, over_cores(other)], [(0, mine.shape[0])] * 2, [tok_rows, size] * inner)
    far = [second(parts[2 * k - 1], k) for k in steps]
    side = [second(parts[2 * k - 2], k) for k in steps]
    near = add([column, *far], [(0, size)] * inner, [tok_rows] * (outer - 1))
    near = [first(near[k - 1], k) for k in range(outer - 1, 0, -1)]
    (moe_output,) = add([kept, *side, *near], [(0, tok_rows)] * (1 + len(side) + len(near)), [tok_rows], last=True)
    return (moe_output, attention_latent)


def solution(mesh):
    placed = (
        P(("groups", "ep", "sub"), None),
        P(("groups", "ep", "sub"), None),
        P(("groups", "ep", "sub"), None),
        P("ep", None, "sub"),
        P("ep", None, "sub"),
        P("ep", "sub", None),
        P(("groups", "ep", "sub"), None, None),
        P(("groups", "ep", "sub"), None, None),
        P(("groups", "ep", "sub")),
    )
    return jax.shard_map(
        per_device,
        mesh=mesh,
        in_specs=placed,
        out_specs=(P(("groups", "ep", "sub"), None), P(("groups", "ep", "sub"), None, None)),
        check_vma=False,
    )
```

```python
import functools

import jax
import jax.numpy as jnp
from jax import lax
from jax.experimental import pallas as pl
from jax.experimental.pallas import tpu as pltpu
from jax.sharding import PartitionSpec as P

LATENT = 512


SOFTMAX_SCALE = 192.0 ** (-0.5)
ROUTE_SCALE = 2.5
LANES = 128
FETCHES = 2


VMEM = pl.BlockSpec(memory_space=pltpu.VMEM)
SMEM = pl.BlockSpec(memory_space=pltpu.SMEM)
ANY = pl.BlockSpec(memory_space=pl.ANY)
HBM = pl.BlockSpec(memory_space=pltpu.HBM)


def in_vmem(shape, dtype):
    return pltpu.VMEM(shape, dtype)


def stored(value):
    return pltpu.with_memory_space_constraint(value, pltpu.HBM)


def held(value):
    return pltpu.with_memory_space_constraint(value, pltpu.VMEM)


def attend_kernel(
    lengths_hbm, query_hbm, cache_hbm, up_hbm, down_hbm, after_ref,
    out_ref, up_ref, down_ref, token_ref, lengths_ref, query_ref, cache_ref, sems,
):
    pairs = [(lengths_hbm, lengths_ref), (query_hbm, query_ref), (cache_hbm, cache_ref)]
    for source, target in ((up_hbm, up_ref), (down_hbm, down_ref)):
        rows = source.shape[0] // FETCHES
        pairs += [(source.at[pl.ds(i * rows, rows)], target.at[pl.ds(i * rows, rows)]) for i in range(FETCHES)]
    copies = [pltpu.make_async_copy(s, t, sems.at[i]) for i, (s, t) in enumerate(pairs)]
    for copy in copies:
        copy.start()
    for copy in copies[:3]:
        copy.wait()
    latent = out_ref.shape[2]
    for r in range(query_ref.shape[0]):
        query, cache = query_ref[r], cache_ref[r]
        scores = SOFTMAX_SCALE * lax.dot_general(
            query, cache, (((0,), (0,)), ((), ())), preferred_element_type=jnp.float32
        )
        visible = lax.broadcasted_iota(jnp.int32, scores.shape, 1) < lengths_ref[r]
        scores = jnp.where(visible, scores, -1e30)
        largest = jnp.max(scores, axis=1, keepdims=True)
        powered = jnp.where(visible, jnp.exp(scores - largest), 0.0)
        probability = (powered / jnp.sum(powered, axis=1, keepdims=True)).astype(jnp.bfloat16)
        out_ref[r] = lax.dot_general(
            probability, cache[:latent], (((1,), (1,)), ((), ())), preferred_element_type=jnp.float32
        ).astype(jnp.bfloat16)
    token_ref[...] = jnp.zeros_like(token_ref)
    for copy in copies[3:]:
        copy.wait()


def attend(query_latent, latent_cache, cache_lengths, weights, after):
    rows, heads, entries = query_latent.shape
    positions = latent_cache.shape[1]
    query, cache = jnp.swapaxes(query_latent, 1, 2), jnp.swapaxes(latent_cache, 1, 2)
    operands = (cache_lengths, query, cache, *weights)
    return pl.pallas_call(
        attend_kernel,
        out_shape=(
            jax.ShapeDtypeStruct((rows, heads, LATENT), jnp.bfloat16),
            *(in_vmem(w.shape, w.dtype) for w in weights),
            in_vmem((8, LANES), jnp.float32),
        ),
        in_specs=[HBM] * 5 + [ANY],
        out_specs=(VMEM,) * 4,
        scratch_shapes=[
            pltpu.SMEM(cache_lengths.shape, jnp.int32),
            pltpu.VMEM(query.shape, query.dtype),
            pltpu.VMEM(cache.shape, cache.dtype),
            pltpu.SemaphoreType.DMA((3 + 2 * FETCHES,)),
        ],
        compiler_params=pltpu.CompilerParams(vmem_limit_bytes=12 << 20),
        cost_estimate=pl.CostEstimate(
            flops=4 * rows * heads * positions * entries,
            bytes_accessed=2 * sum(w.size for w in weights),
            transcendentals=rows * heads * positions,
        ),
    )(*(stored(v) for v in operands), after)


def rounds_up(value, step):
    return -(-value // step) * step


def pack_kernel(hidden_ref, routes_ref, scores_ref, out_ref, rows_ref, named_ref, affinity_ref, sems):
    rows, model_width = hidden_ref.shape
    copies = [
        pltpu.make_async_copy(source, target, sems.at[i])
        for i, (source, target) in enumerate(
            ((routes_ref, named_ref), (scores_ref, affinity_ref), (hidden_ref, rows_ref))
        )
    ]
    for copy in copies:
        copy.start()
    copies[0].wait()
    copies[1].wait()
    scores = affinity_ref[...]
    routes = named_ref[...]
    weights = ROUTE_SCALE * scores / jnp.sum(scores, axis=1, keepdims=True)
    lanes = out_ref.shape[1] - model_width
    lane = lax.broadcasted_iota(jnp.int32, (rows, lanes), 1)
    experts = lanes // 2
    dense = jnp.zeros((rows, lanes), jnp.float32)
    for k in range(routes.shape[1]):
        named = routes[:, k : k + 1]
        dense += jnp.where((lane == named) | (lane == named + experts), weights[:, k : k + 1], 0.0)
    high = dense.astype(jnp.bfloat16).astype(jnp.float32)
    out_ref[:, model_width:] = jnp.where(lane < experts, high, dense - high).astype(jnp.bfloat16)
    copies[2].wait()
    out_ref[:, :model_width] = rows_ref[...]


def pack(hidden_in, expert_routes, route_scores, experts):
    rows, model_width = hidden_in.shape
    lanes = rounds_up(2 * experts, LANES)
    return pl.pallas_call(
        pack_kernel,
        out_shape=in_vmem((rows, model_width + lanes), jnp.bfloat16),
        in_specs=[HBM] * 3,
        out_specs=VMEM,
        scratch_shapes=[
            pltpu.VMEM(hidden_in.shape, hidden_in.dtype),
            pltpu.VMEM(expert_routes.shape, expert_routes.dtype),
            pltpu.VMEM(route_scores.shape, route_scores.dtype),
            pltpu.SemaphoreType.DMA((3,)),
        ],
        compiler_params=pltpu.CompilerParams(vmem_limit_bytes=4 << 20),
        cost_estimate=pl.CostEstimate(flops=1 << 16, bytes_accessed=4 * rows * model_width, transcendentals=0),
    )(stored(hidden_in), stored(expert_routes), stored(route_scores))


def join_kernel(count, *refs):
    value = jnp.concatenate([ref[...].astype(jnp.float32) for ref in refs[:count]], axis=0)
    refs[-1][...] = value.astype(jnp.bfloat16)


def join(pieces, after=()):
    total, width = sum(p.shape[0] for p in pieces), pieces[0].shape[1]
    operands = [*pieces, *after]
    return pl.pallas_call(
        functools.partial(join_kernel, len(pieces)),
        out_shape=in_vmem((total, width), jnp.bfloat16),
        in_specs=[VMEM] * len(operands),
        out_specs=VMEM,
        compiler_params=pltpu.CompilerParams(vmem_limit_bytes=(2 << 20) + 8 * total * width),
        cost_estimate=pl.CostEstimate(flops=total * width, bytes_accessed=4 * total * width, transcendentals=0),
    )(*(held(p) for p in operands))


def fetch_kernel(source_ref, target_ref, token_ref, sems):
    rows = source_ref.shape[0] // FETCHES
    copies = [
        pltpu.make_async_copy(
            source_ref.at[pl.ds(i * rows, rows)], target_ref.at[pl.ds(i * rows, rows)], sems.at[i]
        )
        for i in range(FETCHES)
    ]
    for copy in copies:
        copy.start()
    token_ref[...] = jnp.zeros_like(token_ref)
    for copy in copies:
        copy.wait()


def fetch(value):
    return pl.pallas_call(
        fetch_kernel,
        out_shape=(in_vmem(value.shape, value.dtype), in_vmem((8, LANES), jnp.float32)),
        in_specs=[HBM],
        out_specs=(VMEM, VMEM),
        scratch_shapes=[pltpu.SemaphoreType.DMA((FETCHES,))],
        compiler_params=pltpu.CompilerParams(vmem_limit_bytes=1 << 20),
        cost_estimate=pl.CostEstimate(flops=0, bytes_accessed=2 * value.size, transcendentals=0),
    )(stored(value))


def tie_kernel(value_ref, after_ref, out_ref):
    pass


def tie(value, after):
    return pl.pallas_call(
        tie_kernel,
        out_shape=in_vmem(value.shape, value.dtype),
        in_specs=[VMEM, VMEM],
        out_specs=VMEM,
        input_output_aliases={0: 0},
        compiler_params=pltpu.CompilerParams(vmem_limit_bytes=1 << 20),
        cost_estimate=pl.CostEstimate(flops=0, bytes_accessed=0, transcendentals=0),
    )(held(value), held(after))


def hidden_kernel(count, *refs):
    pieces = refs[:count]
    gate_ref, up_ref, hidden_ref, rows_ref = refs[count:]
    total, _ = rows_ref.shape
    model_width, units = gate_ref.shape
    lanes = rows_ref.shape[1] - model_width
    me = lax.axis_index("ep")
    block = min(total, 256)
    chunk = 256

    low = 0
    for piece in pieces:
        rows_ref[low : low + piece.shape[0], :] = piece[...]
        low += piece.shape[0]

    def units_of(here):
        tail = rows_ref[here, model_width:].astype(jnp.float32)
        lane = lax.broadcasted_iota(jnp.int32, (block, lanes), 1)
        taken = (lane == me) | (lane == me + lanes // 2)
        weight = jnp.sum(jnp.where(taken, tail, 0.0), axis=1, keepdims=True)
        for c in range(units // chunk):
            cols = slice(c * chunk, (c + 1) * chunk)
            x = rows_ref[here, :model_width]
            gate_value = jnp.dot(x, gate_ref[:, cols], preferred_element_type=jnp.float32)
            up_value = jnp.dot(x, up_ref[:, cols], preferred_element_type=jnp.float32)
            value = gate_value / (1.0 + jnp.exp(-gate_value)) * up_value * weight
            hidden_ref[here, cols] = value.astype(jnp.bfloat16)

    if total == block:
        units_of(slice(0, block))
    else:
        pl.loop(0, total // block)(lambda i: units_of(pl.ds(pl.multiple_of(i * block, block), block)))


def hidden_units(pieces, expert_gate, expert_up):
    total, width = sum(p.shape[0] for p in pieces), pieces[0].shape[1]
    model_width, units = expert_gate.shape
    return pl.pallas_call(
        functools.partial(hidden_kernel, len(pieces)),
        out_shape=in_vmem((total, units), jnp.bfloat16),
        in_specs=[VMEM] * (len(pieces) + 2),
        out_specs=VMEM,
        scratch_shapes=[pltpu.VMEM((total, width), jnp.bfloat16)],
        compiler_params=pltpu.CompilerParams(vmem_limit_bytes=(8 << 20) + 4 * total * width),
        cost_estimate=pl.CostEstimate(
            flops=4 * total * model_width * units,
            bytes_accessed=4 * model_width * units + 2 * total * width,
            transcendentals=total * units,
        ),
    )(*(held(v) for v in (*pieces, expert_gate, expert_up)))


def down_kernel(hidden_ref, down_ref, out_ref):
    total, model_width = out_ref.shape
    block = min(total, 256)
    step = 512

    def results_of(cols):
        for i in range(total // block):
            rows = slice(i * block, (i + 1) * block)
            value = jnp.dot(hidden_ref[rows, :], down_ref[:, cols], preferred_element_type=jnp.float32)
            out_ref[rows, cols] = value.astype(jnp.bfloat16)

    if total == block:
        for c in range(model_width // step):
            results_of(slice(c * step, (c + 1) * step))
    else:
        pl.loop(0, model_width // step)(lambda c: results_of(pl.ds(pl.multiple_of(c * step, step), step)))


def down(hidden, expert_down):
    total, units = hidden.shape
    model_width = expert_down.shape[1]
    return pl.pallas_call(
        down_kernel,
        out_shape=in_vmem((total, model_width), jnp.bfloat16),
        in_specs=[VMEM] * 2,
        out_specs=VMEM,
        compiler_params=pltpu.CompilerParams(vmem_limit_bytes=8 << 20),
        cost_estimate=pl.CostEstimate(
            flops=2 * total * model_width * units,
            bytes_accessed=2 * model_width * units + 2 * total * model_width,
            transcendentals=0,
        ),
    )(held(hidden), held(expert_down))


def add_kernel(count, rows, sizes, *refs):
    total = None
    for ref, (low, high) in zip(refs[:count], rows, strict=True):
        value = ref[...].astype(jnp.float32)[low:high]
        total = value if total is None else total + value
    low = 0
    for out_ref, size in zip(refs[count:], sizes, strict=True):
        out_ref[...] = total[low : low + size].astype(jnp.bfloat16)
        low += size


def add(values, rows, sizes, last=False):
    width = values[0].shape[1]
    shape = jax.ShapeDtypeStruct if last else in_vmem
    elements = sum(v.size for v in values)
    return pl.pallas_call(
        functools.partial(add_kernel, len(values), rows, sizes),
        out_shape=tuple(shape((size, width), jnp.bfloat16) for size in sizes),
        in_specs=[VMEM] * len(values),
        out_specs=(VMEM,) * len(sizes),
        compiler_params=pltpu.CompilerParams(vmem_limit_bytes=(4 << 20) + 8 * values[0].size),
        cost_estimate=pl.CostEstimate(flops=elements, bytes_accessed=2 * elements, transcendentals=0),
    )(*(held(v) for v in values))


def per_device(
    hidden_in,
    expert_routes,
    route_scores,
    expert_gate,
    expert_up,
    expert_down,
    query_latent,
    latent_cache,
    cache_lengths,
):
    tok_rows, model_width = hidden_in.shape
    ep_count, sub_count = lax.axis_size("ep"), lax.axis_size("sub")
    inner = 4
    outer = ep_count // inner

    def swap(value, even, odd):
        pairs = [
            (i * sub_count + s, (i ^ (odd if s else even)) * sub_count + s)
            for i in range(ep_count)
            for s in range(sub_count)
        ]
        return lax.ppermute(value, ("ep", "sub"), pairs)

    def first(value, k):
        return swap(value, inner * k, k if inner == outer else inner * k)

    def second(value, k):
        return swap(value, k, inner * k if inner == outer else k)

    def over_cores(value):
        return lax.ppermute(value, "sub", [(i, i ^ 1) for i in range(sub_count)])

    own = pack(hidden_in, expert_routes, route_scores, ep_count)
    near = {k: first(own, k) for k in range(outer - 1, 0, -1)}
    gate, fetched = fetch(expert_gate[0])
    block = join([own] + [near[k] for k in range(1, outer)], [fetched])
    steps = [*range(inner - 2, 0, -1), inner - 1]
    far = {k: second(block, k) for k in steps}
    attention_latent, up, down_rows, token = attend(
        query_latent,
        latent_cache,
        cache_lengths,
        (expert_up[0], expert_down[0]),
        block,
    )
    pieces = [block] + [tie(far[k], token) for k in range(1, inner)]
    received = [over_cores(p) for p in pieces]
    hidden = hidden_units(pieces, gate, up)
    other = down(hidden_units(received, gate, up), down_rows)
    mine = down(hidden, down_rows)

    size = (outer - 1) * tok_rows
    kept, column, *parts = add([mine, over_cores(other)], [(0, mine.shape[0])] * 2, [tok_rows, size] * inner)
    far = [second(parts[2 * k - 1], k) for k in steps]
    side = [second(parts[2 * k - 2], k) for k in steps]
    near = add([column, *far], [(0, size)] * inner, [tok_rows] * (outer - 1))
    near = [first(near[k - 1], k) for k in range(outer - 1, 0, -1)]
    (moe_output,) = add([kept, *side, *near], [(0, tok_rows)] * (1 + len(side) + len(near)), [tok_rows], last=True)
    return (moe_output, attention_latent)


def solution(mesh):
    placed = (
        P(("groups", "ep", "sub"), None),
        P(("groups", "ep", "sub"), None),
        P(("groups", "ep", "sub"), None),
        P("ep", None, "sub"),
        P("ep", None, "sub"),
        P("ep", "sub", None),
        P(("groups", "ep", "sub"), None, None),
        P(("groups", "ep", "sub"), None, None),
        P(("groups", "ep", "sub")),
    )
    return jax.shard_map(
        per_device,
        mesh=mesh,
        in_specs=placed,
        out_specs=(P(("groups", "ep", "sub"), None), P(("groups", "ep", "sub"), None, None)),
        check_vma=False,
    )
```

```python
import functools

import jax
import jax.numpy as jnp
from jax import lax
from jax.experimental import pallas as pl
from jax.experimental.pallas import tpu as pltpu
from jax.sharding import PartitionSpec as P

LATENT = 512


SOFTMAX_SCALE = 192.0 ** (-0.5)
ROUTE_SCALE = 2.5
LANES = 128
FETCHES = 2


VMEM = pl.BlockSpec(memory_space=pltpu.VMEM)
SMEM = pl.BlockSpec(memory_space=pltpu.SMEM)
ANY = pl.BlockSpec(memory_space=pl.ANY)
HBM = pl.BlockSpec(memory_space=pltpu.HBM)


def in_vmem(shape, dtype):
    return pltpu.VMEM(shape, dtype)


def stored(value):
    return pltpu.with_memory_space_constraint(value, pltpu.HBM)


def held(value):
    return pltpu.with_memory_space_constraint(value, pltpu.VMEM)


def attend_kernel(
    lengths_hbm, query_hbm, cache_hbm, up_hbm, down_hbm, after_ref,
    out_ref, up_ref, down_ref, token_ref, lengths_ref, query_ref, cache_ref, sems,
):
    pairs = [(lengths_hbm, lengths_ref), (query_hbm, query_ref), (cache_hbm, cache_ref)]
    for source, target in ((up_hbm, up_ref), (down_hbm, down_ref)):
        rows = source.shape[0] // FETCHES
        pairs += [(source.at[pl.ds(i * rows, rows)], target.at[pl.ds(i * rows, rows)]) for i in range(FETCHES)]
    copies = [pltpu.make_async_copy(s, t, sems.at[i]) for i, (s, t) in enumerate(pairs)]
    for copy in copies:
        copy.start()
    for copy in copies[:3]:
        copy.wait()
    latent = out_ref.shape[2]
    for r in range(query_ref.shape[0]):
        query, cache = query_ref[r], cache_ref[r]
        scores = SOFTMAX_SCALE * lax.dot_general(
            query, cache, (((0,), (0,)), ((), ())), preferred_element_type=jnp.float32
        )
        visible = lax.broadcasted_iota(jnp.int32, scores.shape, 1) < lengths_ref[r]
        scores = jnp.where(visible, scores, -1e30)
        largest = jnp.max(scores, axis=1, keepdims=True)
        powered = jnp.where(visible, jnp.exp(scores - largest), 0.0)
        probability = (powered / jnp.sum(powered, axis=1, keepdims=True)).astype(jnp.bfloat16)
        out_ref[r] = lax.dot_general(
            probability, cache[:latent], (((1,), (1,)), ((), ())), preferred_element_type=jnp.float32
        ).astype(jnp.bfloat16)
    token_ref[...] = jnp.zeros_like(token_ref)
    for copy in copies[3:]:
        copy.wait()


def attend(query_latent, latent_cache, cache_lengths, weights, after):
    rows, heads, entries = query_latent.shape
    positions = latent_cache.shape[1]
    query, cache = jnp.swapaxes(query_latent, 1, 2), jnp.swapaxes(latent_cache, 1, 2)
    operands = (cache_lengths, query, cache, *weights)
    return pl.pallas_call(
        attend_kernel,
        out_shape=(
            jax.ShapeDtypeStruct((rows, heads, LATENT), jnp.bfloat16),
            *(in_vmem(w.shape, w.dtype) for w in weights),
            in_vmem((8, LANES), jnp.float32),
        ),
        in_specs=[HBM] * 5 + [ANY],
        out_specs=(VMEM,) * 4,
        scratch_shapes=[
            pltpu.SMEM(cache_lengths.shape, jnp.int32),
            pltpu.VMEM(query.shape, query.dtype),
            pltpu.VMEM(cache.shape, cache.dtype),
            pltpu.SemaphoreType.DMA((3 + 2 * FETCHES,)),
        ],
        compiler_params=pltpu.CompilerParams(vmem_limit_bytes=12 << 20),
        cost_estimate=pl.CostEstimate(
            flops=4 * rows * heads * positions * entries,
            bytes_accessed=2 * sum(w.size for w in weights),
            transcendentals=rows * heads * positions,
        ),
    )(*(stored(v) for v in operands), after)


def rounds_up(value, step):
    return -(-value // step) * step


def pack_kernel(hidden_ref, routes_ref, scores_ref, out_ref, rows_ref, named_ref, affinity_ref, sems):
    rows, model_width = hidden_ref.shape
    copies = [
        pltpu.make_async_copy(source, target, sems.at[i])
        for i, (source, target) in enumerate(
            ((routes_ref, named_ref), (scores_ref, affinity_ref), (hidden_ref, rows_ref))
        )
    ]
    for copy in copies:
        copy.start()
    copies[0].wait()
    copies[1].wait()
    scores = affinity_ref[...]
    routes = named_ref[...]
    weights = ROUTE_SCALE * scores / jnp.sum(scores, axis=1, keepdims=True)
    lanes = out_ref.shape[1] - model_width
    lane = lax.broadcasted_iota(jnp.int32, (rows, lanes), 1)
    experts = lanes // 2
    dense = jnp.zeros((rows, lanes), jnp.float32)
    for k in range(routes.shape[1]):
        named = routes[:, k : k + 1]
        dense += jnp.where((lane == named) | (lane == named + experts), weights[:, k : k + 1], 0.0)
    high = dense.astype(jnp.bfloat16).astype(jnp.float32)
    out_ref[:, model_width:] = jnp.where(lane < experts, high, dense - high).astype(jnp.bfloat16)
    copies[2].wait()
    out_ref[:, :model_width] = rows_ref[...]


def pack(hidden_in, expert_routes, route_scores, experts):
    rows, model_width = hidden_in.shape
    lanes = rounds_up(2 * experts, LANES)
    return pl.pallas_call(
        pack_kernel,
        out_shape=in_vmem((rows, model_width + lanes), jnp.bfloat16),
        in_specs=[HBM] * 3,
        out_specs=VMEM,
        scratch_shapes=[
            pltpu.VMEM(hidden_in.shape, hidden_in.dtype),
            pltpu.VMEM(expert_routes.shape, expert_routes.dtype),
            pltpu.VMEM(route_scores.shape, route_scores.dtype),
            pltpu.SemaphoreType.DMA((3,)),
        ],
        compiler_params=pltpu.CompilerParams(vmem_limit_bytes=4 << 20),
        cost_estimate=pl.CostEstimate(flops=1 << 16, bytes_accessed=4 * rows * model_width, transcendentals=0),
    )(stored(hidden_in), stored(expert_routes), stored(route_scores))


def join_kernel(count, *refs):
    value = jnp.concatenate([ref[...].astype(jnp.float32) for ref in refs[:count]], axis=0)
    refs[-1][...] = value.astype(jnp.bfloat16)


def join(pieces, after=()):
    total, width = sum(p.shape[0] for p in pieces), pieces[0].shape[1]
    operands = [*pieces, *after]
    return pl.pallas_call(
        functools.partial(join_kernel, len(pieces)),
        out_shape=in_vmem((total, width), jnp.bfloat16),
        in_specs=[VMEM] * len(operands),
        out_specs=VMEM,
        compiler_params=pltpu.CompilerParams(vmem_limit_bytes=(2 << 20) + 8 * total * width),
        cost_estimate=pl.CostEstimate(flops=total * width, bytes_accessed=4 * total * width, transcendentals=0),
    )(*(held(p) for p in operands))


def fetch_kernel(source_ref, target_ref, token_ref, sems):
    rows = source_ref.shape[0] // FETCHES
    copies = [
        pltpu.make_async_copy(
            source_ref.at[pl.ds(i * rows, rows)], target_ref.at[pl.ds(i * rows, rows)], sems.at[i]
        )
        for i in range(FETCHES)
    ]
    for copy in copies:
        copy.start()
    token_ref[...] = jnp.zeros_like(token_ref)
    for copy in copies:
        copy.wait()


def fetch(value):
    return pl.pallas_call(
        fetch_kernel,
        out_shape=(in_vmem(value.shape, value.dtype), in_vmem((8, LANES), jnp.float32)),
        in_specs=[HBM],
        out_specs=(VMEM, VMEM),
        scratch_shapes=[pltpu.SemaphoreType.DMA((FETCHES,))],
        compiler_params=pltpu.CompilerParams(vmem_limit_bytes=1 << 20),
        cost_estimate=pl.CostEstimate(flops=0, bytes_accessed=2 * value.size, transcendentals=0),
    )(stored(value))


def tie_kernel(value_ref, after_ref, out_ref):
    pass


def tie(value, after):
    return pl.pallas_call(
        tie_kernel,
        out_shape=in_vmem(value.shape, value.dtype),
        in_specs=[VMEM, VMEM],
        out_specs=VMEM,
        input_output_aliases={0: 0},
        compiler_params=pltpu.CompilerParams(vmem_limit_bytes=1 << 20),
        cost_estimate=pl.CostEstimate(flops=0, bytes_accessed=0, transcendentals=0),
    )(held(value), held(after))


def hidden_kernel(count, *refs):
    pieces = refs[:count]
    gate_ref, up_ref, hidden_ref, rows_ref = refs[count:]
    total, _ = rows_ref.shape
    model_width, units = gate_ref.shape
    lanes = rows_ref.shape[1] - model_width
    me = lax.axis_index("ep")
    block = min(total, 256)
    chunk = 256

    low = 0
    for piece in pieces:
        rows_ref[low : low + piece.shape[0], :] = piece[...]
        low += piece.shape[0]

    def units_of(here):
        tail = rows_ref[here, model_width:].astype(jnp.float32)
        lane = lax.broadcasted_iota(jnp.int32, (block, lanes), 1)
        taken = (lane == me) | (lane == me + lanes // 2)
        weight = jnp.sum(jnp.where(taken, tail, 0.0), axis=1, keepdims=True)
        for c in range(units // chunk):
            cols = slice(c * chunk, (c + 1) * chunk)
            x = rows_ref[here, :model_width]
            gate_value = jnp.dot(x, gate_ref[:, cols], preferred_element_type=jnp.float32)
            up_value = jnp.dot(x, up_ref[:, cols], preferred_element_type=jnp.float32)
            value = gate_value / (1.0 + jnp.exp(-gate_value)) * up_value * weight
            hidden_ref[here, cols] = value.astype(jnp.bfloat16)

    if total == block:
        units_of(slice(0, block))
    else:
        pl.loop(0, total // block)(lambda i: units_of(pl.ds(pl.multiple_of(i * block, block), block)))


def hidden_units(pieces, expert_gate, expert_up):
    total, width = sum(p.shape[0] for p in pieces), pieces[0].shape[1]
    model_width, units = expert_gate.shape
    return pl.pallas_call(
        functools.partial(hidden_kernel, len(pieces)),
        out_shape=in_vmem((total, units), jnp.bfloat16),
        in_specs=[VMEM] * (len(pieces) + 2),
        out_specs=VMEM,
        scratch_shapes=[pltpu.VMEM((total, width), jnp.bfloat16)],
        compiler_params=pltpu.CompilerParams(vmem_limit_bytes=(8 << 20) + 4 * total * width),
        cost_estimate=pl.CostEstimate(
            flops=4 * total * model_width * units,
            bytes_accessed=4 * model_width * units + 2 * total * width,
            transcendentals=total * units,
        ),
    )(*(held(v) for v in (*pieces, expert_gate, expert_up)))


def down_kernel(hidden_ref, down_ref, out_ref):
    total, model_width = out_ref.shape
    block = min(total, 256)
    step = 512

    def results_of(cols):
        for i in range(total // block):
            rows = slice(i * block, (i + 1) * block)
            value = jnp.dot(hidden_ref[rows, :], down_ref[:, cols], preferred_element_type=jnp.float32)
            out_ref[rows, cols] = value.astype(jnp.bfloat16)

    if total == block:
        for c in range(model_width // step):
            results_of(slice(c * step, (c + 1) * step))
    else:
        pl.loop(0, model_width // step)(lambda c: results_of(pl.ds(pl.multiple_of(c * step, step), step)))


def down(hidden, expert_down):
    total, units = hidden.shape
    model_width = expert_down.shape[1]
    return pl.pallas_call(
        down_kernel,
        out_shape=in_vmem((total, model_width), jnp.bfloat16),
        in_specs=[VMEM] * 2,
        out_specs=VMEM,
        compiler_params=pltpu.CompilerParams(vmem_limit_bytes=8 << 20),
        cost_estimate=pl.CostEstimate(
            flops=2 * total * model_width * units,
            bytes_accessed=2 * model_width * units + 2 * total * model_width,
            transcendentals=0,
        ),
    )(held(hidden), held(expert_down))


def add_kernel(count, rows, sizes, *refs):
    total = None
    for ref, (low, high) in zip(refs[:count], rows, strict=True):
        value = ref[...].astype(jnp.float32)[low:high]
        total = value if total is None else total + value
    low = 0
    for out_ref, size in zip(refs[count:], sizes, strict=True):
        out_ref[...] = total[low : low + size].astype(jnp.bfloat16)
        low += size


def add(values, rows, sizes, last=False):
    width = values[0].shape[1]
    shape = jax.ShapeDtypeStruct if last else in_vmem
    elements = sum(v.size for v in values)
    return pl.pallas_call(
        functools.partial(add_kernel, len(values), rows, sizes),
        out_shape=tuple(shape((size, width), jnp.bfloat16) for size in sizes),
        in_specs=[VMEM] * len(values),
        out_specs=(VMEM,) * len(sizes),
        compiler_params=pltpu.CompilerParams(vmem_limit_bytes=(4 << 20) + 8 * values[0].size),
        cost_estimate=pl.CostEstimate(flops=elements, bytes_accessed=2 * elements, transcendentals=0),
    )(*(held(v) for v in values))


def per_device(
    hidden_in,
    expert_routes,
    route_scores,
    expert_gate,
    expert_up,
    expert_down,
    query_latent,
    latent_cache,
    cache_lengths,
):
    tok_rows, model_width = hidden_in.shape
    ep_count, sub_count = lax.axis_size("ep"), lax.axis_size("sub")
    inner = 4
    outer = ep_count // inner

    def swap(value, even, odd):
        pairs = [
            (i * sub_count + s, (i ^ (odd if s else even)) * sub_count + s)
            for i in range(ep_count)
            for s in range(sub_count)
        ]
        return lax.ppermute(value, ("ep", "sub"), pairs)

    def first(value, k):
        return swap(value, inner * k, k if inner == outer else inner * k)

    def second(value, k):
        return swap(value, k, inner * k if inner == outer else k)

    def over_cores(value):
        return lax.ppermute(value, "sub", [(i, i ^ 1) for i in range(sub_count)])

    own = pack(hidden_in, expert_routes, route_scores, ep_count)
    near = {k: first(own, k) for k in range(outer - 1, 0, -1)}
    gate, fetched = fetch(expert_gate[0])
    last = inner - 1
    ahead = second(own, last)
    received = [near[k] for k in range(1, outer)]
    block, column = join([own, *received], [fetched]), join(received, [ahead])
    steps = [*range(last - 1, 0, -1), last]
    far = {k: second(column if k == last else block, k) for k in steps}
    attention_latent, up, down_rows, token = attend(
        query_latent,
        latent_cache,
        cache_lengths,
        (expert_up[0], expert_down[0]),
        block,
    )
    pieces = [block] + [tie(far[k], token) for k in range(1, last)] + [join([ahead, far[last]], [token])]
    received = [over_cores(p) for p in pieces]
    hidden = hidden_units(pieces, gate, up)
    other = down(hidden_units(received, gate, up), down_rows)
    mine = down(hidden, down_rows)

    size = (outer - 1) * tok_rows
    kept, column, *parts = add([mine, over_cores(other)], [(0, mine.shape[0])] * 2, [tok_rows, size] * inner)
    far = [second(parts[2 * k - 1], k) for k in steps]
    side = [second(parts[2 * k - 2], k) for k in steps]
    near = add([column, *far], [(0, size)] * inner, [tok_rows] * (outer - 1))
    near = [first(near[k - 1], k) for k in range(outer - 1, 0, -1)]
    (moe_output,) = add([kept, *side, *near], [(0, tok_rows)] * (1 + len(side) + len(near)), [tok_rows], last=True)
    return (moe_output, attention_latent)


def solution(mesh):
    placed = (
        P(("groups", "ep", "sub"), None),
        P(("groups", "ep", "sub"), None),
        P(("groups", "ep", "sub"), None),
        P("ep", None, "sub"),
        P("ep", None, "sub"),
        P("ep", "sub", None),
        P(("groups", "ep", "sub"), None, None),
        P(("groups", "ep", "sub"), None, None),
        P(("groups", "ep", "sub")),
    )
    return jax.shard_map(
        per_device,
        mesh=mesh,
        in_specs=placed,
        out_specs=(P(("groups", "ep", "sub"), None), P(("groups", "ep", "sub"), None, None)),
        check_vma=False,
    )
```

```python
import functools

import jax
import jax.numpy as jnp
from jax import lax
from jax.experimental import pallas as pl
from jax.experimental.pallas import tpu as pltpu
from jax.sharding import PartitionSpec as P

LATENT = 512


SOFTMAX_SCALE = 192.0 ** (-0.5)
ROUTE_SCALE = 2.5
LANES = 128
FETCHES = 2


VMEM = pl.BlockSpec(memory_space=pltpu.VMEM)
SMEM = pl.BlockSpec(memory_space=pltpu.SMEM)
ANY = pl.BlockSpec(memory_space=pl.ANY)
HBM = pl.BlockSpec(memory_space=pltpu.HBM)


def in_vmem(shape, dtype):
    return pltpu.VMEM(shape, dtype)


def stored(value):
    return pltpu.with_memory_space_constraint(value, pltpu.HBM)


def held(value):
    return pltpu.with_memory_space_constraint(value, pltpu.VMEM)


def attend_kernel(
    lengths_hbm, query_hbm, cache_hbm, up_hbm, down_hbm, after_ref,
    out_ref, up_ref, down_ref, token_ref, lengths_ref, query_ref, cache_ref, sems,
):
    pairs = [(lengths_hbm, lengths_ref), (query_hbm, query_ref), (cache_hbm, cache_ref)]
    for source, target in ((up_hbm, up_ref), (down_hbm, down_ref)):
        rows = source.shape[0] // FETCHES
        pairs += [(source.at[pl.ds(i * rows, rows)], target.at[pl.ds(i * rows, rows)]) for i in range(FETCHES)]
    copies = [pltpu.make_async_copy(s, t, sems.at[i]) for i, (s, t) in enumerate(pairs)]
    for copy in copies:
        copy.start()
    for copy in copies[:3]:
        copy.wait()
    latent = out_ref.shape[2]
    for r in range(query_ref.shape[0]):
        query, cache = query_ref[r], cache_ref[r]
        scores = SOFTMAX_SCALE * lax.dot_general(
            query, cache, (((0,), (0,)), ((), ())), preferred_element_type=jnp.float32
        )
        visible = lax.broadcasted_iota(jnp.int32, scores.shape, 1) < lengths_ref[r]
        scores = jnp.where(visible, scores, -1e30)
        largest = jnp.max(scores, axis=1, keepdims=True)
        powered = jnp.where(visible, jnp.exp(scores - largest), 0.0)
        probability = (powered / jnp.sum(powered, axis=1, keepdims=True)).astype(jnp.bfloat16)
        out_ref[r] = lax.dot_general(
            probability, cache[:latent], (((1,), (1,)), ((), ())), preferred_element_type=jnp.float32
        ).astype(jnp.bfloat16)
    token_ref[...] = jnp.zeros_like(token_ref)
    for copy in copies[3:]:
        copy.wait()


def attend(query_latent, latent_cache, cache_lengths, weights, after):
    rows, heads, entries = query_latent.shape
    positions = latent_cache.shape[1]
    query, cache = jnp.swapaxes(query_latent, 1, 2), jnp.swapaxes(latent_cache, 1, 2)
    operands = (cache_lengths, query, cache, *weights)
    return pl.pallas_call(
        attend_kernel,
        out_shape=(
            jax.ShapeDtypeStruct((rows, heads, LATENT), jnp.bfloat16),
            *(in_vmem(w.shape, w.dtype) for w in weights),
            in_vmem((8, LANES), jnp.float32),
        ),
        in_specs=[HBM] * 5 + [ANY],
        out_specs=(VMEM,) * 4,
        scratch_shapes=[
            pltpu.SMEM(cache_lengths.shape, jnp.int32),
            pltpu.VMEM(query.shape, query.dtype),
            pltpu.VMEM(cache.shape, cache.dtype),
            pltpu.SemaphoreType.DMA((3 + 2 * FETCHES,)),
        ],
        compiler_params=pltpu.CompilerParams(vmem_limit_bytes=12 << 20),
        cost_estimate=pl.CostEstimate(
            flops=4 * rows * heads * positions * entries,
            bytes_accessed=2 * sum(w.size for w in weights),
            transcendentals=rows * heads * positions,
        ),
    )(*(stored(v) for v in operands), after)


def rounds_up(value, step):
    return -(-value // step) * step


def pack_kernel(hidden_ref, routes_ref, scores_ref, out_ref, rows_ref, named_ref, affinity_ref, sems):
    rows, model_width = hidden_ref.shape
    copies = [
        pltpu.make_async_copy(source, target, sems.at[i])
        for i, (source, target) in enumerate(
            ((routes_ref, named_ref), (scores_ref, affinity_ref), (hidden_ref, rows_ref))
        )
    ]
    for copy in copies:
        copy.start()
    copies[0].wait()
    copies[1].wait()
    scores = affinity_ref[...]
    routes = named_ref[...]
    weights = ROUTE_SCALE * scores / jnp.sum(scores, axis=1, keepdims=True)
    lanes = out_ref.shape[1] - model_width
    lane = lax.broadcasted_iota(jnp.int32, (rows, lanes), 1)
    experts = lanes // 2
    dense = jnp.zeros((rows, lanes), jnp.float32)
    for k in range(routes.shape[1]):
        named = routes[:, k : k + 1]
        dense += jnp.where((lane == named) | (lane == named + experts), weights[:, k : k + 1], 0.0)
    high = dense.astype(jnp.bfloat16).astype(jnp.float32)
    out_ref[:, model_width:] = jnp.where(lane < experts, high, dense - high).astype(jnp.bfloat16)
    copies[2].wait()
    out_ref[:, :model_width] = rows_ref[...]


def pack(hidden_in, expert_routes, route_scores, experts):
    rows, model_width = hidden_in.shape
    lanes = rounds_up(2 * experts, LANES)
    return pl.pallas_call(
        pack_kernel,
        out_shape=in_vmem((rows, model_width + lanes), jnp.bfloat16),
        in_specs=[HBM] * 3,
        out_specs=VMEM,
        scratch_shapes=[
            pltpu.VMEM(hidden_in.shape, hidden_in.dtype),
            pltpu.VMEM(expert_routes.shape, expert_routes.dtype),
            pltpu.VMEM(route_scores.shape, route_scores.dtype),
            pltpu.SemaphoreType.DMA((3,)),
        ],
        compiler_params=pltpu.CompilerParams(vmem_limit_bytes=4 << 20),
        cost_estimate=pl.CostEstimate(flops=1 << 16, bytes_accessed=4 * rows * model_width, transcendentals=0),
    )(stored(hidden_in), stored(expert_routes), stored(route_scores))


def join_kernel(count, *refs):
    value = jnp.concatenate([ref[...].astype(jnp.float32) for ref in refs[:count]], axis=0)
    refs[-1][...] = value.astype(jnp.bfloat16)


def join(pieces, after=()):
    total, width = sum(p.shape[0] for p in pieces), pieces[0].shape[1]
    operands = [*pieces, *after]
    return pl.pallas_call(
        functools.partial(join_kernel, len(pieces)),
        out_shape=in_vmem((total, width), jnp.bfloat16),
        in_specs=[VMEM] * len(operands),
        out_specs=VMEM,
        compiler_params=pltpu.CompilerParams(vmem_limit_bytes=(2 << 20) + 8 * total * width),
        cost_estimate=pl.CostEstimate(flops=total * width, bytes_accessed=4 * total * width, transcendentals=0),
    )(*(held(p) for p in operands))


def fetch_kernel(source_ref, target_ref, token_ref, sems):
    rows = source_ref.shape[0] // FETCHES
    copies = [
        pltpu.make_async_copy(
            source_ref.at[pl.ds(i * rows, rows)], target_ref.at[pl.ds(i * rows, rows)], sems.at[i]
        )
        for i in range(FETCHES)
    ]
    for copy in copies:
        copy.start()
    token_ref[...] = jnp.zeros_like(token_ref)
    for copy in copies:
        copy.wait()


def fetch(value):
    return pl.pallas_call(
        fetch_kernel,
        out_shape=(in_vmem(value.shape, value.dtype), in_vmem((8, LANES), jnp.float32)),
        in_specs=[HBM],
        out_specs=(VMEM, VMEM),
        scratch_shapes=[pltpu.SemaphoreType.DMA((FETCHES,))],
        compiler_params=pltpu.CompilerParams(vmem_limit_bytes=1 << 20),
        cost_estimate=pl.CostEstimate(flops=0, bytes_accessed=2 * value.size, transcendentals=0),
    )(stored(value))


def tie_kernel(value_ref, after_ref, out_ref):
    pass


def tie(value, after):
    return pl.pallas_call(
        tie_kernel,
        out_shape=in_vmem(value.shape, value.dtype),
        in_specs=[VMEM, VMEM],
        out_specs=VMEM,
        input_output_aliases={0: 0},
        compiler_params=pltpu.CompilerParams(vmem_limit_bytes=1 << 20),
        cost_estimate=pl.CostEstimate(flops=0, bytes_accessed=0, transcendentals=0),
    )(held(value), held(after))


def hidden_kernel(count, *refs):
    pieces = refs[:count]
    gate_ref, up_ref, hidden_ref, rows_ref = refs[count:]
    total, _ = rows_ref.shape
    model_width, units = gate_ref.shape
    lanes = rows_ref.shape[1] - model_width
    me = lax.axis_index("ep")
    block = min(total, 256)
    chunk = 256

    low = 0
    for piece in pieces:
        rows_ref[low : low + piece.shape[0], :] = piece[...]
        low += piece.shape[0]

    def units_of(here):
        tail = rows_ref[here, model_width:].astype(jnp.float32)
        lane = lax.broadcasted_iota(jnp.int32, (block, lanes), 1)
        taken = (lane == me) | (lane == me + lanes // 2)
        weight = jnp.sum(jnp.where(taken, tail, 0.0), axis=1, keepdims=True)
        for c in range(units // chunk):
            cols = slice(c * chunk, (c + 1) * chunk)
            x = rows_ref[here, :model_width]
            gate_value = jnp.dot(x, gate_ref[:, cols], preferred_element_type=jnp.float32)
            up_value = jnp.dot(x, up_ref[:, cols], preferred_element_type=jnp.float32)
            value = gate_value / (1.0 + jnp.exp(-gate_value)) * up_value * weight
            hidden_ref[here, cols] = value.astype(jnp.bfloat16)

    if total == block:
        units_of(slice(0, block))
    else:
        pl.loop(0, total // block)(lambda i: units_of(pl.ds(pl.multiple_of(i * block, block), block)))


def hidden_units(pieces, expert_gate, expert_up):
    total, width = sum(p.shape[0] for p in pieces), pieces[0].shape[1]
    model_width, units = expert_gate.shape
    return pl.pallas_call(
        functools.partial(hidden_kernel, len(pieces)),
        out_shape=in_vmem((total, units), jnp.bfloat16),
        in_specs=[VMEM] * (len(pieces) + 2),
        out_specs=VMEM,
        scratch_shapes=[pltpu.VMEM((total, width), jnp.bfloat16)],
        compiler_params=pltpu.CompilerParams(vmem_limit_bytes=(8 << 20) + 4 * total * width),
        cost_estimate=pl.CostEstimate(
            flops=4 * total * model_width * units,
            bytes_accessed=4 * model_width * units + 2 * total * width,
            transcendentals=total * units,
        ),
    )(*(held(v) for v in (*pieces, expert_gate, expert_up)))


def down_kernel(hidden_ref, down_ref, out_ref):
    total, model_width = out_ref.shape
    block = min(total, 256)
    step = 512

    def results_of(cols):
        for i in range(total // block):
            rows = slice(i * block, (i + 1) * block)
            value = jnp.dot(hidden_ref[rows, :], down_ref[:, cols], preferred_element_type=jnp.float32)
            out_ref[rows, cols] = value.astype(jnp.bfloat16)

    if total == block:
        for c in range(model_width // step):
            results_of(slice(c * step, (c + 1) * step))
    else:
        pl.loop(0, model_width // step)(lambda c: results_of(pl.ds(pl.multiple_of(c * step, step), step)))


def down(hidden, expert_down):
    total, units = hidden.shape
    model_width = expert_down.shape[1]
    return pl.pallas_call(
        down_kernel,
        out_shape=in_vmem((total, model_width), jnp.bfloat16),
        in_specs=[VMEM] * 2,
        out_specs=VMEM,
        compiler_params=pltpu.CompilerParams(vmem_limit_bytes=8 << 20),
        cost_estimate=pl.CostEstimate(
            flops=2 * total * model_width * units,
            bytes_accessed=2 * model_width * units + 2 * total * model_width,
            transcendentals=0,
        ),
    )(held(hidden), held(expert_down))


def add_kernel(count, rows, sizes, *refs):
    total = None
    for ref, (low, high) in zip(refs[:count], rows, strict=True):
        value = ref[...].astype(jnp.float32)[low:high]
        total = value if total is None else total + value
    low = 0
    for out_ref, size in zip(refs[count:], sizes, strict=True):
        out_ref[...] = total[low : low + size].astype(jnp.bfloat16)
        low += size


def add(values, rows, sizes, last=False):
    width = values[0].shape[1]
    shape = jax.ShapeDtypeStruct if last else in_vmem
    elements = sum(v.size for v in values)
    return pl.pallas_call(
        functools.partial(add_kernel, len(values), rows, sizes),
        out_shape=tuple(shape((size, width), jnp.bfloat16) for size in sizes),
        in_specs=[VMEM] * len(values),
        out_specs=(VMEM,) * len(sizes),
        compiler_params=pltpu.CompilerParams(vmem_limit_bytes=(4 << 20) + 8 * values[0].size),
        cost_estimate=pl.CostEstimate(flops=elements, bytes_accessed=2 * elements, transcendentals=0),
    )(*(held(v) for v in values))


def per_device(
    hidden_in,
    expert_routes,
    route_scores,
    expert_gate,
    expert_up,
    expert_down,
    query_latent,
    latent_cache,
    cache_lengths,
):
    tok_rows, model_width = hidden_in.shape
    ep_count, sub_count = lax.axis_size("ep"), lax.axis_size("sub")
    inner = 4
    outer = ep_count // inner

    def swap(value, even, odd):
        pairs = [
            (i * sub_count + s, (i ^ (odd if s else even)) * sub_count + s)
            for i in range(ep_count)
            for s in range(sub_count)
        ]
        return lax.ppermute(value, ("ep", "sub"), pairs)

    def first(value, k):
        return swap(value, inner * k, k if inner == outer else inner * k)

    def second(value, k):
        return swap(value, k, inner * k if inner == outer else k)

    def over_cores(value):
        return lax.ppermute(value, "sub", [(i, i ^ 1) for i in range(sub_count)])

    own = pack(hidden_in, expert_routes, route_scores, ep_count)
    near = {k: first(own, k) for k in range(outer - 1, 0, -1)}
    gate, fetched = fetch(expert_gate[0])
    block = join([own] + [near[k] for k in range(1, outer)], [fetched])
    steps = [*range(2, inner), 1]
    far = {k: second(block, k) for k in steps}
    attention_latent, up, down_rows, token = attend(
        query_latent,
        latent_cache,
        cache_lengths,
        (expert_up[0], expert_down[0]),
        block,
    )
    pieces = [block] + [tie(far[k], token) for k in range(1, inner)]
    received = [over_cores(p) for p in pieces]
    hidden = hidden_units(pieces, gate, up)
    other = down(hidden_units(received, gate, up), down_rows)
    mine = down(hidden, down_rows)

    size = (outer - 1) * tok_rows
    kept, column, *parts = add([mine, over_cores(other)], [(0, mine.shape[0])] * 2, [tok_rows, size] * inner)
    far = [second(parts[2 * k - 1], k) for k in steps]
    side = [second(parts[2 * k - 2], k) for k in steps]
    near = add([column, *far], [(0, size)] * inner, [tok_rows] * (outer - 1))
    near = [first(near[k - 1], k) for k in range(outer - 1, 0, -1)]
    (moe_output,) = add([kept, *side, *near], [(0, tok_rows)] * (1 + len(side) + len(near)), [tok_rows], last=True)
    return (moe_output, attention_latent)


def solution(mesh):
    placed = (
        P(("groups", "ep", "sub"), None),
        P(("groups", "ep", "sub"), None),
        P(("groups", "ep", "sub"), None),
        P("ep", None, "sub"),
        P("ep", None, "sub"),
        P("ep", "sub", None),
        P(("groups", "ep", "sub"), None, None),
        P(("groups", "ep", "sub"), None, None),
        P(("groups", "ep", "sub")),
    )
    return jax.shard_map(
        per_device,
        mesh=mesh,
        in_specs=placed,
        out_specs=(P(("groups", "ep", "sub"), None), P(("groups", "ep", "sub"), None, None)),
        check_vma=False,
    )
```

```python
import functools

import jax
import jax.numpy as jnp
from jax import lax
from jax.experimental import pallas as pl
from jax.experimental.pallas import tpu as pltpu
from jax.sharding import PartitionSpec as P

LATENT = 512


SOFTMAX_SCALE = 192.0 ** (-0.5)
ROUTE_SCALE = 2.5
LANES = 128
FETCHES = 2


VMEM = pl.BlockSpec(memory_space=pltpu.VMEM)
SMEM = pl.BlockSpec(memory_space=pltpu.SMEM)
ANY = pl.BlockSpec(memory_space=pl.ANY)
HBM = pl.BlockSpec(memory_space=pltpu.HBM)


def in_vmem(shape, dtype):
    return pltpu.VMEM(shape, dtype)


def stored(value):
    return pltpu.with_memory_space_constraint(value, pltpu.HBM)


def held(value):
    return pltpu.with_memory_space_constraint(value, pltpu.VMEM)


def attend_kernel(
    lengths_hbm, query_hbm, cache_hbm, up_hbm, down_hbm, after_ref,
    out_ref, up_ref, down_ref, token_ref, lengths_ref, query_ref, cache_ref, sems,
):
    pairs = [(lengths_hbm, lengths_ref), (query_hbm, query_ref), (cache_hbm, cache_ref)]
    for source, target in ((up_hbm, up_ref), (down_hbm, down_ref)):
        rows = source.shape[0] // FETCHES
        pairs += [(source.at[pl.ds(i * rows, rows)], target.at[pl.ds(i * rows, rows)]) for i in range(FETCHES)]
    copies = [pltpu.make_async_copy(s, t, sems.at[i]) for i, (s, t) in enumerate(pairs)]
    for copy in copies:
        copy.start()
    for copy in copies[:3]:
        copy.wait()
    latent = out_ref.shape[2]
    for r in range(query_ref.shape[0]):
        query, cache = query_ref[r], cache_ref[r]
        scores = SOFTMAX_SCALE * lax.dot_general(
            query, cache, (((0,), (0,)), ((), ())), preferred_element_type=jnp.float32
        )
        visible = lax.broadcasted_iota(jnp.int32, scores.shape, 1) < lengths_ref[r]
        scores = jnp.where(visible, scores, -1e30)
        largest = jnp.max(scores, axis=1, keepdims=True)
        powered = jnp.where(visible, jnp.exp(scores - largest), 0.0)
        probability = (powered / jnp.sum(powered, axis=1, keepdims=True)).astype(jnp.bfloat16)
        out_ref[r] = lax.dot_general(
            probability, cache[:latent], (((1,), (1,)), ((), ())), preferred_element_type=jnp.float32
        ).astype(jnp.bfloat16)
    token_ref[...] = jnp.zeros_like(token_ref)
    for copy in copies[3:]:
        copy.wait()


def attend(query_latent, latent_cache, cache_lengths, weights, after):
    rows, heads, entries = query_latent.shape
    positions = latent_cache.shape[1]
    query, cache = jnp.swapaxes(query_latent, 1, 2), jnp.swapaxes(latent_cache, 1, 2)
    operands = (cache_lengths, query, cache, *weights)
    return pl.pallas_call(
        attend_kernel,
        out_shape=(
            jax.ShapeDtypeStruct((rows, heads, LATENT), jnp.bfloat16),
            *(in_vmem(w.shape, w.dtype) for w in weights),
            in_vmem((8, LANES), jnp.float32),
        ),
        in_specs=[HBM] * 5 + [ANY],
        out_specs=(VMEM,) * 4,
        scratch_shapes=[
            pltpu.SMEM(cache_lengths.shape, jnp.int32),
            pltpu.VMEM(query.shape, query.dtype),
            pltpu.VMEM(cache.shape, cache.dtype),
            pltpu.SemaphoreType.DMA((3 + 2 * FETCHES,)),
        ],
        compiler_params=pltpu.CompilerParams(vmem_limit_bytes=12 << 20),
        cost_estimate=pl.CostEstimate(
            flops=4 * rows * heads * positions * entries,
            bytes_accessed=2 * sum(w.size for w in weights),
            transcendentals=rows * heads * positions,
        ),
    )(*(stored(v) for v in operands), after)


def rounds_up(value, step):
    return -(-value // step) * step


def pack_kernel(hidden_ref, routes_ref, scores_ref, out_ref, rows_ref, named_ref, affinity_ref, sems):
    rows, model_width = hidden_ref.shape
    copies = [
        pltpu.make_async_copy(source, target, sems.at[i])
        for i, (source, target) in enumerate(
            ((routes_ref, named_ref), (scores_ref, affinity_ref), (hidden_ref, rows_ref))
        )
    ]
    for copy in copies:
        copy.start()
    copies[0].wait()
    copies[1].wait()
    scores = affinity_ref[...]
    routes = named_ref[...]
    weights = ROUTE_SCALE * scores / jnp.sum(scores, axis=1, keepdims=True)
    lanes = out_ref.shape[1] - model_width
    lane = lax.broadcasted_iota(jnp.int32, (rows, lanes), 1)
    experts = lanes // 2
    dense = jnp.zeros((rows, lanes), jnp.float32)
    for k in range(routes.shape[1]):
        named = routes[:, k : k + 1]
        dense += jnp.where((lane == named) | (lane == named + experts), weights[:, k : k + 1], 0.0)
    high = dense.astype(jnp.bfloat16).astype(jnp.float32)
    out_ref[:, model_width:] = jnp.where(lane < experts, high, dense - high).astype(jnp.bfloat16)
    copies[2].wait()
    out_ref[:, :model_width] = rows_ref[...]


def pack(hidden_in, expert_routes, route_scores, experts):
    rows, model_width = hidden_in.shape
    lanes = rounds_up(2 * experts, LANES)
    return pl.pallas_call(
        pack_kernel,
        out_shape=in_vmem((rows, model_width + lanes), jnp.bfloat16),
        in_specs=[HBM] * 3,
        out_specs=VMEM,
        scratch_shapes=[
            pltpu.VMEM(hidden_in.shape, hidden_in.dtype),
            pltpu.VMEM(expert_routes.shape, expert_routes.dtype),
            pltpu.VMEM(route_scores.shape, route_scores.dtype),
            pltpu.SemaphoreType.DMA((3,)),
        ],
        compiler_params=pltpu.CompilerParams(vmem_limit_bytes=4 << 20),
        cost_estimate=pl.CostEstimate(flops=1 << 16, bytes_accessed=4 * rows * model_width, transcendentals=0),
    )(stored(hidden_in), stored(expert_routes), stored(route_scores))


def join_kernel(count, *refs):
    value = jnp.concatenate([ref[...].astype(jnp.float32) for ref in refs[:count]], axis=0)
    refs[-1][...] = value.astype(jnp.bfloat16)


def join(pieces, after=()):
    total, width = sum(p.shape[0] for p in pieces), pieces[0].shape[1]
    operands = [*pieces, *after]
    return pl.pallas_call(
        functools.partial(join_kernel, len(pieces)),
        out_shape=in_vmem((total, width), jnp.bfloat16),
        in_specs=[VMEM] * len(operands),
        out_specs=VMEM,
        compiler_params=pltpu.CompilerParams(vmem_limit_bytes=(2 << 20) + 8 * total * width),
        cost_estimate=pl.CostEstimate(flops=total * width, bytes_accessed=4 * total * width, transcendentals=0),
    )(*(held(p) for p in operands))


def fetch_kernel(source_ref, target_ref, token_ref, sems):
    rows = source_ref.shape[0] // FETCHES
    copies = [
        pltpu.make_async_copy(
            source_ref.at[pl.ds(i * rows, rows)], target_ref.at[pl.ds(i * rows, rows)], sems.at[i]
        )
        for i in range(FETCHES)
    ]
    for copy in copies:
        copy.start()
    token_ref[...] = jnp.zeros_like(token_ref)
    for copy in copies:
        copy.wait()


def fetch(value):
    return pl.pallas_call(
        fetch_kernel,
        out_shape=(in_vmem(value.shape, value.dtype), in_vmem((8, LANES), jnp.float32)),
        in_specs=[HBM],
        out_specs=(VMEM, VMEM),
        scratch_shapes=[pltpu.SemaphoreType.DMA((FETCHES,))],
        compiler_params=pltpu.CompilerParams(vmem_limit_bytes=1 << 20),
        cost_estimate=pl.CostEstimate(flops=0, bytes_accessed=2 * value.size, transcendentals=0),
    )(stored(value))


def tie_kernel(value_ref, after_ref, out_ref):
    pass


def tie(value, after):
    return pl.pallas_call(
        tie_kernel,
        out_shape=in_vmem(value.shape, value.dtype),
        in_specs=[VMEM, VMEM],
        out_specs=VMEM,
        input_output_aliases={0: 0},
        compiler_params=pltpu.CompilerParams(vmem_limit_bytes=1 << 20),
        cost_estimate=pl.CostEstimate(flops=0, bytes_accessed=0, transcendentals=0),
    )(held(value), held(after))


def hidden_kernel(count, *refs):
    pieces = refs[:count]
    gate_ref, up_ref, hidden_ref, rows_ref = refs[count:]
    total, _ = rows_ref.shape
    model_width, units = gate_ref.shape
    lanes = rows_ref.shape[1] - model_width
    me = lax.axis_index("ep")
    block = min(total, 256)
    chunk = 256

    low = 0
    for piece in pieces:
        rows_ref[low : low + piece.shape[0], :] = piece[...]
        low += piece.shape[0]

    def units_of(here):
        tail = rows_ref[here, model_width:].astype(jnp.float32)
        lane = lax.broadcasted_iota(jnp.int32, (block, lanes), 1)
        taken = (lane == me) | (lane == me + lanes // 2)
        weight = jnp.sum(jnp.where(taken, tail, 0.0), axis=1, keepdims=True)
        for c in range(units // chunk):
            cols = slice(c * chunk, (c + 1) * chunk)
            x = rows_ref[here, :model_width]
            gate_value = jnp.dot(x, gate_ref[:, cols], preferred_element_type=jnp.float32)
            up_value = jnp.dot(x, up_ref[:, cols], preferred_element_type=jnp.float32)
            value = gate_value / (1.0 + jnp.exp(-gate_value)) * up_value * weight
            hidden_ref[here, cols] = value.astype(jnp.bfloat16)

    if total == block:
        units_of(slice(0, block))
    else:
        pl.loop(0, total // block)(lambda i: units_of(pl.ds(pl.multiple_of(i * block, block), block)))


def hidden_units(pieces, expert_gate, expert_up):
    total, width = sum(p.shape[0] for p in pieces), pieces[0].shape[1]
    model_width, units = expert_gate.shape
    return pl.pallas_call(
        functools.partial(hidden_kernel, len(pieces)),
        out_shape=in_vmem((total, units), jnp.bfloat16),
        in_specs=[VMEM] * (len(pieces) + 2),
        out_specs=VMEM,
        scratch_shapes=[pltpu.VMEM((total, width), jnp.bfloat16)],
        compiler_params=pltpu.CompilerParams(vmem_limit_bytes=(8 << 20) + 4 * total * width),
        cost_estimate=pl.CostEstimate(
            flops=4 * total * model_width * units,
            bytes_accessed=4 * model_width * units + 2 * total * width,
            transcendentals=total * units,
        ),
    )(*(held(v) for v in (*pieces, expert_gate, expert_up)))


def down_kernel(first, hidden_ref, down_ref, out_ref):
    total, width = out_ref.shape
    block = min(total, 256)
    step = 512

    def results_of(source, cols):
        for i in range(total // block):
            rows = slice(i * block, (i + 1) * block)
            value = jnp.dot(hidden_ref[rows, :], down_ref[:, source], preferred_element_type=jnp.float32)
            out_ref[rows, cols] = value.astype(jnp.bfloat16)

    if total == block:
        for c in range(0, width, step):
            results_of(slice(first + c, first + c + step), slice(c, c + step))
    else:

        @pl.loop(0, width // step)
        def _(c):
            at = pl.multiple_of(c * step, step)
            results_of(pl.ds(pl.multiple_of(first + at, step), step), pl.ds(at, step))


def down(hidden, expert_down, first, last):
    total, units = hidden.shape
    width = last - first
    return pl.pallas_call(
        functools.partial(down_kernel, first),
        out_shape=in_vmem((total, width), jnp.bfloat16),
        in_specs=[VMEM] * 2,
        out_specs=VMEM,
        compiler_params=pltpu.CompilerParams(vmem_limit_bytes=8 << 20),
        cost_estimate=pl.CostEstimate(
            flops=2 * total * width * units,
            bytes_accessed=2 * width * units + 2 * total * width,
            transcendentals=0,
        ),
    )(held(hidden), held(expert_down))


def merge_kernel(count, sizes, mine_ref, *refs):
    left = 0
    for part_ref in refs[:count]:
        width = part_ref.shape[1]
        total = mine_ref[:, left : left + width].astype(jnp.float32) + part_ref[...].astype(jnp.float32)
        low = 0
        for out_ref, size in zip(refs[count:], sizes, strict=True):
            out_ref[:, left : left + width] = total[low : low + size].astype(jnp.bfloat16)
            low += size
        left += width


def merge(mine, parts, sizes):
    return pl.pallas_call(
        functools.partial(merge_kernel, len(parts), sizes),
        out_shape=tuple(in_vmem((size, mine.shape[1]), jnp.bfloat16) for size in sizes),
        in_specs=[VMEM] * (1 + len(parts)),
        out_specs=(VMEM,) * len(sizes),
        compiler_params=pltpu.CompilerParams(vmem_limit_bytes=(4 << 20) + 8 * mine.size),
        cost_estimate=pl.CostEstimate(flops=mine.size, bytes_accessed=6 * mine.size, transcendentals=0),
    )(held(mine), *(held(p) for p in parts))


def add_kernel(count, rows, sizes, *refs):
    total = None
    for ref, (low, high) in zip(refs[:count], rows, strict=True):
        value = ref[...].astype(jnp.float32)[low:high]
        total = value if total is None else total + value
    low = 0
    for out_ref, size in zip(refs[count:], sizes, strict=True):
        out_ref[...] = total[low : low + size].astype(jnp.bfloat16)
        low += size


def add(values, rows, sizes, last=False):
    width = values[0].shape[1]
    shape = jax.ShapeDtypeStruct if last else in_vmem
    elements = sum(v.size for v in values)
    return pl.pallas_call(
        functools.partial(add_kernel, len(values), rows, sizes),
        out_shape=tuple(shape((size, width), jnp.bfloat16) for size in sizes),
        in_specs=[VMEM] * len(values),
        out_specs=(VMEM,) * len(sizes),
        compiler_params=pltpu.CompilerParams(vmem_limit_bytes=(4 << 20) + 8 * values[0].size),
        cost_estimate=pl.CostEstimate(flops=elements, bytes_accessed=2 * elements, transcendentals=0),
    )(*(held(v) for v in values))


def per_device(
    hidden_in,
    expert_routes,
    route_scores,
    expert_gate,
    expert_up,
    expert_down,
    query_latent,
    latent_cache,
    cache_lengths,
):
    tok_rows, model_width = hidden_in.shape
    ep_count, sub_count = lax.axis_size("ep"), lax.axis_size("sub")
    inner = 4
    outer = ep_count // inner

    def swap(value, even, odd):
        pairs = [
            (i * sub_count + s, (i ^ (odd if s else even)) * sub_count + s)
            for i in range(ep_count)
            for s in range(sub_count)
        ]
        return lax.ppermute(value, ("ep", "sub"), pairs)

    def first(value, k):
        return swap(value, inner * k, k if inner == outer else inner * k)

    def second(value, k):
        return swap(value, k, inner * k if inner == outer else k)

    def over_cores(value):
        return lax.ppermute(value, "sub", [(i, i ^ 1) for i in range(sub_count)])

    own = pack(hidden_in, expert_routes, route_scores, ep_count)
    near = {k: first(own, k) for k in range(outer - 1, 0, -1)}
    gate, fetched = fetch(expert_gate[0])
    block = join([own] + [near[k] for k in range(1, outer)], [fetched])
    steps = [*range(2, inner), 1]
    far = {k: second(block, k) for k in steps}
    attention_latent, up, down_rows, token = attend(
        query_latent,
        latent_cache,
        cache_lengths,
        (expert_up[0], expert_down[0]),
        block,
    )
    pieces = [block] + [tie(far[k], token) for k in range(1, inner)]
    received = [over_cores(p) for p in pieces]
    hidden = hidden_units(pieces, gate, up)
    partner = hidden_units(received, gate, up)
    cut = model_width // 1024 * 512
    other = [down(partner, down_rows, first, last) for first, last in ((0, cut), (cut, model_width))]
    other = [over_cores(part) for part in other]
    mine = down(hidden, down_rows, 0, model_width)

    size = (outer - 1) * tok_rows
    kept, column, *parts = merge(mine, other, [tok_rows, size] * inner)
    far = [second(parts[2 * k - 1], k) for k in steps]
    side = [second(parts[2 * k - 2], k) for k in steps]
    near = add([column, *far], [(0, size)] * inner, [tok_rows] * (outer - 1))
    near = [first(near[k - 1], k) for k in range(outer - 1, 0, -1)]
    (moe_output,) = add([kept, *side, *near], [(0, tok_rows)] * (1 + len(side) + len(near)), [tok_rows], last=True)
    return (moe_output, attention_latent)


def solution(mesh):
    placed = (
        P(("groups", "ep", "sub"), None),
        P(("groups", "ep", "sub"), None),
        P(("groups", "ep", "sub"), None),
        P("ep", None, "sub"),
        P("ep", None, "sub"),
        P("ep", "sub", None),
        P(("groups", "ep", "sub"), None, None),
        P(("groups", "ep", "sub"), None, None),
        P(("groups", "ep", "sub")),
    )
    return jax.shard_map(
        per_device,
        mesh=mesh,
        in_specs=placed,
        out_specs=(P(("groups", "ep", "sub"), None), P(("groups", "ep", "sub"), None, None)),
        check_vma=False,
    )
```

```python
import functools

import jax
import jax.numpy as jnp
from jax import lax
from jax.experimental import pallas as pl
from jax.experimental.pallas import tpu as pltpu
from jax.sharding import PartitionSpec as P

LATENT = 512


SOFTMAX_SCALE = 192.0 ** (-0.5)
ROUTE_SCALE = 2.5
LANES = 128
FETCHES = 2


VMEM = pl.BlockSpec(memory_space=pltpu.VMEM)
SMEM = pl.BlockSpec(memory_space=pltpu.SMEM)
ANY = pl.BlockSpec(memory_space=pl.ANY)
HBM = pl.BlockSpec(memory_space=pltpu.HBM)


def in_vmem(shape, dtype):
    return pltpu.VMEM(shape, dtype)


def stored(value):
    return pltpu.with_memory_space_constraint(value, pltpu.HBM)


def held(value):
    return pltpu.with_memory_space_constraint(value, pltpu.VMEM)


def attend_kernel(
    lengths_hbm, query_hbm, cache_hbm, up_hbm, down_hbm, after_ref,
    out_ref, up_ref, down_ref, token_ref, lengths_ref, query_ref, cache_ref, sems,
):
    pairs = [(lengths_hbm, lengths_ref), (query_hbm, query_ref), (cache_hbm, cache_ref)]
    for source, target in ((up_hbm, up_ref), (down_hbm, down_ref)):
        rows = source.shape[0] // FETCHES
        pairs += [(source.at[pl.ds(i * rows, rows)], target.at[pl.ds(i * rows, rows)]) for i in range(FETCHES)]
    copies = [pltpu.make_async_copy(s, t, sems.at[i]) for i, (s, t) in enumerate(pairs)]
    for copy in copies:
        copy.start()
    for copy in copies[:3]:
        copy.wait()
    latent = out_ref.shape[2]
    for r in range(query_ref.shape[0]):
        query, cache = query_ref[r], cache_ref[r]
        scores = SOFTMAX_SCALE * lax.dot_general(
            query, cache, (((0,), (0,)), ((), ())), preferred_element_type=jnp.float32
        )
        visible = lax.broadcasted_iota(jnp.int32, scores.shape, 1) < lengths_ref[r]
        scores = jnp.where(visible, scores, -1e30)
        largest = jnp.max(scores, axis=1, keepdims=True)
        powered = jnp.where(visible, jnp.exp(scores - largest), 0.0)
        probability = (powered / jnp.sum(powered, axis=1, keepdims=True)).astype(jnp.bfloat16)
        out_ref[r] = lax.dot_general(
            probability, cache[:latent], (((1,), (1,)), ((), ())), preferred_element_type=jnp.float32
        ).astype(jnp.bfloat16)
    token_ref[...] = jnp.zeros_like(token_ref)
    for copy in copies[3:]:
        copy.wait()


def attend(query_latent, latent_cache, cache_lengths, weights, after):
    rows, heads, entries = query_latent.shape
    positions = latent_cache.shape[1]
    query, cache = jnp.swapaxes(query_latent, 1, 2), jnp.swapaxes(latent_cache, 1, 2)
    operands = (cache_lengths, query, cache, *weights)
    return pl.pallas_call(
        attend_kernel,
        out_shape=(
            jax.ShapeDtypeStruct((rows, heads, LATENT), jnp.bfloat16),
            *(in_vmem(w.shape, w.dtype) for w in weights),
            in_vmem((8, LANES), jnp.float32),
        ),
        in_specs=[HBM] * 5 + [ANY],
        out_specs=(VMEM,) * 4,
        scratch_shapes=[
            pltpu.SMEM(cache_lengths.shape, jnp.int32),
            pltpu.VMEM(query.shape, query.dtype),
            pltpu.VMEM(cache.shape, cache.dtype),
            pltpu.SemaphoreType.DMA((3 + 2 * FETCHES,)),
        ],
        compiler_params=pltpu.CompilerParams(vmem_limit_bytes=12 << 20),
        cost_estimate=pl.CostEstimate(
            flops=4 * rows * heads * positions * entries,
            bytes_accessed=2 * sum(w.size for w in weights),
            transcendentals=rows * heads * positions,
        ),
    )(*(stored(v) for v in operands), after)


def rounds_up(value, step):
    return -(-value // step) * step


def pack_kernel(hidden_ref, routes_ref, scores_ref, out_ref, rows_ref, named_ref, affinity_ref, sems):
    rows, model_width = hidden_ref.shape
    copies = [
        pltpu.make_async_copy(source, target, sems.at[i])
        for i, (source, target) in enumerate(
            ((routes_ref, named_ref), (scores_ref, affinity_ref), (hidden_ref, rows_ref))
        )
    ]
    for copy in copies:
        copy.start()
    copies[0].wait()
    copies[1].wait()
    scores = affinity_ref[...]
    routes = named_ref[...]
    weights = ROUTE_SCALE * scores / jnp.sum(scores, axis=1, keepdims=True)
    lanes = out_ref.shape[1] - model_width
    lane = lax.broadcasted_iota(jnp.int32, (rows, lanes), 1)
    experts = lanes // 2
    dense = jnp.zeros((rows, lanes), jnp.float32)
    for k in range(routes.shape[1]):
        named = routes[:, k : k + 1]
        dense += jnp.where((lane == named) | (lane == named + experts), weights[:, k : k + 1], 0.0)
    high = dense.astype(jnp.bfloat16).astype(jnp.float32)
    out_ref[:, model_width:] = jnp.where(lane < experts, high, dense - high).astype(jnp.bfloat16)
    copies[2].wait()
    out_ref[:, :model_width] = rows_ref[...]


def pack(hidden_in, expert_routes, route_scores, experts):
    rows, model_width = hidden_in.shape
    lanes = rounds_up(2 * experts, LANES)
    return pl.pallas_call(
        pack_kernel,
        out_shape=in_vmem((rows, model_width + lanes), jnp.bfloat16),
        in_specs=[HBM] * 3,
        out_specs=VMEM,
        scratch_shapes=[
            pltpu.VMEM(hidden_in.shape, hidden_in.dtype),
            pltpu.VMEM(expert_routes.shape, expert_routes.dtype),
            pltpu.VMEM(route_scores.shape, route_scores.dtype),
            pltpu.SemaphoreType.DMA((3,)),
        ],
        compiler_params=pltpu.CompilerParams(vmem_limit_bytes=4 << 20),
        cost_estimate=pl.CostEstimate(flops=1 << 16, bytes_accessed=4 * rows * model_width, transcendentals=0),
    )(stored(hidden_in), stored(expert_routes), stored(route_scores))


def join_kernel(count, *refs):
    value = jnp.concatenate([ref[...].astype(jnp.float32) for ref in refs[:count]], axis=0)
    refs[-1][...] = value.astype(jnp.bfloat16)


def join(pieces, after=()):
    total, width = sum(p.shape[0] for p in pieces), pieces[0].shape[1]
    operands = [*pieces, *after]
    return pl.pallas_call(
        functools.partial(join_kernel, len(pieces)),
        out_shape=in_vmem((total, width), jnp.bfloat16),
        in_specs=[VMEM] * len(operands),
        out_specs=VMEM,
        compiler_params=pltpu.CompilerParams(vmem_limit_bytes=(2 << 20) + 8 * total * width),
        cost_estimate=pl.CostEstimate(flops=total * width, bytes_accessed=4 * total * width, transcendentals=0),
    )(*(held(p) for p in operands))


def fetch_kernel(source_ref, target_ref, token_ref, sems):
    rows = source_ref.shape[0] // FETCHES
    copies = [
        pltpu.make_async_copy(
            source_ref.at[pl.ds(i * rows, rows)], target_ref.at[pl.ds(i * rows, rows)], sems.at[i]
        )
        for i in range(FETCHES)
    ]
    for copy in copies:
        copy.start()
    token_ref[...] = jnp.zeros_like(token_ref)
    for copy in copies:
        copy.wait()


def fetch(value):
    return pl.pallas_call(
        fetch_kernel,
        out_shape=(in_vmem(value.shape, value.dtype), in_vmem((8, LANES), jnp.float32)),
        in_specs=[HBM],
        out_specs=(VMEM, VMEM),
        scratch_shapes=[pltpu.SemaphoreType.DMA((FETCHES,))],
        compiler_params=pltpu.CompilerParams(vmem_limit_bytes=1 << 20),
        cost_estimate=pl.CostEstimate(flops=0, bytes_accessed=2 * value.size, transcendentals=0),
    )(stored(value))


def tie_kernel(value_ref, after_ref, out_ref):
    pass


def tie(value, after):
    return pl.pallas_call(
        tie_kernel,
        out_shape=in_vmem(value.shape, value.dtype),
        in_specs=[VMEM, VMEM],
        out_specs=VMEM,
        input_output_aliases={0: 0},
        compiler_params=pltpu.CompilerParams(vmem_limit_bytes=1 << 20),
        cost_estimate=pl.CostEstimate(flops=0, bytes_accessed=0, transcendentals=0),
    )(held(value), held(after))


def hidden_kernel(count, *refs):
    pieces = refs[:count]
    gate_ref, up_ref = refs[count : count + 2]
    hidden_ref, rows_ref = refs[-2:]
    total, _ = rows_ref.shape
    model_width, units = gate_ref.shape
    lanes = rows_ref.shape[1] - model_width
    me = lax.axis_index("ep")
    block = min(total, 256)
    chunk = 256

    low = 0
    for piece in pieces:
        rows_ref[low : low + piece.shape[0], :] = piece[...]
        low += piece.shape[0]

    def units_of(here):
        tail = rows_ref[here, model_width:].astype(jnp.float32)
        lane = lax.broadcasted_iota(jnp.int32, (block, lanes), 1)
        taken = (lane == me) | (lane == me + lanes // 2)
        weight = jnp.sum(jnp.where(taken, tail, 0.0), axis=1, keepdims=True)
        for c in range(units // chunk):
            cols = slice(c * chunk, (c + 1) * chunk)
            x = rows_ref[here, :model_width]
            gate_value = jnp.dot(x, gate_ref[:, cols], preferred_element_type=jnp.float32)
            up_value = jnp.dot(x, up_ref[:, cols], preferred_element_type=jnp.float32)
            value = gate_value / (1.0 + jnp.exp(-gate_value)) * up_value * weight
            hidden_ref[here, cols] = value.astype(jnp.bfloat16)

    if total == block:
        units_of(slice(0, block))
    else:
        pl.loop(0, total // block)(lambda i: units_of(pl.ds(pl.multiple_of(i * block, block), block)))


def hidden_units(pieces, expert_gate, expert_up, after=()):
    total, width = sum(p.shape[0] for p in pieces), pieces[0].shape[1]
    model_width, units = expert_gate.shape
    return pl.pallas_call(
        functools.partial(hidden_kernel, len(pieces)),
        out_shape=in_vmem((total, units), jnp.bfloat16),
        in_specs=[VMEM] * (len(pieces) + 2 + len(after)),
        out_specs=VMEM,
        scratch_shapes=[pltpu.VMEM((total, width), jnp.bfloat16)],
        compiler_params=pltpu.CompilerParams(vmem_limit_bytes=(8 << 20) + 4 * total * width),
        cost_estimate=pl.CostEstimate(
            flops=4 * total * model_width * units,
            bytes_accessed=4 * model_width * units + 2 * total * width,
            transcendentals=total * units,
        ),
    )(*(held(v) for v in (*pieces, expert_gate, expert_up, *after)))


def down_kernel(first, hidden_ref, down_ref, out_ref):
    total, width = out_ref.shape
    block = min(total, 256)
    step = 512

    def results_of(source, cols):
        for i in range(total // block):
            rows = slice(i * block, (i + 1) * block)
            value = jnp.dot(hidden_ref[rows, :], down_ref[:, source], preferred_element_type=jnp.float32)
            out_ref[rows, cols] = value.astype(jnp.bfloat16)

    if total == block:
        for c in range(0, width, step):
            results_of(slice(first + c, first + c + step), slice(c, c + step))
    else:

        @pl.loop(0, width // step)
        def _(c):
            at = pl.multiple_of(c * step, step)
            results_of(pl.ds(pl.multiple_of(first + at, step), step), pl.ds(at, step))


def down(hidden, expert_down, first, last):
    total, units = hidden.shape
    width = last - first
    return pl.pallas_call(
        functools.partial(down_kernel, first),
        out_shape=in_vmem((total, width), jnp.bfloat16),
        in_specs=[VMEM] * 2,
        out_specs=VMEM,
        compiler_params=pltpu.CompilerParams(vmem_limit_bytes=8 << 20),
        cost_estimate=pl.CostEstimate(
            flops=2 * total * width * units,
            bytes_accessed=2 * width * units + 2 * total * width,
            transcendentals=0,
        ),
    )(held(hidden), held(expert_down))


def merge_kernel(count, sizes, mine_ref, *refs):
    left = 0
    for part_ref in refs[:count]:
        width = part_ref.shape[1]
        total = mine_ref[:, left : left + width].astype(jnp.float32) + part_ref[...].astype(jnp.float32)
        low = 0
        for out_ref, size in zip(refs[count:], sizes, strict=True):
            out_ref[:, left : left + width] = total[low : low + size].astype(jnp.bfloat16)
            low += size
        left += width


def merge(mine, parts, sizes):
    return pl.pallas_call(
        functools.partial(merge_kernel, len(parts), sizes),
        out_shape=tuple(in_vmem((size, mine.shape[1]), jnp.bfloat16) for size in sizes),
        in_specs=[VMEM] * (1 + len(parts)),
        out_specs=(VMEM,) * len(sizes),
        compiler_params=pltpu.CompilerParams(vmem_limit_bytes=(4 << 20) + 8 * mine.size),
        cost_estimate=pl.CostEstimate(flops=mine.size, bytes_accessed=6 * mine.size, transcendentals=0),
    )(held(mine), *(held(p) for p in parts))


def add_kernel(count, rows, sizes, *refs):
    total = None
    for ref, (low, high) in zip(refs[:count], rows, strict=True):
        value = ref[...].astype(jnp.float32)[low:high]
        total = value if total is None else total + value
    low = 0
    for out_ref, size in zip(refs[count:], sizes, strict=True):
        out_ref[...] = total[low : low + size].astype(jnp.bfloat16)
        low += size


def add(values, rows, sizes, last=False):
    width = values[0].shape[1]
    shape = jax.ShapeDtypeStruct if last else in_vmem
    elements = sum(v.size for v in values)
    return pl.pallas_call(
        functools.partial(add_kernel, len(values), rows, sizes),
        out_shape=tuple(shape((size, width), jnp.bfloat16) for size in sizes),
        in_specs=[VMEM] * len(values),
        out_specs=(VMEM,) * len(sizes),
        compiler_params=pltpu.CompilerParams(vmem_limit_bytes=(4 << 20) + 8 * values[0].size),
        cost_estimate=pl.CostEstimate(flops=elements, bytes_accessed=2 * elements, transcendentals=0),
    )(*(held(v) for v in values))


def per_device(
    hidden_in,
    expert_routes,
    route_scores,
    expert_gate,
    expert_up,
    expert_down,
    query_latent,
    latent_cache,
    cache_lengths,
):
    tok_rows, model_width = hidden_in.shape
    ep_count, sub_count = lax.axis_size("ep"), lax.axis_size("sub")
    inner = 4
    outer = ep_count // inner

    def swap(value, even, odd):
        pairs = [
            (i * sub_count + s, (i ^ (odd if s else even)) * sub_count + s)
            for i in range(ep_count)
            for s in range(sub_count)
        ]
        return lax.ppermute(value, ("ep", "sub"), pairs)

    def first(value, k):
        return swap(value, inner * k, k if inner == outer else inner * k)

    def second(value, k):
        return swap(value, k, inner * k if inner == outer else k)

    def over_cores(value):
        return lax.ppermute(value, "sub", [(i, i ^ 1) for i in range(sub_count)])

    own = pack(hidden_in, expert_routes, route_scores, ep_count)
    near = {k: first(own, k) for k in range(outer - 1, 0, -1)}
    gate, fetched = fetch(expert_gate[0])
    block = join([own] + [near[k] for k in range(1, outer)], [fetched])
    steps = [*range(2, inner), 1]
    far = {k: second(block, k) for k in steps}
    attention_latent, up, down_rows, token = attend(
        query_latent,
        latent_cache,
        cache_lengths,
        (expert_up[0], expert_down[0]),
        block,
    )
    pieces = [block] + [tie(far[k], token) for k in range(1, inner)]
    received = [over_cores(p) for p in pieces]
    hidden = hidden_units(pieces, gate, up)
    partner = hidden_units(received, gate, up, [hidden])
    cut = model_width // 1024 * 512
    other = [down(partner, down_rows, first, last) for first, last in ((0, cut), (cut, model_width))]
    other = [over_cores(part) for part in other]
    mine = down(hidden, down_rows, 0, model_width)

    size = (outer - 1) * tok_rows
    kept, column, *parts = merge(mine, other, [tok_rows, size] * inner)
    far = [second(parts[2 * k - 1], k) for k in steps]
    side = [second(parts[2 * k - 2], k) for k in steps]
    near = add([column, *far], [(0, size)] * inner, [tok_rows] * (outer - 1))
    near = [first(near[k - 1], k) for k in range(outer - 1, 0, -1)]
    (moe_output,) = add([kept, *side, *near], [(0, tok_rows)] * (1 + len(side) + len(near)), [tok_rows], last=True)
    return (moe_output, attention_latent)


def solution(mesh):
    placed = (
        P(("groups", "ep", "sub"), None),
        P(("groups", "ep", "sub"), None),
        P(("groups", "ep", "sub"), None),
        P("ep", None, "sub"),
        P("ep", None, "sub"),
        P("ep", "sub", None),
        P(("groups", "ep", "sub"), None, None),
        P(("groups", "ep", "sub"), None, None),
        P(("groups", "ep", "sub")),
    )
    return jax.shard_map(
        per_device,
        mesh=mesh,
        in_specs=placed,
        out_specs=(P(("groups", "ep", "sub"), None), P(("groups", "ep", "sub"), None, None)),
        check_vma=False,
    )
```

```python
import functools

import jax
import jax.numpy as jnp
from jax import lax
from jax.experimental import pallas as pl
from jax.experimental.pallas import tpu as pltpu
from jax.sharding import PartitionSpec as P

LATENT = 512


SOFTMAX_SCALE = 192.0 ** (-0.5)
ROUTE_SCALE = 2.5
LANES = 128
FETCHES = 2


VMEM = pl.BlockSpec(memory_space=pltpu.VMEM)
SMEM = pl.BlockSpec(memory_space=pltpu.SMEM)
ANY = pl.BlockSpec(memory_space=pl.ANY)
HBM = pl.BlockSpec(memory_space=pltpu.HBM)


def in_vmem(shape, dtype):
    return pltpu.VMEM(shape, dtype)


def stored(value):
    return pltpu.with_memory_space_constraint(value, pltpu.HBM)


def held(value):
    return pltpu.with_memory_space_constraint(value, pltpu.VMEM)


def attend_kernel(
    lengths_hbm, query_hbm, cache_hbm, up_hbm, down_hbm, after_ref,
    out_ref, up_ref, down_ref, token_ref, lengths_ref, query_ref, cache_ref, sems,
):
    pairs = [(lengths_hbm, lengths_ref), (query_hbm, query_ref), (cache_hbm, cache_ref)]
    for source, target in ((up_hbm, up_ref), (down_hbm, down_ref)):
        rows = source.shape[0] // FETCHES
        pairs += [(source.at[pl.ds(i * rows, rows)], target.at[pl.ds(i * rows, rows)]) for i in range(FETCHES)]
    copies = [pltpu.make_async_copy(s, t, sems.at[i]) for i, (s, t) in enumerate(pairs)]
    for copy in copies:
        copy.start()
    for copy in copies[:3]:
        copy.wait()
    latent = out_ref.shape[2]
    for r in range(query_ref.shape[0]):
        query, cache = query_ref[r], cache_ref[r]
        scores = SOFTMAX_SCALE * lax.dot_general(
            query, cache, (((0,), (0,)), ((), ())), preferred_element_type=jnp.float32
        )
        visible = lax.broadcasted_iota(jnp.int32, scores.shape, 1) < lengths_ref[r]
        scores = jnp.where(visible, scores, -1e30)
        largest = jnp.max(scores, axis=1, keepdims=True)
        powered = jnp.where(visible, jnp.exp(scores - largest), 0.0)
        probability = (powered / jnp.sum(powered, axis=1, keepdims=True)).astype(jnp.bfloat16)
        out_ref[r] = lax.dot_general(
            probability, cache[:latent], (((1,), (1,)), ((), ())), preferred_element_type=jnp.float32
        ).astype(jnp.bfloat16)
    token_ref[...] = jnp.zeros_like(token_ref)
    for copy in copies[3:]:
        copy.wait()


def attend(query_latent, latent_cache, cache_lengths, weights, after):
    rows, heads, entries = query_latent.shape
    positions = latent_cache.shape[1]
    query, cache = jnp.swapaxes(query_latent, 1, 2), jnp.swapaxes(latent_cache, 1, 2)
    operands = (cache_lengths, query, cache, *weights)
    return pl.pallas_call(
        attend_kernel,
        out_shape=(
            jax.ShapeDtypeStruct((rows, heads, LATENT), jnp.bfloat16),
            *(in_vmem(w.shape, w.dtype) for w in weights),
            in_vmem((8, LANES), jnp.float32),
        ),
        in_specs=[HBM] * 5 + [ANY],
        out_specs=(VMEM,) * 4,
        scratch_shapes=[
            pltpu.SMEM(cache_lengths.shape, jnp.int32),
            pltpu.VMEM(query.shape, query.dtype),
            pltpu.VMEM(cache.shape, cache.dtype),
            pltpu.SemaphoreType.DMA((3 + 2 * FETCHES,)),
        ],
        compiler_params=pltpu.CompilerParams(vmem_limit_bytes=12 << 20),
        cost_estimate=pl.CostEstimate(
            flops=4 * rows * heads * positions * entries,
            bytes_accessed=2 * sum(w.size for w in weights),
            transcendentals=rows * heads * positions,
        ),
    )(*(stored(v) for v in operands), after)


def rounds_up(value, step):
    return -(-value // step) * step


def pack_kernel(hidden_ref, routes_ref, scores_ref, out_ref, rows_ref, named_ref, affinity_ref, sems):
    rows, model_width = hidden_ref.shape
    copies = [
        pltpu.make_async_copy(source, target, sems.at[i])
        for i, (source, target) in enumerate(
            ((routes_ref, named_ref), (scores_ref, affinity_ref), (hidden_ref, rows_ref))
        )
    ]
    for copy in copies:
        copy.start()
    copies[0].wait()
    copies[1].wait()
    scores = affinity_ref[...]
    routes = named_ref[...]
    weights = ROUTE_SCALE * scores / jnp.sum(scores, axis=1, keepdims=True)
    lanes = out_ref.shape[1] - model_width
    lane = lax.broadcasted_iota(jnp.int32, (rows, lanes), 1)
    experts = lanes // 2
    dense = jnp.zeros((rows, lanes), jnp.float32)
    for k in range(routes.shape[1]):
        named = routes[:, k : k + 1]
        dense += jnp.where((lane == named) | (lane == named + experts), weights[:, k : k + 1], 0.0)
    high = dense.astype(jnp.bfloat16).astype(jnp.float32)
    out_ref[:, model_width:] = jnp.where(lane < experts, high, dense - high).astype(jnp.bfloat16)
    copies[2].wait()
    out_ref[:, :model_width] = rows_ref[...]


def pack(hidden_in, expert_routes, route_scores, experts):
    rows, model_width = hidden_in.shape
    lanes = rounds_up(2 * experts, LANES)
    return pl.pallas_call(
        pack_kernel,
        out_shape=in_vmem((rows, model_width + lanes), jnp.bfloat16),
        in_specs=[HBM] * 3,
        out_specs=VMEM,
        scratch_shapes=[
            pltpu.VMEM(hidden_in.shape, hidden_in.dtype),
            pltpu.VMEM(expert_routes.shape, expert_routes.dtype),
            pltpu.VMEM(route_scores.shape, route_scores.dtype),
            pltpu.SemaphoreType.DMA((3,)),
        ],
        compiler_params=pltpu.CompilerParams(vmem_limit_bytes=4 << 20),
        cost_estimate=pl.CostEstimate(flops=1 << 16, bytes_accessed=4 * rows * model_width, transcendentals=0),
    )(stored(hidden_in), stored(expert_routes), stored(route_scores))


def join_kernel(count, *refs):
    value = jnp.concatenate([ref[...].astype(jnp.float32) for ref in refs[:count]], axis=0)
    refs[-1][...] = value.astype(jnp.bfloat16)


def join(pieces, after=()):
    total, width = sum(p.shape[0] for p in pieces), pieces[0].shape[1]
    operands = [*pieces, *after]
    return pl.pallas_call(
        functools.partial(join_kernel, len(pieces)),
        out_shape=in_vmem((total, width), jnp.bfloat16),
        in_specs=[VMEM] * len(operands),
        out_specs=VMEM,
        compiler_params=pltpu.CompilerParams(vmem_limit_bytes=(2 << 20) + 8 * total * width),
        cost_estimate=pl.CostEstimate(flops=total * width, bytes_accessed=4 * total * width, transcendentals=0),
    )(*(held(p) for p in operands))


def fetch_kernel(source_ref, target_ref, token_ref, sems):
    rows = source_ref.shape[0] // FETCHES
    copies = [
        pltpu.make_async_copy(
            source_ref.at[pl.ds(i * rows, rows)], target_ref.at[pl.ds(i * rows, rows)], sems.at[i]
        )
        for i in range(FETCHES)
    ]
    for copy in copies:
        copy.start()
    token_ref[...] = jnp.zeros_like(token_ref)
    for copy in copies:
        copy.wait()


def fetch(value):
    return pl.pallas_call(
        fetch_kernel,
        out_shape=(in_vmem(value.shape, value.dtype), in_vmem((8, LANES), jnp.float32)),
        in_specs=[HBM],
        out_specs=(VMEM, VMEM),
        scratch_shapes=[pltpu.SemaphoreType.DMA((FETCHES,))],
        compiler_params=pltpu.CompilerParams(vmem_limit_bytes=1 << 20),
        cost_estimate=pl.CostEstimate(flops=0, bytes_accessed=2 * value.size, transcendentals=0),
    )(stored(value))


def tie_kernel(value_ref, after_ref, out_ref):
    pass


def tie(value, after):
    return pl.pallas_call(
        tie_kernel,
        out_shape=in_vmem(value.shape, value.dtype),
        in_specs=[VMEM, VMEM],
        out_specs=VMEM,
        input_output_aliases={0: 0},
        compiler_params=pltpu.CompilerParams(vmem_limit_bytes=1 << 20),
        cost_estimate=pl.CostEstimate(flops=0, bytes_accessed=0, transcendentals=0),
    )(held(value), held(after))


def hidden_kernel(count, *refs):
    pieces = refs[:count]
    gate_ref, up_ref = refs[count : count + 2]
    hidden_ref, rows_ref = refs[-2:]
    total, _ = rows_ref.shape
    model_width, units = gate_ref.shape
    lanes = rows_ref.shape[1] - model_width
    me = lax.axis_index("ep")
    block = min(total, 256)
    chunk = 256

    low = 0
    for piece in pieces:
        rows_ref[low : low + piece.shape[0], :] = piece[...]
        low += piece.shape[0]

    def units_of(here):
        tail = rows_ref[here, model_width:].astype(jnp.float32)
        lane = lax.broadcasted_iota(jnp.int32, (block, lanes), 1)
        taken = (lane == me) | (lane == me + lanes // 2)
        weight = jnp.sum(jnp.where(taken, tail, 0.0), axis=1, keepdims=True)
        for c in range(units // chunk):
            cols = slice(c * chunk, (c + 1) * chunk)
            x = rows_ref[here, :model_width]
            gate_value = jnp.dot(x, gate_ref[:, cols], preferred_element_type=jnp.float32)
            up_value = jnp.dot(x, up_ref[:, cols], preferred_element_type=jnp.float32)
            value = gate_value / (1.0 + jnp.exp(-gate_value)) * up_value * weight
            hidden_ref[here, cols] = value.astype(jnp.bfloat16)

    if total == block:
        units_of(slice(0, block))
    else:
        pl.loop(0, total // block)(lambda i: units_of(pl.ds(pl.multiple_of(i * block, block), block)))


def hidden_units(pieces, expert_gate, expert_up, after=()):
    total, width = sum(p.shape[0] for p in pieces), pieces[0].shape[1]
    model_width, units = expert_gate.shape
    return pl.pallas_call(
        functools.partial(hidden_kernel, len(pieces)),
        out_shape=in_vmem((total, units), jnp.bfloat16),
        in_specs=[VMEM] * (len(pieces) + 2 + len(after)),
        out_specs=VMEM,
        scratch_shapes=[pltpu.VMEM((total, width), jnp.bfloat16)],
        compiler_params=pltpu.CompilerParams(vmem_limit_bytes=(8 << 20) + 4 * total * width),
        cost_estimate=pl.CostEstimate(
            flops=4 * total * model_width * units,
            bytes_accessed=4 * model_width * units + 2 * total * width,
            transcendentals=total * units,
        ),
    )(*(held(v) for v in (*pieces, expert_gate, expert_up, *after)))


def down_kernel(first, hidden_ref, down_ref, out_ref):
    total, width = out_ref.shape
    block = min(total, 256)
    step = 512

    def results_of(source, cols):
        for i in range(total // block):
            rows = slice(i * block, (i + 1) * block)
            value = jnp.dot(hidden_ref[rows, :], down_ref[:, source], preferred_element_type=jnp.float32)
            out_ref[rows, cols] = value.astype(jnp.bfloat16)

    if total == block:
        for c in range(0, width, step):
            results_of(slice(first + c, first + c + step), slice(c, c + step))
    else:

        @pl.loop(0, width // step)
        def _(c):
            at = pl.multiple_of(c * step, step)
            results_of(pl.ds(pl.multiple_of(first + at, step), step), pl.ds(at, step))


def down(hidden, expert_down, first, last):
    total, units = hidden.shape
    width = last - first
    return pl.pallas_call(
        functools.partial(down_kernel, first),
        out_shape=in_vmem((total, width), jnp.bfloat16),
        in_specs=[VMEM] * 2,
        out_specs=VMEM,
        compiler_params=pltpu.CompilerParams(vmem_limit_bytes=8 << 20),
        cost_estimate=pl.CostEstimate(
            flops=2 * total * width * units,
            bytes_accessed=2 * width * units + 2 * total * width,
            transcendentals=0,
        ),
    )(held(hidden), held(expert_down))


def merge_kernel(count, sizes, mine_ref, *refs):
    left = 0
    for part_ref in refs[:count]:
        width = part_ref.shape[1]
        total = mine_ref[:, left : left + width].astype(jnp.float32) + part_ref[...].astype(jnp.float32)
        low = 0
        for out_ref, size in zip(refs[count:], sizes, strict=True):
            out_ref[:, left : left + width] = total[low : low + size].astype(jnp.bfloat16)
            low += size
        left += width


def merge(mine, parts, sizes):
    return pl.pallas_call(
        functools.partial(merge_kernel, len(parts), sizes),
        out_shape=tuple(in_vmem((size, mine.shape[1]), jnp.bfloat16) for size in sizes),
        in_specs=[VMEM] * (1 + len(parts)),
        out_specs=(VMEM,) * len(sizes),
        compiler_params=pltpu.CompilerParams(vmem_limit_bytes=(4 << 20) + 8 * mine.size),
        cost_estimate=pl.CostEstimate(flops=mine.size, bytes_accessed=6 * mine.size, transcendentals=0),
    )(held(mine), *(held(p) for p in parts))


def add_kernel(count, rows, sizes, *refs):
    total = None
    for ref, (low, high) in zip(refs[:count], rows, strict=True):
        value = ref[...].astype(jnp.float32)[low:high]
        total = value if total is None else total + value
    low = 0
    for out_ref, size in zip(refs[count:], sizes, strict=True):
        out_ref[...] = total[low : low + size].astype(jnp.bfloat16)
        low += size


def add(values, rows, sizes, last=False):
    width = values[0].shape[1]
    shape = jax.ShapeDtypeStruct if last else in_vmem
    elements = sum(v.size for v in values)
    return pl.pallas_call(
        functools.partial(add_kernel, len(values), rows, sizes),
        out_shape=tuple(shape((size, width), jnp.bfloat16) for size in sizes),
        in_specs=[VMEM] * len(values),
        out_specs=(VMEM,) * len(sizes),
        compiler_params=pltpu.CompilerParams(vmem_limit_bytes=(4 << 20) + 8 * values[0].size),
        cost_estimate=pl.CostEstimate(flops=elements, bytes_accessed=2 * elements, transcendentals=0),
    )(*(held(v) for v in values))


def per_device(
    hidden_in,
    expert_routes,
    route_scores,
    expert_gate,
    expert_up,
    expert_down,
    query_latent,
    latent_cache,
    cache_lengths,
):
    tok_rows, model_width = hidden_in.shape
    ep_count, sub_count = lax.axis_size("ep"), lax.axis_size("sub")
    inner = 4
    outer = ep_count // inner

    def swap(value, even, odd):
        pairs = [
            (i * sub_count + s, (i ^ (odd if s else even)) * sub_count + s)
            for i in range(ep_count)
            for s in range(sub_count)
        ]
        return lax.ppermute(value, ("ep", "sub"), pairs)

    def first(value, k):
        k = outer - k
        return swap(value, inner * k, k if inner == outer else inner * k)

    def second(value, k):
        k = inner - k
        return swap(value, k, inner * k if inner == outer else k)

    def over_cores(value):
        return lax.ppermute(value, "sub", [(i, i ^ 1) for i in range(sub_count)])

    own = pack(hidden_in, expert_routes, route_scores, ep_count)
    near = {k: first(own, k) for k in range(outer - 1, 0, -1)}
    gate, fetched = fetch(expert_gate[0])
    block = join([own] + [near[k] for k in range(1, outer)], [fetched])
    steps = [*range(inner - 2, 0, -1), inner - 1]
    far = {k: second(block, k) for k in steps}
    attention_latent, up, down_rows, token = attend(
        query_latent,
        latent_cache,
        cache_lengths,
        (expert_up[0], expert_down[0]),
        block,
    )
    pieces = [block] + [tie(far[k], token) for k in range(1, inner)]
    received = [over_cores(p) for p in pieces]
    hidden = hidden_units(pieces, gate, up)
    partner = hidden_units(received, gate, up, [hidden])
    cut = model_width // 1024 * 512
    other = [down(partner, down_rows, first, last) for first, last in ((0, cut), (cut, model_width))]
    other = [over_cores(part) for part in other]
    mine = down(hidden, down_rows, 0, model_width)

    size = (outer - 1) * tok_rows
    kept, column, *parts = merge(mine, other, [tok_rows, size] * inner)
    far = [second(parts[2 * k - 1], k) for k in steps]
    side = [second(parts[2 * k - 2], k) for k in steps]
    near = add([column, *far], [(0, size)] * inner, [tok_rows] * (outer - 1))
    near = [first(near[k - 1], k) for k in range(1, outer)]
    (moe_output,) = add([kept, *side, *near], [(0, tok_rows)] * (1 + len(side) + len(near)), [tok_rows], last=True)
    return (moe_output, attention_latent)


def solution(mesh):
    placed = (
        P(("groups", "ep", "sub"), None),
        P(("groups", "ep", "sub"), None),
        P(("groups", "ep", "sub"), None),
        P("ep", None, "sub"),
        P("ep", None, "sub"),
        P("ep", "sub", None),
        P(("groups", "ep", "sub"), None, None),
        P(("groups", "ep", "sub"), None, None),
        P(("groups", "ep", "sub")),
    )
    return jax.shard_map(
        per_device,
        mesh=mesh,
        in_specs=placed,
        out_specs=(P(("groups", "ep", "sub"), None), P(("groups", "ep", "sub"), None, None)),
        check_vma=False,
    )
```
